32 devices in a mesh: row: 8 (over y, x, core), col: 4 (over z).
Axes of the slice: x: 2, y: 2, z: 4, core: 2. Of those that a mesh axis runs over, the one named last changes fastest.
Arguments:
- video_rows: bfloat16 [12288, 1024], P(('row', 'col')), may hold values from -1.5 to 1.5
- video_ids: int32 [12288], P(('row', 'col')), may hold values from 0 to 767
- imu_rows: bfloat16 [12288, 1024], P(('row', 'col')), may hold values from -1.5 to 1.5
- imu_ids: int32 [12288], P(('row', 'col')), may hold values from 0 to 767
- audio_rows: bfloat16 [12288, 1024], P(('row', 'col')), may hold values from -1.5 to 1.5
- audio_ids: int32 [12288], P(('row', 'col')), may hold values from 0 to 767
- imu_log_scale: float32 [1], replicated, may hold values from 0 to 1
- imu_bias: float32 [1], replicated, may hold values from -3 to -1
- audio_log_scale: float32 [1], replicated, may hold values from 0 to 1
- audio_bias: float32 [1], replicated, may hold values from -3 to -1
Outputs:
- video_grad: float32 [12288, 1024], P(('row', 'col'))
- imu_grad: float32 [12288, 1024], P(('row', 'col'))
- audio_grad: float32 [12288, 1024], P(('row', 'col'))
- row_loss: float32 [12288], P(('row', 'col'))
The draws below stay inside these ranges and needn't reach their ends.
All inputs are finite; a program needn't handle non-finite values.
Results may differ from the reference program's by a relative error of at most 0.0025.
Values may be sent and summed in bfloat16 or wider, within the bound.
No kernel may reach another device: no remote copies, remote signals or barrier semaphores. Data moves between devices by JAX's collectives and lax.ppermute only.
A program may use at most 128 MiB of HBM per device.

```python
import jax
import jax.numpy as jnp
from jax import lax

D = 1024
TOK_DEV = 384
STEPS = 4
BATCH = 12288
IDS = 768
N_ROW = 8
N_COL = 4


def place_ends(values, rng, least, top_value):
    longest = values.shape.index(max(values.shape))
    spots = []
    for shift in (0, 1):
        where = [jax.random.randint(jax.random.fold_in(rng, axis), (), 0, length) for axis, length in enumerate(values.shape)]
        where[longest] = (where[longest] + shift) % values.shape[longest]
        spots.append(tuple(where))
    return values.at[spots[0]].set(least).at[spots[1]].set(top_value)


def block_scale(own_key, shape, cuts, low, high):
    gain, own = 1.0, jax.random.fold_in(own_key, 6)
    for position, shards_of in cuts:
        heights = jnp.exp(jax.random.uniform(jax.random.fold_in(own, position), (shards_of,), jnp.float32, low / len(cuts), high / len(cuts)))
        gain = gain * jnp.repeat(heights, shape[position] // shards_of).reshape([-1 if axis == position else 1 for axis in range(len(shape))])
    return gain


def normal_values(key, dims, scale, limit, shards=(), kind=jnp.bfloat16):
    array = jax.random.normal(key, dims, jnp.float32) * scale
    if len(shards) > 0:
        array = block_scale(key, dims, shards, -0.22, 0.18) * array
    return jnp.clip(array, min=-limit, max=limit).astype(kind)


def setup_inputs(seed: int = 0) -> dict:
    keys = jax.random.split(jax.random.key(seed), 11)
    video_rows = normal_values(keys[0], (BATCH, D), 0.25, 1.5, ((0, 32),))
    video_ids = place_ends(jax.random.randint(keys[1], (BATCH,), 0, IDS), jax.random.fold_in(keys[1], 1), 0, IDS - 1).astype(jnp.int32)
    imu_rows = normal_values(keys[2], (BATCH, D), 0.25, 1.5, ((0, 32),))
    imu_ids = place_ends(jax.random.randint(keys[3], (BATCH,), 0, IDS), jax.random.fold_in(keys[3], 1), 0, IDS - 1).astype(jnp.int32)
    audio_rows = normal_values(keys[4], (BATCH, D), 0.25, 1.5, ((0, 32),))
    audio_ids = place_ends(jax.random.randint(keys[5], (BATCH,), 0, IDS), jax.random.fold_in(keys[5], 1), 0, IDS - 1).astype(jnp.int32)
    imu_log_scale = jnp.clip(jax.random.uniform(keys[6], (1,), jnp.float32, 0.0, 1.0), 0.0, 1.0)
    imu_bias = jnp.clip(jax.random.uniform(keys[7], (1,), jnp.float32, -3.0, -1.0), -3.0, -1.0)
    audio_log_scale = jnp.clip(jax.random.uniform(keys[8], (1,), jnp.float32, 0.0, 1.0), 0.0, 1.0)
    audio_bias = jnp.clip(jax.random.uniform(keys[9], (1,), jnp.float32, -3.0, -1.0), -3.0, -1.0)
    return {"video_rows": video_rows, "video_ids": video_ids, "imu_rows": imu_rows, "imu_ids": imu_ids, "audio_rows": audio_rows, "audio_ids": audio_ids, "imu_log_scale": imu_log_scale, "imu_bias": imu_bias, "audio_log_scale": audio_log_scale, "audio_bias": audio_bias}


def pair_tile(video_block, video_tags, partner, partner_tags, scale, offset):
    products = lax.dot_general(video_block, partner, (((1,), (1,)), ((), ())), preferred_element_type=jnp.float32)
    logits = scale * products + offset
    signs = jnp.where(video_tags[:, None] == partner_tags[None, :], 1.0, -1.0).astype(logits.dtype)
    losses = jax.nn.softplus(-signs * logits)
    weighted = (-signs * jax.nn.sigmoid(-signs * logits) * scale).astype(jnp.bfloat16)
    video_term = jnp.dot(weighted, partner, preferred_element_type=jnp.float32)
    partner_term = lax.dot_general(weighted, video_block, (((0,), (0,)), ((), ())), preferred_element_type=jnp.float32)
    return jnp.sum(losses, axis=1), video_term, partner_term


def reference(video_rows, video_ids, imu_rows, imu_ids, audio_rows, audio_ids, imu_log_scale, imu_bias, audio_log_scale, audio_bias):
    blocks = N_ROW * N_COL
    shape_four = (N_ROW, N_COL, TOK_DEV, D)
    shape_tags = (N_ROW, N_COL, TOK_DEV)
    video_flat = video_rows.reshape(blocks, TOK_DEV, D)
    video_tags = video_ids.reshape(blocks, TOK_DEV)
    imu_four = imu_rows.reshape(shape_four)
    imu_tags = imu_ids.reshape(shape_tags)
    audio_four = audio_rows.reshape(shape_four)
    audio_tags = audio_ids.reshape(shape_tags)
    scale_imu = jnp.exp(imu_log_scale[0])
    scale_audio = jnp.exp(audio_log_scale[0])
    offset_imu = imu_bias[0]
    offset_audio = audio_bias[0]
    loss_sum = jnp.zeros((blocks, TOK_DEV), jnp.float32)
    video_acc = jnp.zeros((blocks, TOK_DEV, D), jnp.float32)
    imu_acc = jnp.zeros(shape_four, jnp.float32)
    audio_acc = jnp.zeros(shape_four, jnp.float32)
    for rotation in range(STEPS):
        imu_now = jnp.roll(imu_four, rotation, axis=0).reshape(blocks, TOK_DEV, D)
        imu_tag_now = jnp.roll(imu_tags, rotation, axis=0).reshape(blocks, TOK_DEV)
        audio_now = jnp.roll(audio_four, rotation, axis=1).reshape(blocks, TOK_DEV, D)
        audio_tag_now = jnp.roll(audio_tags, rotation, axis=1).reshape(blocks, TOK_DEV)

        def one_block(items):
            video_block, video_tag, imu_block, imu_tag, audio_block, audio_tag = items
            loss_imu, video_imu, imu_term = pair_tile(video_block, video_tag, imu_block, imu_tag, scale_imu, offset_imu)
            loss_audio, video_audio, audio_term = pair_tile(video_block, video_tag, audio_block, audio_tag, scale_audio, offset_audio)
            return loss_imu + loss_audio, video_imu + video_audio, imu_term, audio_term

        losses, video_terms, imu_terms, audio_terms = lax.map(one_block, (video_flat, video_tags, imu_now, imu_tag_now, audio_now, audio_tag_now))
        loss_sum = loss_sum + losses
        video_acc = video_acc + video_terms
        imu_acc = imu_acc + jnp.roll(imu_terms.reshape(shape_four), -rotation, axis=0)
        audio_acc = audio_acc + jnp.roll(audio_terms.reshape(shape_four), -rotation, axis=1)
    row_loss = (loss_sum / (2.0 * STEPS * TOK_DEV)).reshape(-1)
    return video_acc.reshape(-1, D), imu_acc.reshape(-1, D), audio_acc.reshape(-1, D), row_loss
```

```python
import jax
import jax.numpy as jnp
from jax import lax
from jax.sharding import PartitionSpec as P

STEPS = 4
CHUNKS = 2


def passed_along(shard, axis, by):
    devices = lax.axis_size(axis)
    return lax.ppermute(shard, axis, [(i, (i + by) % devices) for i in range(devices)])


def along(shard, axis, pairs):
    return lax.ppermute(shard, axis, pairs)


def weights(video, video_tags, partner, partner_tags, scale, offset):
    products = lax.dot_general(
        video, partner, (((1,), (1,)), ((), ())), preferred_element_type=jnp.float32
    )
    logits = scale * products + offset
    signs = jnp.where(video_tags[:, None] == partner_tags[None, :], 1.0, -1.0)
    losses = jax.nn.softplus(-signs * logits)
    weighted = (-signs * jax.nn.sigmoid(-signs * logits) * scale).astype(jnp.bfloat16)
    return losses, weighted


def to_video(weighted, partner):
    return jnp.dot(weighted, partner, preferred_element_type=jnp.float32)


def to_partner(weighted, video):
    return lax.dot_general(
        weighted, video, (((0,), (0,)), ((), ())), preferred_element_type=jnp.float32
    )


def row_sum(losses):
    return jnp.sum(losses, axis=1)


def imu_exchange(video, video_tags, imu, imu_tags):
    devices = lax.axis_size("row")
    swap = [(r, r ^ 1) for r in range(devices)]

    def mixed(even, odd):
        return [(r, (r + (odd if r % 2 else even)) % devices) for r in range(devices)]

    imu_two = passed_along((imu, imu_tags), "row", 2)
    video_two = passed_along((video, video_tags), "row", -2)
    imu_mixed = along((imu, imu_tags), "row", mixed(1, 3))
    video_mixed = along((video, video_tags), "row", mixed(-3, -1))
    imu_swap = along(imu_two, "row", swap)
    video_swap = along(video_two, "row", swap)
    return (imu_two, imu_mixed, imu_swap), (video_two, video_mixed, video_swap)


def imu_part(video, video_tags, imu, imu_tags, scale, offset):
    imus, videos = imu_exchange(video, video_tags, imu, imu_tags)
    losses, weighted = weights(video, video_tags, imu, imu_tags, scale, offset)
    loss = row_sum(losses)
    video_grad = to_video(weighted, imu)
    imu_grad = to_partner(weighted, video)
    for other, tags in imus:
        losses, weighted = weights(video, video_tags, other, tags, scale, offset)
        loss = loss + row_sum(losses)
        video_grad = video_grad + to_video(weighted, other)
    for other, tags in videos:
        _, weighted = weights(other, tags, imu, imu_tags, scale, offset)
        imu_grad = imu_grad + to_partner(weighted, other)
    return loss, video_grad, imu_grad


def audio_ring(video, video_tags, audio, audio_tags, scale, offset):
    loss, video_grad, audio_grad = 0.0, 0.0, 0.0
    block, tags = audio, audio_tags
    for rotation in range(STEPS):
        if rotation > 0:
            block, tags = passed_along((block, tags), "col", 1)
            audio_grad = passed_along(audio_grad, "col", 1)
        losses, weighted = weights(video, video_tags, block, tags, scale, offset)
        loss = loss + row_sum(losses)
        video_grad = video_grad + to_video(weighted, block)
        audio_grad = audio_grad + to_partner(weighted, video)
    audio_grad = passed_along(audio_grad, "col", -(STEPS - 1))
    return loss, video_grad, audio_grad


def audio_chain(video, video_tags, audio, audio_tags, scale, offset):
    across = [(1, 2), (2, 1)]
    inward = [(0, 1), (3, 2)]
    outward = [(1, 0), (2, 3)]
    beyond = [(0, 2), (3, 1)]
    step = audio.shape[0] // CHUNKS
    chunks = [slice(k * step, (k + 1) * step) for k in range(CHUNKS)]

    mid, mid_tags = along((audio, audio_tags), "col", across)
    video_out, video_out_tags = along((video, video_tags), "col", inward)
    far, far_tags = along((audio, audio_tags), "col", beyond)
    audio_out, audio_out_tags = along((audio, audio_tags), "col", inward)

    def meet(v, v_tags, a, a_tags):
        losses, weighted = weights(v, v_tags, a, a_tags, scale, offset)
        return row_sum(losses), weighted

    own_loss, own_w = meet(video, video_tags, audio, audio_tags)
    mid_loss, mid_w = meet(video, video_tags, mid, mid_tags)
    far_loss, far_w = meet(video, video_tags, far, far_tags)
    out_loss, out_w = meet(video, video_tags, audio_out, audio_out_tags)
    own_loss_o, own_w_o = meet(video_out, video_out_tags, audio, audio_tags)
    mid_loss_o, mid_w_o = meet(video_out, video_out_tags, mid, mid_tags)
    far_loss_o, far_w_o = meet(video_out, video_out_tags, far, far_tags)

    def sums(w, w_o, rows):
        both = to_partner(w[:, rows], video) + to_partner(w_o[:, rows], video_out)
        return both.astype(jnp.bfloat16)

    mid_sums = [sums(mid_w, mid_w_o, rows) for rows in chunks]
    far_sums = [sums(far_w, far_w_o, rows) for rows in chunks]
    out_own = [to_partner(out_w[:, rows], video) for rows in chunks]

    mid_got = [None] * CHUNKS
    far_got = [None] * CHUNKS
    mid_got[0] = along(mid_sums[0], "col", across)
    for k in range(CHUNKS):
        far_got[k] = along(far_sums[k], "col", across)
    for k in range(1, CHUNKS):
        mid_got[k] = along(mid_sums[k], "col", across)
    video_back = (
        to_video(own_w_o, audio) + to_video(mid_w_o, mid) + to_video(far_w_o, far)
    ).astype(jnp.bfloat16)
    video_got = along(video_back, "col", outward)
    loss_got = along(own_loss_o + mid_loss_o + far_loss_o, "col", outward)
    out_got = [
        along((own + got.astype(jnp.float32)).astype(jnp.bfloat16), "col", outward)
        for own, got in zip(out_own, far_got)
    ]

    place = lax.axis_index("col")
    inner = (place == 1) | (place == 2)
    loss = own_loss + jnp.where(inner, mid_loss + far_loss + out_loss, loss_got)
    video_grad = (
        to_video(own_w, audio)
        + to_video(mid_w, mid)
        + to_video(far_w, far)
        + to_video(out_w, audio_out)
        + video_got.astype(jnp.float32)
    )
    own_grad = to_partner(own_w, video) + to_partner(own_w_o, video_out)
    got = [m.astype(jnp.float32) + o.astype(jnp.float32) for m, o in zip(mid_got, out_got)]
    audio_grad = own_grad + jnp.concatenate(got, axis=0)
    return loss, video_grad, audio_grad


def per_device(
    video_rows,
    video_ids,
    imu_rows,
    imu_ids,
    audio_rows,
    audio_ids,
    imu_log_scale,
    imu_bias,
    audio_log_scale,
    audio_bias,
):
    audio_part = audio_chain if lax.axis_size("col") == STEPS else audio_ring
    audio_loss, audio_video, audio_grad = audio_part(
        video_rows, video_ids, audio_rows, audio_ids, jnp.exp(audio_log_scale[0]), audio_bias[0]
    )
    imu_loss, imu_video, imu_grad = imu_part(
        video_rows, video_ids, imu_rows, imu_ids, jnp.exp(imu_log_scale[0]), imu_bias[0]
    )
    row_loss = (imu_loss + audio_loss) / (2.0 * STEPS * video_rows.shape[0])
    return (imu_video + audio_video, imu_grad, audio_grad, row_loss)


def solution(mesh):
    rows, vector = P(("row", "col"), None), P(("row", "col"))
    return jax.shard_map(
        per_device,
        mesh=mesh,
        in_specs=(rows, vector, rows, vector, rows, vector, P(), P(), P(), P()),
        out_specs=(rows, rows, rows, vector),
        check_vma=False,
    )
```

```python
import functools

import jax
import jax.numpy as jnp
from jax import lax
from jax.experimental import pallas as pl
from jax.experimental.pallas import tpu as pltpu
from jax.sharding import PartitionSpec as P

STEPS = 4
CHUNKS = 2
SLAB = 64
COLUMNS = 512
VIDEO, IMU, AUDIO = 0, 1, 2

F32 = jnp.float32
BF16 = jnp.bfloat16


def moved(block, axis, pairs):
    return lax.ppermute(block, axis, pairs)


def shifted(block, axis, by):
    devices = lax.axis_size(axis)
    return moved(block, axis, [(i, (i + by) % devices) for i in range(devices)])


def meet(video, video_ids, partner, partner_ids, scale, offset, products, weights):
    rows = partner.shape[0]
    products[...] = lax.dot_general(
        partner[...], video[...], (((1,), (1,)), ((), ())), preferred_element_type=F32
    )
    tags = jnp.transpose(jnp.broadcast_to(partner_ids, (8, rows)))[:, :1]
    total = jnp.zeros((8, video.shape[0]), F32)
    for start in range(0, rows, SLAB):
        part = slice(start, start + SLAB)
        logits = scale * products[part, :] + offset
        same = tags[part, :] == video_ids
        flipped = -logits
        z = jnp.where(same, flipped, logits)
        e = jnp.exp(jnp.minimum(logits, flipped))
        inverse = 1.0 / (1.0 + e)
        sigmoid = jnp.where(z >= 0.0, inverse, e * inverse)
        weights[part, :] = (jnp.where(same, -scale, scale) * sigmoid).astype(BF16)
        log1p = jnp.where(e < 0.005, e * (1.0 - 0.5 * e), jnp.log(1.0 + e))
        losses = jnp.maximum(z, 0.0) + log1p
        total = total + jnp.sum(losses.reshape(SLAB // 8, 8, video.shape[0]), axis=0)
    return jnp.sum(total, axis=0, keepdims=True)


def column_parts(ref):
    return [slice(c, c + COLUMNS) for c in range(0, ref.shape[1], COLUMNS)]


def to_video(weights, partner, part):
    return lax.dot_general(
        weights[...], partner[:, part], (((0,), (0,)), ((), ())), preferred_element_type=F32
    )


def to_partner(weights, video, part):
    return jnp.dot(weights[...], video[:, part], preferred_element_type=F32)


def scale_offset(scalars, modality):
    base = 0 if modality == IMU else 2
    return scalars[base], scalars[base + 1]


def own_kernel(
    scalars, ids, video, imu, audio,
    imu_loss, imu_video, imu_grad, audio_loss, audio_video, audio_grad,
    products, weights,
):
    for modality, block, loss, video_grad, grad in (
        (AUDIO, audio, audio_loss, audio_video, audio_grad),
        (IMU, imu, imu_loss, imu_video, imu_grad),
    ):
        scale, offset = scale_offset(scalars, modality)
        loss[...] = meet(
            video, ids[VIDEO : VIDEO + 1, :], block, ids[modality : modality + 1, :],
            scale, offset, products, weights,
        )
        for part in column_parts(video):
            video_grad[:, part] = to_video(weights, block, part)
            grad[:, part] = to_partner(weights, video, part)


def imu_kernel(
    imu_by, video_by, scalars, ids, all_ids, video, imu, other_imu, other_video,
    loss_in, video_in, grad_in, loss, video_grad, grad, products, weights,
):
    scale, offset = scale_offset(scalars, IMU)
    row, col = lax.axis_index("row"), lax.axis_index("col")
    devices, columns = lax.axis_size("row"), lax.axis_size("col")
    odd = row % 2

    def tags(by, modality):
        at = (row + jnp.where(odd == 1, by[1], by[0]) + devices) % devices
        return all_ids[at * columns + col, modality : modality + 1, :]

    loss[...] = loss_in[...] + meet(
        video, ids[VIDEO : VIDEO + 1, :], other_imu, tags(imu_by, IMU),
        scale, offset, products, weights,
    )
    for part in column_parts(video):
        video_grad[:, part] = video_in[:, part] + to_video(weights, other_imu, part)
    meet(
        other_video, tags(video_by, VIDEO), imu, ids[IMU : IMU + 1, :],
        scale, offset, products, weights,
    )
    for part in column_parts(video):
        grad[:, part] = grad_in[:, part] + to_partner(weights, other_video, part)


def audio_tags(all_ids, col, modality):
    at = lax.axis_index("row") * lax.axis_size("col") + col
    return all_ids[at, modality : modality + 1, :]


def middle_kernel(
    scalars, ids, all_ids, video, audio, middle, outer_video,
    loss_in, video_in, grad_in,
    loss, outer_loss, video_grad, outer_grad, grad, sums_0, sums_1, products, weights, outer_weights,
):
    scale, offset = scale_offset(scalars, AUDIO)
    col = lax.axis_index("col")
    own_tags = ids[VIDEO : VIDEO + 1, :]
    outer_tags = audio_tags(all_ids, jnp.where(col < 2, 0, 3), VIDEO)
    middle_tags = audio_tags(all_ids, 3 - col, AUDIO)
    half = sums_0.shape[0]
    loss[...] = loss_in[...] + meet(
        video, own_tags, middle, middle_tags, scale, offset, products, weights
    )
    of_outer = meet(
        outer_video, outer_tags, middle, middle_tags, scale, offset, products, outer_weights
    )
    for part in column_parts(video):
        video_grad[:, part] = video_in[:, part] + to_video(weights, middle, part)
        outer_grad[:, part] = to_video(outer_weights, middle, part)
        both = to_partner(weights, video, part) + to_partner(outer_weights, outer_video, part)
        sums_0[:, part] = both[:half].astype(BF16)
        sums_1[:, part] = both[half:].astype(BF16)
    outer_loss[...] = of_outer + meet(
        outer_video, outer_tags, audio, ids[AUDIO : AUDIO + 1, :],
        scale, offset, products, outer_weights,
    )
    for part in column_parts(video):
        outer_grad[:, part] += to_video(outer_weights, audio, part)
        grad[:, part] = grad_in[:, part] + to_partner(outer_weights, outer_video, part)


def far_kernel(
    scalars, ids, all_ids, video, outer_video, far,
    loss_in, outer_loss_in, video_in, outer_in,
    loss, outer_loss, video_grad, outer_grad, sums_0, sums_1, products, weights, outer_weights,
):
    scale, offset = scale_offset(scalars, AUDIO)
    col = lax.axis_index("col")
    own_tags = ids[VIDEO : VIDEO + 1, :]
    outer_tags = audio_tags(all_ids, jnp.where(col < 2, 0, 3), VIDEO)
    far_tags = audio_tags(all_ids, jnp.where(col < 2, 3, 0), AUDIO)
    half = sums_0.shape[0]
    loss[...] = loss_in[...] + meet(
        video, own_tags, far, far_tags, scale, offset, products, weights
    )
    outer_loss[...] = outer_loss_in[...] + meet(
        outer_video, outer_tags, far, far_tags, scale, offset, products, outer_weights
    )
    for part in column_parts(video):
        both = to_partner(weights, video, part) + to_partner(outer_weights, outer_video, part)
        sums_0[:, part] = both[:half].astype(BF16)
        sums_1[:, part] = both[half:].astype(BF16)
        video_grad[:, part] = video_in[:, part] + to_video(weights, far, part)
        outer_grad[:, part] = (outer_in[:, part] + to_video(outer_weights, far, part)).astype(BF16)


def near_kernel(
    scalars, ids, all_ids, video, near, loss_in, video_in,
    loss, video_grad, sums_0, sums_1, products, weights,
):
    scale, offset = scale_offset(scalars, AUDIO)
    col = lax.axis_index("col")
    half = sums_0.shape[0]
    loss[...] = loss_in[...] + meet(
        video, ids[VIDEO : VIDEO + 1, :],
        near, audio_tags(all_ids, jnp.where(col < 2, 0, 3), AUDIO),
        scale, offset, products, weights,
    )
    for part in column_parts(video):
        term = to_partner(weights, video, part)
        sums_0[:, part] = term[:half]
        sums_1[:, part] = term[half:]
        video_grad[:, part] = video_in[:, part] + to_video(weights, near, part)


def call(kernel, outs, args, meetings, matmuls, rows, width, weights=1):
    smem, vmem = pl.BlockSpec(memory_space=pltpu.SMEM), pl.BlockSpec(memory_space=pltpu.VMEM)
    size = sum(a.size * a.dtype.itemsize for a in args)
    return pl.pallas_call(
        kernel,
        out_shape=[jax.ShapeDtypeStruct(*out) for out in outs],
        in_specs=[smem] + [vmem] * (len(args) - 1),
        out_specs=[vmem] * len(outs),
        scratch_shapes=[pltpu.VMEM((rows, rows), F32)] + [pltpu.VMEM((rows, rows), BF16)] * weights,
        compiler_params=pltpu.CompilerParams(vmem_limit_bytes=32 * 2**20),
        cost_estimate=pl.CostEstimate(
            flops=2 * matmuls * rows * rows * width,
            bytes_accessed=2 * size,
            transcendentals=3 * meetings * rows * rows,
        ),
    )(*args)


def imu_exchange(video, imu):
    devices = lax.axis_size("row")

    def mixed(even, odd):
        return [(r, (r + (odd if r % 2 else even)) % devices) for r in range(devices)]

    swap = [(r, r ^ 1) for r in range(devices)]
    imu_two = shifted(imu, "row", 2)
    video_two = shifted(video, "row", -2)
    imu_swap = moved(imu_two, "row", swap)
    video_swap = moved(video_two, "row", swap)
    imu_mixed = moved(imu, "row", mixed(1, 3))
    video_mixed = moved(video, "row", mixed(-3, -1))
    return (
        (imu_two, (-2, -2), video_two, (2, 2)),
        (imu_swap, (-1, -3), video_swap, (3, 1)),
        (imu_mixed, (-3, -1), video_mixed, (1, 3)),
    )


def audio_chain(scalars, ids, all_ids, video, audio, own):
    rows, width = video.shape
    across, inward = [(1, 2), (2, 1)], [(0, 1), (3, 2)]
    outward, beyond = [(1, 0), (2, 3)], [(0, 2), (3, 1)]
    loss, video_grad, grad = own
    half = rows // CHUNKS
    line, square, piece = (1, rows), (rows, width), (half, width)

    middle = moved(audio, "col", across)
    outer_video = moved(video, "col", inward)
    far = moved(audio, "col", beyond)
    near = moved(audio, "col", inward)

    loss, outer_loss, video_grad, outer_grad, grad, middle_0, middle_1 = call(
        middle_kernel,
        [(line, F32), (line, F32), (square, F32), (square, F32), (square, F32), (piece, BF16), (piece, BF16)],
        (scalars, ids, all_ids, video, audio, middle, outer_video, loss, video_grad, grad),
        3, 8, rows, width, 2,
    )
    got_middle_0 = moved(middle_0, "col", across)
    loss, outer_loss, video_grad, outer_grad, far_0, far_1 = call(
        far_kernel,
        [(line, F32), (line, F32), (square, F32), (square, BF16), (piece, BF16), (piece, BF16)],
        (scalars, ids, all_ids, video, outer_video, far, loss, outer_loss, video_grad, outer_grad),
        2, 6, rows, width, 2,
    )
    got_far_0 = moved(far_0, "col", across)
    got_far_1 = moved(far_1, "col", across)
    got_middle_1 = moved(middle_1, "col", across)
    got_outer = moved(outer_grad, "col", outward)
    got_loss = moved(outer_loss, "col", outward)
    loss, video_grad, near_0, near_1 = call(
        near_kernel,
        [(line, F32), (square, F32), (piece, F32), (piece, F32)],
        (scalars, ids, all_ids, video, near, loss, video_grad),
        1, 3, rows, width,
    )
    got_near_0 = moved((near_0 + got_far_0.astype(F32)).astype(BF16), "col", outward)
    got_near_1 = moved((near_1 + got_far_1.astype(F32)).astype(BF16), "col", outward)

    place = lax.axis_index("col")
    inner = (place == 1) | (place == 2)
    loss = jnp.where(inner, loss, own[0] + got_loss)
    video_grad = video_grad + got_outer.astype(F32)
    got = [
        m.astype(F32) + n.astype(F32)
        for m, n in ((got_middle_0, got_near_0), (got_middle_1, got_near_1))
    ]
    return loss, video_grad, grad + jnp.concatenate(got, axis=0)


def audio_ring(scalars, video_ids, audio_ids, video, audio, own):
    scale, offset = scale_offset(scalars, AUDIO)
    loss, video_grad, grad = own
    block, tags = audio, audio_ids
    for _ in range(1, STEPS):
        block, tags = shifted((block, tags), "col", 1)
        grad = shifted(grad, "col", 1)
        products = lax.dot_general(
            video, block, (((1,), (1,)), ((), ())), preferred_element_type=F32
        )
        logits = scale * products + offset
        signs = jnp.where(video_ids[:, None] == tags[None, :], 1.0, -1.0)
        weighted = (-signs * jax.nn.sigmoid(-signs * logits) * scale).astype(BF16)
        loss = loss + jnp.sum(jax.nn.softplus(-signs * logits), axis=1)[None, :]
        video_grad = video_grad + jnp.dot(weighted, block, preferred_element_type=F32)
        grad = grad + lax.dot_general(
            weighted, video, (((0,), (0,)), ((), ())), preferred_element_type=F32
        )
    return loss, video_grad, shifted(grad, "col", -(STEPS - 1))


def per_device(
    video, video_ids, imu, imu_ids, audio, audio_ids,
    imu_log_scale, imu_bias, audio_log_scale, audio_bias,
):
    rows, width = video.shape
    line, square = (1, rows), (rows, width)
    scalars = jnp.concatenate(
        [jnp.exp(imu_log_scale), imu_bias, jnp.exp(audio_log_scale), audio_bias]
    )
    ids = jnp.stack([video_ids, imu_ids, audio_ids])
    all_ids = lax.all_gather(ids, ("row", "col"))

    imu_loss, imu_video, imu_grad, audio_loss, audio_video, audio_grad = call(
        own_kernel,
        [(line, F32), (square, F32), (square, F32)] * 2,
        (scalars, ids, video, imu, audio),
        2, 6, rows, width,
    )
    own = (audio_loss, audio_video, audio_grad)
    if lax.axis_size("col") == STEPS:
        audio_out = audio_chain(scalars, ids, all_ids, video, audio, own)
    else:
        audio_out = audio_ring(scalars, video_ids, audio_ids, video, audio, own)
    audio_loss, audio_video, audio_grad = audio_out

    for other_imu, imu_by, other_video, video_by in imu_exchange(video, imu):
        imu_loss, imu_video, imu_grad = call(
            functools.partial(imu_kernel, imu_by, video_by),
            [(line, F32), (square, F32), (square, F32)],
            (scalars, ids, all_ids, video, imu, other_imu, other_video, imu_loss, imu_video, imu_grad),
            2, 4, rows, width,
        )
    row_loss = (imu_loss + audio_loss)[0] / (2.0 * STEPS * rows)
    return (imu_video + audio_video, imu_grad, audio_grad, row_loss)


def solution(mesh):
    rows, vector = P(("row", "col"), None), P(("row", "col"))
    return jax.shard_map(
        per_device,
        mesh=mesh,
        in_specs=(rows, vector, rows, vector, rows, vector, P(), P(), P(), P()),
        out_specs=(rows, rows, rows, vector),
        check_vma=False,
    )
```

```python
import jax
import jax.numpy as jnp
from jax import lax
from jax.experimental import pallas as pl
from jax.experimental.pallas import tpu as pltpu
from jax.sharding import PartitionSpec as P

STEPS = 4
SLAB = 64
COLUMNS = 512
TAG_ROWS = 16
TAG_BASE = 256
MEETING_COST = 2_500_000_000

F32 = jnp.float32
BF16 = jnp.bfloat16


def moved(block, axis, pairs):
    return lax.ppermute(block, axis, pairs)


def shifted(block, axis, by):
    devices = lax.axis_size(axis)
    return moved(block, axis, [(i, (i + by) % devices) for i in range(devices)])


def pack_kernel(*refs):
    blocks, ids, packed = refs[:3], refs[3:6], refs[6:]
    for block, tags, out in zip(blocks, ids, packed):
        rows, width = block.shape
        out[:rows, :] = block[...]
        tag = tags[...].reshape(1, rows)
        high = tag // TAG_BASE
        low = tag - high * TAG_BASE
        wide = jnp.concatenate([high, low, jnp.zeros((TAG_ROWS - 2, rows), jnp.int32)], axis=0)
        out[rows:, :rows] = wide.astype(F32).astype(BF16)
        out[rows:, rows:] = jnp.zeros((TAG_ROWS, width - rows), BF16)


def tags_of(block):
    rows = block.shape[0] - TAG_ROWS
    tags = block[rows:, :rows].astype(F32)
    return tags[0:1] * TAG_BASE + tags[1:2]


def meet(video, partner, scalars, products, weights):
    rows = weights.shape[0]
    log_scale, offset = scalars[0][0], scalars[1][0]
    scale = jnp.exp(jnp.full((1, rows), log_scale, F32))
    products[...] = lax.dot_general(
        partner[:rows, :], video[:rows, :], (((1,), (1,)), ((), ())), preferred_element_type=F32
    )
    video_tags = tags_of(video)
    partner_tags = jnp.transpose(jnp.broadcast_to(tags_of(partner), (8, rows)))[:, :1]
    total = jnp.zeros((8, rows), F32)
    for start in range(0, rows, SLAB):
        part = slice(start, start + SLAB)
        logits = scale * products[part, :] + offset
        same = partner_tags[part, :] == video_tags
        flipped = -logits
        z = jnp.where(same, flipped, logits)
        e = jnp.exp(jnp.minimum(logits, flipped))
        inverse = 1.0 / (1.0 + e)
        sigmoid = jnp.where(z >= 0.0, inverse, e * inverse)
        weights[part, :] = (jnp.where(same, -scale, scale) * sigmoid).astype(BF16)
        log1p = jnp.where(e < 0.005, e * (1.0 - 0.5 * e), jnp.log(1.0 + e))
        losses = jnp.maximum(z, 0.0) + log1p
        total = total + jnp.sum(losses.reshape(SLAB // 8, 8, rows), axis=0)
    return jnp.sum(total, axis=0, keepdims=True)


def column_parts(ref):
    return [slice(c, c + COLUMNS) for c in range(0, ref.shape[1], COLUMNS)]


def to_video(weights, partner, part):
    rows = weights.shape[0]
    return lax.dot_general(
        weights[...], partner[:rows, part], (((0,), (0,)), ((), ())), preferred_element_type=F32
    )


def to_partner(weights, video, part):
    return jnp.dot(weights[...], video[: weights.shape[0], part], preferred_element_type=F32)


def at_inner(loss):
    col = lax.axis_index("col")
    return jnp.where((col == 1) | (col == 2), loss, 0.0)


def own_kernel(
    imu_log_scale, imu_bias, audio_log_scale, audio_bias, video, imu, audio,
    loss, video_grad, imu_grad, audio_grad, products, weights,
):
    loss[...] = meet(video, audio, (audio_log_scale, audio_bias), products, weights)
    for part in column_parts(video):
        video_grad[:, part] = to_video(weights, audio, part)
        audio_grad[:, part] = to_partner(weights, video, part)
    loss[...] += meet(video, imu, (imu_log_scale, imu_bias), products, weights)
    for part in column_parts(video):
        video_grad[:, part] += to_video(weights, imu, part)
        imu_grad[:, part] = to_partner(weights, video, part)


def imu_kernel(
    log_scale, bias, video, imu, other_imu, other_video, loss_in, video_in, grad_in, *refs
):
    *gathered, products, weights = refs
    if len(gathered) == 6:
        audio_in, got, loss, video_grad, grad, audio_grad = gathered
        audio_grad[...] = audio_in[...] + got[...].astype(F32)
    else:
        loss, video_grad, grad = gathered
    scalars = (log_scale, bias)
    loss[...] = loss_in[...] + meet(video, other_imu, scalars, products, weights)
    for part in column_parts(video):
        video_grad[:, part] = video_in[:, part] + to_video(weights, other_imu, part)
    meet(other_video, imu, scalars, products, weights)
    for part in column_parts(video):
        grad[:, part] = grad_in[:, part] + to_partner(weights, other_video, part)


def ring_kernel(
    log_scale, bias, video, audio, loss_in, video_in, grad_in,
    loss, video_grad, grad, products, weights,
):
    loss[...] = loss_in[...] + meet(video, audio, (log_scale, bias), products, weights)
    for part in column_parts(video):
        video_grad[:, part] = video_in[:, part] + to_video(weights, audio, part)
        grad[:, part] = grad_in[:, part] + to_partner(weights, video, part)


def middle_kernel(
    log_scale, bias, video, pair_video, audio, middle, loss_in, video_in, grad_in,
    loss, pair_loss, video_grad, pair_grad, grad, sums, products, weights, pair_weights,
):
    scalars = (log_scale, bias)
    loss[...] = loss_in[...] + at_inner(meet(video, middle, scalars, products, weights))
    of_pair = at_inner(meet(pair_video, middle, scalars, products, pair_weights))
    for part in column_parts(video):
        both = to_partner(weights, video, part) + to_partner(pair_weights, pair_video, part)
        sums[:, part] = both.astype(BF16)
        video_grad[:, part] = video_in[:, part] + to_video(weights, middle, part)
        pair_grad[:, part] = to_video(pair_weights, middle, part)
    pair_loss[...] = of_pair + meet(pair_video, audio, scalars, products, weights)
    for part in column_parts(video):
        pair_grad[:, part] += to_video(weights, audio, part)
        grad[:, part] = grad_in[:, part] + to_partner(weights, pair_video, part)


def far_kernel(
    log_scale, bias, video, pair_video, far, loss_in, pair_loss_in, video_in, pair_in,
    loss, pair_loss, video_grad, pair_grad, sums, products, weights, pair_weights,
):
    scalars = (log_scale, bias)
    loss[...] = loss_in[...] + at_inner(meet(video, far, scalars, products, weights))
    pair_loss[...] = pair_loss_in[...] + at_inner(
        meet(pair_video, far, scalars, products, pair_weights)
    )
    for part in column_parts(video):
        both = to_partner(weights, video, part) + to_partner(pair_weights, pair_video, part)
        sums[:, part] = both.astype(BF16)
        video_grad[:, part] = video_in[:, part] + to_video(weights, far, part)
        pair_grad[:, part] = (pair_in[:, part] + to_video(pair_weights, far, part)).astype(BF16)


def call(kernel, outs, scalars, args, rows=None, weights=1, meetings=2):
    smem, vmem = pl.BlockSpec(memory_space=pltpu.SMEM), pl.BlockSpec(memory_space=pltpu.VMEM)
    scratch = []
    if rows is not None:
        scratch = [pltpu.VMEM((rows, rows), F32)] + [pltpu.VMEM((rows, rows), BF16)] * weights
    return pl.pallas_call(
        kernel,
        out_shape=[jax.ShapeDtypeStruct(*out) for out in outs],
        in_specs=[smem] * len(scalars) + [vmem] * len(args),
        out_specs=[vmem] * len(outs),
        scratch_shapes=scratch,
        compiler_params=pltpu.CompilerParams(vmem_limit_bytes=20 * 2**20),
        cost_estimate=pl.CostEstimate(
            flops=0 if rows is None else meetings * MEETING_COST,
            bytes_accessed=2 * sum(a.size * a.dtype.itemsize for a in args),
            transcendentals=0,
        ),
    )(*scalars, *args)


def imu_exchange(video, imu):
    devices = lax.axis_size("row")

    def mixed(even, odd):
        return [(r, (r + (odd if r % 2 else even)) % devices) for r in range(devices)]

    swap = [(r, r ^ 1) for r in range(devices)]
    imu_two = shifted(imu, "row", 2)
    video_two = shifted(video, "row", -2)
    imu_swap = moved(imu_two, "row", swap)
    video_swap = moved(video_two, "row", swap)
    imu_mixed = moved(imu, "row", mixed(1, 3))
    video_mixed = moved(video, "row", mixed(-3, -1))
    return (imu_two, video_two), (imu_swap, video_swap), (imu_mixed, video_mixed)


def per_device(
    video, video_ids, imu, imu_ids, audio, audio_ids,
    imu_log_scale, imu_bias, audio_log_scale, audio_bias,
):
    rows, width = video.shape
    line, square, narrow = ((1, rows), F32), ((rows, width), F32), ((rows, width), BF16)
    packed = ((rows + TAG_ROWS, width), BF16)
    of_imu, of_audio = (imu_log_scale, imu_bias), (audio_log_scale, audio_bias)
    chain = lax.axis_size("col") == STEPS
    pair, across = [(0, 1), (1, 0), (2, 3), (3, 2)], [(1, 2), (2, 1)]
    inward, outward = [(0, 2), (3, 1)], [(2, 0), (1, 3)]

    video, imu, audio = call(
        pack_kernel, [packed] * 3, (), (video, imu, audio, video_ids, imu_ids, audio_ids)
    )
    if chain:
        middle = moved(audio, "col", across)
        pair_video = moved(video, "col", pair)
        far = moved(audio, "col", inward)
    by_two, by_swap, by_mixed = imu_exchange(video, imu)

    def imu_stage(partners, loss, video_grad, imu_grad, *gathered):
        args = (video, imu, *partners, loss, video_grad, imu_grad, *gathered)
        outs = [line, square, square] + [square] * (len(gathered) > 0)
        return call(imu_kernel, outs, of_imu, args, rows)

    loss, video_grad, imu_grad, grad = call(
        own_kernel, [line, square, square, square], of_imu + of_audio, (video, imu, audio), rows
    )
    loss, video_grad, imu_grad = imu_stage(by_two, loss, video_grad, imu_grad)
    if chain:
        loss, pair_loss, video_grad, pair_grad, grad, middle_sums = call(
            middle_kernel,
            [line, line, square, square, square, narrow],
            of_audio,
            (video, pair_video, audio, middle, loss, video_grad, grad),
            rows, 2, 3,
        )
        got_middle = moved(middle_sums, "col", across)
    loss, video_grad, imu_grad = imu_stage(by_swap, loss, video_grad, imu_grad)
    if chain:
        loss, pair_loss, video_grad, pair_grad, far_sums = call(
            far_kernel,
            [line, line, square, narrow, narrow],
            of_audio,
            (video, pair_video, far, loss, pair_loss, video_grad, pair_grad),
            rows, 2,
        )
        got_far = moved(far_sums, "col", outward)
        got_video = moved(pair_grad, "col", pair)
        got_loss = moved(pair_loss, "col", pair)
    if chain:
        loss, video_grad, imu_grad, grad = imu_stage(
            by_mixed, loss, video_grad, imu_grad, grad, got_middle
        )
        grad = grad + got_far.astype(F32)
        video_grad = video_grad + got_video.astype(F32)
        loss = loss + got_loss
    else:
        loss, video_grad, imu_grad = imu_stage(by_mixed, loss, video_grad, imu_grad)
        for _ in range(1, STEPS):
            audio = shifted(audio, "col", 1)
            grad = shifted(grad, "col", 1)
            args = (video, audio, loss, video_grad, grad)
            loss, video_grad, grad = call(
                ring_kernel, [line, square, square], of_audio, args, rows
            )
        grad = shifted(grad, "col", -(STEPS - 1))
    return (video_grad, imu_grad, grad, loss[0] / (2.0 * STEPS * rows))


def solution(mesh):
    rows, vector = P(("row", "col"), None), P(("row", "col"))
    return jax.shard_map(
        per_device,
        mesh=mesh,
        in_specs=(rows, vector, rows, vector, rows, vector, P(), P(), P(), P()),
        out_specs=(rows, rows, rows, vector),
        check_vma=False,
    )
```

```python
import jax
import jax.numpy as jnp
from jax import lax
from jax.experimental import pallas as pl
from jax.experimental.pallas import tpu as pltpu
from jax.sharding import PartitionSpec as P

STEPS = 4
SLAB = 64
COLUMNS = 512
TAG_ROWS = 16
TAG_BASE = 256
MEETING_COST = 2_500_000_000

F32 = jnp.float32
BF16 = jnp.bfloat16


def moved(block, axis, pairs):
    return lax.ppermute(block, axis, pairs)


def shifted(block, axis, by):
    devices = lax.axis_size(axis)
    return moved(block, axis, [(i, (i + by) % devices) for i in range(devices)])


def pack_kernel(*refs):
    blocks, ids, packed = refs[:3], refs[3:6], refs[6:9]
    tags, wide, (block_done, tags_done) = refs[9:12], refs[12], refs[13:]
    rows, width = blocks[0].shape
    copies = [
        pltpu.make_async_copy(block, out.at[:rows, :], block_done.at[k])
        for k, (block, out) in enumerate(zip(blocks, packed))
    ]
    tag_copies = [
        pltpu.make_async_copy(source, tags[k], tags_done.at[k]) for k, source in enumerate(ids)
    ]
    for copy in tag_copies + copies:
        copy.start()
    for copy in tag_copies:
        copy.wait()
    for k in range(3):
        tag = tags[k][...].reshape(1, rows)
        high = tag // TAG_BASE
        low = tag - high * TAG_BASE
        both = jnp.concatenate([high, low, jnp.zeros((TAG_ROWS - 2, rows), jnp.int32)], axis=0)
        wide[k, :, :rows] = both.astype(F32).astype(BF16)
        wide[k, :, rows:] = jnp.zeros((TAG_ROWS, width - rows), BF16)
    tails = [
        pltpu.make_async_copy(wide.at[k], out.at[rows:, :], tags_done.at[k])
        for k, out in enumerate(packed)
    ]
    for copy in tails:
        copy.start()
    for copy in copies + tails:
        copy.wait()


def pack(blocks, ids):
    rows, width = blocks[0].shape
    hbm = pl.BlockSpec(memory_space=pltpu.HBM)
    return pl.pallas_call(
        pack_kernel,
        out_shape=[jax.ShapeDtypeStruct((rows + TAG_ROWS, width), BF16)] * 3,
        in_specs=[hbm] * 6,
        out_specs=[hbm] * 3,
        scratch_shapes=[
            *[pltpu.VMEM((rows,), jnp.int32)] * 3,
            pltpu.VMEM((3, TAG_ROWS, width), BF16),
            pltpu.SemaphoreType.DMA((3,)),
            pltpu.SemaphoreType.DMA((3,)),
        ],
        compiler_params=pltpu.CompilerParams(vmem_limit_bytes=60 * 2**20),
    )(*blocks, *ids)


def tags_of(block):
    rows = block.shape[0] - TAG_ROWS
    tags = block[rows:, :rows].astype(F32)
    return tags[0:1] * TAG_BASE + tags[1:2]


def meet(video, partner, scalars, products, weights):
    rows = weights.shape[0]
    log_scale, offset = scalars[0][0], scalars[1][0]
    scale = jnp.exp(jnp.full((1, rows), log_scale, F32))
    products[...] = lax.dot_general(
        partner[:rows, :], video[:rows, :], (((1,), (1,)), ((), ())), preferred_element_type=F32
    )
    video_tags = tags_of(video)
    partner_tags = jnp.transpose(jnp.broadcast_to(tags_of(partner), (8, rows)))[:, :1]
    total = jnp.zeros((8, rows), F32)
    for start in range(0, rows, SLAB):
        part = slice(start, start + SLAB)
        logits = scale * products[part, :] + offset
        same = partner_tags[part, :] == video_tags
        flipped = -logits
        z = jnp.where(same, flipped, logits)
        e = jnp.exp(jnp.minimum(logits, flipped))
        inverse = 1.0 / (1.0 + e)
        sigmoid = jnp.where(z >= 0.0, inverse, e * inverse)
        weights[part, :] = (jnp.where(same, -scale, scale) * sigmoid).astype(BF16)
        log1p = jnp.where(e < 0.005, e * (1.0 - 0.5 * e), jnp.log(1.0 + e))
        losses = jnp.maximum(z, 0.0) + log1p
        total = total + jnp.sum(losses.reshape(SLAB // 8, 8, rows), axis=0)
    return jnp.sum(total, axis=0, keepdims=True)


def column_parts(ref):
    return [slice(c, c + COLUMNS) for c in range(0, ref.shape[1], COLUMNS)]


def to_video(weights, partner, part):
    rows = weights.shape[0]
    return lax.dot_general(
        weights[...], partner[:rows, part], (((0,), (0,)), ((), ())), preferred_element_type=F32
    )


def to_partner(weights, video, part):
    return jnp.dot(weights[...], video[: weights.shape[0], part], preferred_element_type=F32)


def at_inner(loss):
    col = lax.axis_index("col")
    return jnp.where((col == 1) | (col == 2), loss, 0.0)


def own_kernel(
    imu_log_scale, imu_bias, audio_log_scale, audio_bias, video, imu, audio,
    loss, video_grad, imu_grad, audio_grad, products, weights,
):
    loss[...] = meet(video, audio, (audio_log_scale, audio_bias), products, weights)
    for part in column_parts(video):
        video_grad[:, part] = to_video(weights, audio, part)
        audio_grad[:, part] = to_partner(weights, video, part)
    loss[...] += meet(video, imu, (imu_log_scale, imu_bias), products, weights)
    for part in column_parts(video):
        video_grad[:, part] += to_video(weights, imu, part)
        imu_grad[:, part] = to_partner(weights, video, part)


def imu_kernel(
    log_scale, bias, video, imu, other_imu, other_video, loss_in, video_in, grad_in, *refs
):
    *gathered, products, weights = refs
    if len(gathered) == 6:
        audio_in, got, loss, video_grad, grad, audio_grad = gathered
        audio_grad[...] = audio_in[...] + got[...].astype(F32)
    else:
        loss, video_grad, grad = gathered
    scalars = (log_scale, bias)
    loss[...] = loss_in[...] + meet(video, other_imu, scalars, products, weights)
    for part in column_parts(video):
        video_grad[:, part] = video_in[:, part] + to_video(weights, other_imu, part)
    meet(other_video, imu, scalars, products, weights)
    for part in column_parts(video):
        grad[:, part] = grad_in[:, part] + to_partner(weights, other_video, part)


def ring_kernel(
    log_scale, bias, video, audio, loss_in, video_in, grad_in,
    loss, video_grad, grad, products, weights,
):
    loss[...] = loss_in[...] + meet(video, audio, (log_scale, bias), products, weights)
    for part in column_parts(video):
        video_grad[:, part] = video_in[:, part] + to_video(weights, audio, part)
        grad[:, part] = grad_in[:, part] + to_partner(weights, video, part)


def middle_kernel(
    log_scale, bias, video, pair_video, audio, middle, loss_in, video_in, grad_in,
    loss, pair_loss, video_grad, pair_grad, grad, sums, products, weights, pair_weights,
):
    scalars = (log_scale, bias)
    loss[...] = loss_in[...] + at_inner(meet(video, middle, scalars, products, weights))
    of_pair = at_inner(meet(pair_video, middle, scalars, products, pair_weights))
    for part in column_parts(video):
        both = to_partner(weights, video, part) + to_partner(pair_weights, pair_video, part)
        sums[:, part] = both.astype(BF16)
        video_grad[:, part] = video_in[:, part] + to_video(weights, middle, part)
        pair_grad[:, part] = to_video(pair_weights, middle, part)
    pair_loss[...] = of_pair + meet(pair_video, audio, scalars, products, weights)
    for part in column_parts(video):
        pair_grad[:, part] += to_video(weights, audio, part)
        grad[:, part] = grad_in[:, part] + to_partner(weights, pair_video, part)


def far_kernel(
    log_scale, bias, video, pair_video, far, loss_in, pair_loss_in, video_in, pair_in,
    loss, video_grad, pair_grad, sums, products, weights, pair_weights,
):
    scalars = (log_scale, bias)
    rows, width = sums.shape
    loss[...] = loss_in[...] + at_inner(meet(video, far, scalars, products, weights))
    left = pair_loss_in[...] + at_inner(meet(pair_video, far, scalars, products, pair_weights))
    terms = []
    for _ in range(3):
        terms.append(left.astype(BF16).astype(F32))
        left = left - terms[-1]
    terms.append(jnp.zeros((TAG_ROWS - 3, rows), F32))
    pair_grad[rows:, :rows] = jnp.concatenate(terms, axis=0).astype(BF16)
    pair_grad[rows:, rows:] = jnp.zeros((TAG_ROWS, width - rows), BF16)
    for part in column_parts(video):
        both = to_partner(weights, video, part) + to_partner(pair_weights, pair_video, part)
        sums[:, part] = both.astype(BF16)
        video_grad[:, part] = video_in[:, part] + to_video(weights, far, part)
        pair_sum = pair_in[:, part] + to_video(pair_weights, far, part)
        pair_grad[:rows, part] = pair_sum.astype(BF16)


def call(kernel, outs, scalars, args, rows=None, weights=1, meetings=2):
    smem, vmem = pl.BlockSpec(memory_space=pltpu.SMEM), pl.BlockSpec(memory_space=pltpu.VMEM)
    scratch = []
    if rows is not None:
        scratch = [pltpu.VMEM((rows, rows), F32)] + [pltpu.VMEM((rows, rows), BF16)] * weights
    return pl.pallas_call(
        kernel,
        out_shape=[jax.ShapeDtypeStruct(*out) for out in outs],
        in_specs=[smem] * len(scalars) + [vmem] * len(args),
        out_specs=[vmem] * len(outs),
        scratch_shapes=scratch,
        compiler_params=pltpu.CompilerParams(vmem_limit_bytes=20 * 2**20),
        cost_estimate=pl.CostEstimate(
            flops=0 if rows is None else meetings * MEETING_COST,
            bytes_accessed=2 * sum(a.size * a.dtype.itemsize for a in args),
            transcendentals=0,
        ),
    )(*scalars, *args)


def imu_exchange(video, imu):
    devices = lax.axis_size("row")

    def mixed(even, odd):
        return [(r, (r + (odd if r % 2 else even)) % devices) for r in range(devices)]

    swap = [(r, r ^ 1) for r in range(devices)]
    imu_two = shifted(imu, "row", 2)
    video_two = shifted(video, "row", -2)
    imu_swap = moved(imu_two, "row", swap)
    video_swap = moved(video_two, "row", swap)
    imu_mixed = moved(imu, "row", mixed(1, 3))
    video_mixed = moved(video, "row", mixed(-3, -1))
    return (imu_two, video_two), (imu_swap, video_swap), (imu_mixed, video_mixed)


def per_device(
    video, video_ids, imu, imu_ids, audio, audio_ids,
    imu_log_scale, imu_bias, audio_log_scale, audio_bias,
):
    rows, width = video.shape
    line, square, narrow = ((1, rows), F32), ((rows, width), F32), ((rows, width), BF16)
    packed = ((rows + TAG_ROWS, width), BF16)
    of_imu, of_audio = (imu_log_scale, imu_bias), (audio_log_scale, audio_bias)
    chain = lax.axis_size("col") == STEPS
    pair, across = [(0, 1), (1, 0), (2, 3), (3, 2)], [(1, 2), (2, 1)]
    inward, outward = [(0, 2), (3, 1)], [(2, 0), (1, 3)]

    video, imu, audio = pack((video, imu, audio), (video_ids, imu_ids, audio_ids))
    if chain:
        middle = moved(audio, "col", across)
        pair_video = moved(video, "col", pair)
        far = moved(audio, "col", inward)
    by_two, by_swap, by_mixed = imu_exchange(video, imu)

    def imu_stage(partners, loss, video_grad, imu_grad, *gathered):
        args = (video, imu, *partners, loss, video_grad, imu_grad, *gathered)
        outs = [line, square, square] + [square] * (len(gathered) > 0)
        return call(imu_kernel, outs, of_imu, args, rows)

    loss, video_grad, imu_grad, grad = call(
        own_kernel, [line, square, square, square], of_imu + of_audio, (video, imu, audio), rows
    )
    if chain:
        loss, pair_loss, video_grad, pair_grad, grad, middle_sums = call(
            middle_kernel,
            [line, line, square, square, square, narrow],
            of_audio,
            (video, pair_video, audio, middle, loss, video_grad, grad),
            rows, 2, 3,
        )
        got_middle = moved(middle_sums, "col", across)
        loss, video_grad, pair_grad, far_sums = call(
            far_kernel,
            [line, square, packed, narrow],
            of_audio,
            (video, pair_video, far, loss, pair_loss, video_grad, pair_grad),
            rows, 2,
        )
        got_video = moved(pair_grad, "col", pair)
        got_far = moved(far_sums, "col", outward)
    loss, video_grad, imu_grad = imu_stage(by_mixed, loss, video_grad, imu_grad)
    loss, video_grad, imu_grad = imu_stage(by_two, loss, video_grad, imu_grad)
    if chain:
        loss, video_grad, imu_grad, grad = imu_stage(
            by_swap, loss, video_grad, imu_grad, grad, got_middle
        )
        grad = grad + got_far.astype(F32)
        video_grad = video_grad + got_video[:rows].astype(F32)
        loss = loss + jnp.sum(got_video[rows:, :rows].astype(F32), axis=0, keepdims=True)
    else:
        loss, video_grad, imu_grad = imu_stage(by_swap, loss, video_grad, imu_grad)
        for _ in range(1, STEPS):
            audio = shifted(audio, "col", 1)
            grad = shifted(grad, "col", 1)
            args = (video, audio, loss, video_grad, grad)
            loss, video_grad, grad = call(
                ring_kernel, [line, square, square], of_audio, args, rows
            )
        grad = shifted(grad, "col", -(STEPS - 1))
    return (video_grad, imu_grad, grad, loss[0] / (2.0 * STEPS * rows))


def solution(mesh):
    rows, vector = P(("row", "col"), None), P(("row", "col"))
    return jax.shard_map(
        per_device,
        mesh=mesh,
        in_specs=(rows, vector, rows, vector, rows, vector, P(), P(), P(), P()),
        out_specs=(rows, rows, rows, vector),
        check_vma=False,
    )
```

```python
import jax
import jax.numpy as jnp
from jax import lax
from jax.experimental import pallas as pl
from jax.experimental.pallas import tpu as pltpu
from jax.sharding import PartitionSpec as P

STEPS = 4
SLAB = 64
COLUMNS = 512
TAG_ROWS = 16
TAG_BASE = 256
MEETING_COST = 2_500_000_000

F32 = jnp.float32
BF16 = jnp.bfloat16


def pack_kernel(*refs):
    blocks, ids, packed = refs[:3], refs[3:6], refs[6:9]
    tags, (block_done, tags_done) = refs[9:12], refs[12:]
    rows, width = blocks[0].shape
    copies = [
        pltpu.make_async_copy(block, out.at[:rows, :], block_done.at[k])
        for k, (block, out) in enumerate(zip(blocks, packed))
    ]
    tag_copies = [
        pltpu.make_async_copy(source, tags[k], tags_done.at[k]) for k, source in enumerate(ids)
    ]
    for copy in tag_copies + copies:
        copy.start()
    for copy in tag_copies:
        copy.wait()
    for k, out in enumerate(packed):
        tag = tags[k][...].reshape(1, rows)
        high = tag // TAG_BASE
        low = tag - high * TAG_BASE
        both = jnp.concatenate([high, low, jnp.zeros((TAG_ROWS - 2, rows), jnp.int32)], axis=0)
        out[rows:, :rows] = both.astype(F32).astype(BF16)
        out[rows:, rows:] = jnp.zeros((TAG_ROWS, width - rows), BF16)
    for copy in copies:
        copy.wait()


def pack(blocks, ids):
    rows, width = blocks[0].shape
    hbm, vmem = pl.BlockSpec(memory_space=pltpu.HBM), pl.BlockSpec(memory_space=pltpu.VMEM)
    return pl.pallas_call(
        pack_kernel,
        out_shape=[jax.ShapeDtypeStruct((rows + TAG_ROWS, width), BF16)] * 3,
        in_specs=[hbm] * 6,
        out_specs=[vmem] * 3,
        scratch_shapes=[
            *[pltpu.VMEM((rows,), jnp.int32)] * 3,
            pltpu.SemaphoreType.DMA((3,)),
            pltpu.SemaphoreType.DMA((3,)),
        ],
        compiler_params=pltpu.CompilerParams(vmem_limit_bytes=60 * 2**20),
    )(*blocks, *ids)


def tags_of(block):
    rows = block.shape[0] - TAG_ROWS
    tags = block[rows:, :rows].astype(F32)
    return tags[0:1] * TAG_BASE + tags[1:2]


def meet(video, partner, scalars, products, weights):
    rows = weights.shape[0]
    log_scale, offset = scalars[0][0], scalars[1][0]
    scale = jnp.exp(jnp.full((1, rows), log_scale, F32))
    products[...] = lax.dot_general(
        partner[:rows, :], video[:rows, :], (((1,), (1,)), ((), ())), preferred_element_type=F32
    )
    video_tags = tags_of(video)
    partner_tags = jnp.transpose(jnp.broadcast_to(tags_of(partner), (8, rows)))[:, :1]
    total = jnp.zeros((8, rows), F32)
    for start in range(0, rows, SLAB):
        part = slice(start, start + SLAB)
        logits = scale * products[part, :] + offset
        same = partner_tags[part, :] == video_tags
        flipped = -logits
        z = jnp.where(same, flipped, logits)
        e = jnp.exp(jnp.minimum(logits, flipped))
        inverse = 1.0 / (1.0 + e)
        sigmoid = jnp.where(z >= 0.0, inverse, e * inverse)
        weights[part, :] = (jnp.where(same, -scale, scale) * sigmoid).astype(BF16)
        log1p = jnp.where(e < 0.005, e * (1.0 - 0.5 * e), jnp.log(1.0 + e))
        losses = jnp.maximum(z, 0.0) + log1p
        total = total + jnp.sum(losses.reshape(SLAB // 8, 8, rows), axis=0)
    return jnp.sum(total, axis=0, keepdims=True)


def column_parts(ref):
    return [slice(c, c + COLUMNS) for c in range(0, ref.shape[1], COLUMNS)]


def to_video(weights, partner, part):
    rows = weights.shape[0]
    return lax.dot_general(
        weights[...], partner[:rows, part], (((0,), (0,)), ((), ())), preferred_element_type=F32
    )


def to_partner(weights, video, part):
    return jnp.dot(weights[...], video[: weights.shape[0], part], preferred_element_type=F32)


def own_kernel(
    imu_log_scale, imu_bias, audio_log_scale, audio_bias, video, imu, audio,
    loss, video_grad, imu_grad, audio_grad, products, weights,
):
    loss[...] = meet(video, audio, (audio_log_scale, audio_bias), products, weights)
    for part in column_parts(video):
        video_grad[:, part] = to_video(weights, audio, part)
        audio_grad[:, part] = to_partner(weights, video, part)
    loss[...] += meet(video, imu, (imu_log_scale, imu_bias), products, weights)
    for part in column_parts(video):
        video_grad[:, part] += to_video(weights, imu, part)
        imu_grad[:, part] = to_partner(weights, video, part)


def near_kernel(
    log_scale, bias, other_video, partner, grad_in,
    other_loss, other_grad, grad, products, weights,
):
    other_loss[...] = meet(other_video, partner, (log_scale, bias), products, weights)
    for part in column_parts(partner):
        other_grad[:, part] = to_video(weights, partner, part)
        grad[:, part] = grad_in[:, part] + to_partner(weights, other_video, part)


def far_kernel(
    log_scale, bias, video, other_video, partner, loss_in, video_in, other_loss_in, other_in,
    loss, video_grad, other_grad, sums, products, weights, other_weights,
):
    scalars = (log_scale, bias)
    rows, width = sums.shape
    loss[...] = loss_in[...] + meet(video, partner, scalars, products, weights)
    left = other_loss_in[...] + meet(other_video, partner, scalars, products, other_weights)
    terms = []
    for _ in range(3):
        terms.append(left.astype(BF16).astype(F32))
        left = left - terms[-1]
    terms.append(jnp.zeros((TAG_ROWS - 3, rows), F32))
    other_grad[rows:, :rows] = jnp.concatenate(terms, axis=0).astype(BF16)
    other_grad[rows:, rows:] = jnp.zeros((TAG_ROWS, width - rows), BF16)
    for part in column_parts(video):
        both = to_partner(weights, video, part) + to_partner(other_weights, other_video, part)
        sums[:, part] = both.astype(BF16)
        other_sum = other_in[:, part] + to_video(other_weights, partner, part)
        other_grad[:rows, part] = other_sum.astype(BF16)
        video_grad[:, part] = video_in[:, part] + to_video(weights, partner, part)


def call(kernel, outs, scalars, args, rows, weights=1, meetings=2):
    smem, vmem = pl.BlockSpec(memory_space=pltpu.SMEM), pl.BlockSpec(memory_space=pltpu.VMEM)
    scratch = [pltpu.VMEM((rows, rows), F32)] + [pltpu.VMEM((rows, rows), BF16)] * weights
    return pl.pallas_call(
        kernel,
        out_shape=[jax.ShapeDtypeStruct(*out) for out in outs],
        in_specs=[smem] * len(scalars) + [vmem] * len(args),
        out_specs=[vmem] * len(outs),
        scratch_shapes=scratch,
        compiler_params=pltpu.CompilerParams(vmem_limit_bytes=20 * 2**20),
        cost_estimate=pl.CostEstimate(
            flops=meetings * MEETING_COST,
            bytes_accessed=2 * sum(a.size * a.dtype.itemsize for a in args),
            transcendentals=0,
        ),
    )(*scalars, *args)


class Tile:
    def __init__(self, axis):
        self.axis = axis
        devices = lax.axis_size(axis)
        if devices == STEPS:
            self.video = [(p ^ 1, p) for p in range(devices)]
            self.partner = [(p ^ 2, p) for p in range(devices)]
        else:
            self.video = [((p + 1) % devices, p) for p in range(devices)]
            self.partner = [((p - 2) % devices, p) for p in range(devices)]

    def bring_video(self, block):
        return lax.ppermute(block, self.axis, self.video)

    def bring_partner(self, block):
        return lax.ppermute(block, self.axis, self.partner)

    def return_video(self, block):
        return lax.ppermute(block, self.axis, [(b, a) for a, b in self.video])

    def return_partner(self, block):
        return lax.ppermute(block, self.axis, [(b, a) for a, b in self.partner])


def per_device(
    video, video_ids, imu, imu_ids, audio, audio_ids,
    imu_log_scale, imu_bias, audio_log_scale, audio_bias,
):
    rows, width = video.shape
    line, square, narrow = ((1, rows), F32), ((rows, width), F32), ((rows, width), BF16)
    packed = ((rows + TAG_ROWS, width), BF16)
    of_imu, of_audio = (imu_log_scale, imu_bias), (audio_log_scale, audio_bias)
    along_row, along_col = Tile("row"), Tile("col")

    video, imu, audio = pack((video, imu, audio), (video_ids, imu_ids, audio_ids))
    col_video = along_col.bring_video(video)
    col_audio = along_col.bring_partner(audio)
    row_imu = along_row.bring_partner(imu)
    row_video = along_row.bring_video(video)

    def near(scalars, other_video, partner, grad):
        args = (other_video, partner, grad)
        return call(near_kernel, [line, square, square], scalars, args, rows, 1, 1)

    def far(scalars, *args):
        return call(far_kernel, [line, square, packed, narrow], scalars, args, rows, 2)

    loss, video_grad, imu_grad, audio_grad = call(
        own_kernel, [line, square, square, square], of_imu + of_audio, (video, imu, audio), rows
    )
    col_loss, col_grad, audio_grad = near(of_audio, col_video, audio, audio_grad)
    loss, video_grad, col_grad, audio_sums = far(
        of_audio, video, col_video, col_audio, loss, video_grad, col_loss, col_grad
    )
    got_audio = along_col.return_partner(audio_sums)
    got_col = along_col.return_video(col_grad)
    row_loss, row_grad, imu_grad = near(of_imu, row_video, imu, imu_grad)
    loss, video_grad, row_grad, imu_sums = far(
        of_imu, video, row_video, row_imu, loss, video_grad, row_loss, row_grad
    )
    got_imu = along_row.return_partner(imu_sums)
    got_row = along_row.return_video(row_grad)

    for got in (got_col, got_row):
        video_grad = video_grad + got[:rows].astype(F32)
        loss = loss + jnp.sum(got[rows:, :rows].astype(F32), axis=0, keepdims=True)
    imu_grad = imu_grad + got_imu.astype(F32)
    audio_grad = audio_grad + got_audio.astype(F32)
    return (video_grad, imu_grad, audio_grad, loss[0] / (2.0 * STEPS * rows))


def solution(mesh):
    rows, vector = P(("row", "col"), None), P(("row", "col"))
    return jax.shard_map(
        per_device,
        mesh=mesh,
        in_specs=(rows, vector, rows, vector, rows, vector, P(), P(), P(), P()),
        out_specs=(rows, rows, rows, vector),
        check_vma=False,
    )
```

```python
import jax
import jax.numpy as jnp
from jax import lax
from jax.experimental import pallas as pl
from jax.experimental.pallas import tpu as pltpu
from jax.sharding import PartitionSpec as P

STEPS = 4
SLAB = 64
COLUMNS = 512
TAG_ROWS = 16
TAG_BASE = 256
OWN_COST = COL_COST = ROW_COST = 2_500_000_000
SUM_COST = 40_000_000_000

F32 = jnp.float32
BF16 = jnp.bfloat16


def pack_kernel(*refs):
    blocks, ids, packed = refs[:3], refs[3:6], refs[6:9]
    tags, (block_done, tags_done) = refs[9:12], refs[12:]
    rows, width = blocks[0].shape
    copies = [
        pltpu.make_async_copy(block, out.at[:rows, :], block_done.at[k])
        for k, (block, out) in enumerate(zip(blocks, packed))
    ]
    tag_copies = [
        pltpu.make_async_copy(source, tags[k], tags_done.at[k]) for k, source in enumerate(ids)
    ]
    for copy in tag_copies + copies:
        copy.start()
    for copy in tag_copies:
        copy.wait()
    for k, out in enumerate(packed):
        tag = tags[k][...].reshape(1, rows)
        high = tag // TAG_BASE
        low = tag - high * TAG_BASE
        both = jnp.concatenate([high, low, jnp.zeros((TAG_ROWS - 2, rows), jnp.int32)], axis=0)
        out[rows:, :rows] = both.astype(F32).astype(BF16)
        out[rows:, rows:] = jnp.zeros((TAG_ROWS, width - rows), BF16)
    for copy in copies:
        copy.wait()


def pack(blocks, ids):
    rows, width = blocks[0].shape
    hbm, vmem = pl.BlockSpec(memory_space=pltpu.HBM), pl.BlockSpec(memory_space=pltpu.VMEM)
    return pl.pallas_call(
        pack_kernel,
        out_shape=[jax.ShapeDtypeStruct((rows + TAG_ROWS, width), BF16)] * 3,
        in_specs=[hbm] * 6,
        out_specs=[vmem] * 3,
        scratch_shapes=[
            *[pltpu.VMEM((rows,), jnp.int32)] * 3,
            pltpu.SemaphoreType.DMA((3,)),
            pltpu.SemaphoreType.DMA((3,)),
        ],
        compiler_params=pltpu.CompilerParams(vmem_limit_bytes=60 * 2**20),
    )(*blocks, *ids)


def tags_of(block):
    rows = block.shape[0] - TAG_ROWS
    tags = block[rows:, :rows].astype(F32)
    return tags[0:1] * TAG_BASE + tags[1:2]


def meet(video, partner, scalars, products, weights):
    rows = weights.shape[0]
    log_scale, offset = scalars[0][0], scalars[1][0]
    scale = jnp.exp(jnp.full((1, rows), log_scale, F32))
    products[...] = lax.dot_general(
        partner[:rows, :], video[:rows, :], (((1,), (1,)), ((), ())), preferred_element_type=F32
    )
    video_tags = tags_of(video)
    partner_tags = jnp.transpose(jnp.broadcast_to(tags_of(partner), (8, rows)))[:, :1]
    total = jnp.zeros((8, rows), F32)
    for start in range(0, rows, SLAB):
        part = slice(start, start + SLAB)
        logits = scale * products[part, :] + offset
        same = partner_tags[part, :] == video_tags
        flipped = -logits
        z = jnp.where(same, flipped, logits)
        e = jnp.exp(jnp.minimum(logits, flipped))
        inverse = 1.0 / (1.0 + e)
        sigmoid = jnp.where(z >= 0.0, inverse, e * inverse)
        weights[part, :] = (jnp.where(same, -scale, scale) * sigmoid).astype(BF16)
        log1p = jnp.where(e < 0.005, e * (1.0 - 0.5 * e), jnp.log(1.0 + e))
        losses = jnp.maximum(z, 0.0) + log1p
        total = total + jnp.sum(losses.reshape(SLAB // 8, 8, rows), axis=0)
    return jnp.sum(total, axis=0, keepdims=True)


def column_parts(ref):
    return [slice(c, c + COLUMNS) for c in range(0, ref.shape[1], COLUMNS)]


def to_video(weights, partner, part):
    rows = weights.shape[0]
    return lax.dot_general(
        weights[...], partner[:rows, part], (((0,), (0,)), ((), ())), preferred_element_type=F32
    )


def to_partner(weights, video, part):
    return jnp.dot(weights[...], video[: weights.shape[0], part], preferred_element_type=F32)


def own_kernel(
    imu_log_scale, imu_bias, audio_log_scale, audio_bias, video, imu, audio,
    loss, video_grad, imu_grad, audio_grad, products, weights,
):
    loss[...] = meet(video, audio, (audio_log_scale, audio_bias), products, weights)
    for part in column_parts(video):
        video_grad[:, part] = to_video(weights, audio, part)
        audio_grad[:, part] = to_partner(weights, video, part)
    loss[...] += meet(video, imu, (imu_log_scale, imu_bias), products, weights)
    for part in column_parts(video):
        video_grad[:, part] += to_video(weights, imu, part)
        imu_grad[:, part] = to_partner(weights, video, part)


def near_kernel(
    log_scale, bias, other_video, partner, grad_in,
    other_loss, other_grad, grad, products, weights,
):
    other_loss[...] = meet(other_video, partner, (log_scale, bias), products, weights)
    for part in column_parts(partner):
        other_grad[:, part] = to_video(weights, partner, part)
        grad[:, part] = grad_in[:, part] + to_partner(weights, other_video, part)


def far_kernel(
    log_scale, bias, video, other_video, partner, loss_in, video_in, other_loss_in, other_in,
    loss, video_grad, other_grad, sums, products, weights, other_weights,
):
    scalars = (log_scale, bias)
    rows, width = sums.shape
    loss[...] = loss_in[...] + meet(video, partner, scalars, products, weights)
    left = other_loss_in[...] + meet(other_video, partner, scalars, products, other_weights)
    terms = []
    for _ in range(3):
        terms.append(left.astype(BF16).astype(F32))
        left = left - terms[-1]
    terms.append(jnp.zeros((TAG_ROWS - 3, rows), F32))
    other_grad[rows:, :rows] = jnp.concatenate(terms, axis=0).astype(BF16)
    other_grad[rows:, rows:] = jnp.zeros((TAG_ROWS, width - rows), BF16)
    for part in column_parts(video):
        both = to_partner(weights, video, part) + to_partner(other_weights, other_video, part)
        sums[:, part] = both.astype(BF16)
        other_sum = other_in[:, part] + to_video(other_weights, partner, part)
        other_grad[:rows, part] = other_sum.astype(BF16)
        video_grad[:, part] = video_in[:, part] + to_video(weights, partner, part)


def sum_kernel(got_video, got_partner, video_in, partner_in, loss_in, video_grad, grad, loss):
    rows = video_grad.shape[0]
    grad[...] = partner_in[...] + got_partner[...].astype(F32)
    video_grad[...] = video_in[...] + got_video[:rows, :].astype(F32)
    came = got_video[rows:, :rows].astype(F32)
    loss[...] = loss_in[...] + jnp.sum(came, axis=0, keepdims=True)


def call(kernel, outs, scalars, args, rows, weights=1, cost=OWN_COST):
    smem, vmem = pl.BlockSpec(memory_space=pltpu.SMEM), pl.BlockSpec(memory_space=pltpu.VMEM)
    scratch = [pltpu.VMEM((rows, rows), F32)] + [pltpu.VMEM((rows, rows), BF16)] * weights
    scratch = scratch if weights else []
    return pl.pallas_call(
        kernel,
        out_shape=[jax.ShapeDtypeStruct(*out) for out in outs],
        in_specs=[smem] * len(scalars) + [vmem] * len(args),
        out_specs=[vmem] * len(outs),
        scratch_shapes=scratch,
        compiler_params=pltpu.CompilerParams(vmem_limit_bytes=20 * 2**20),
        cost_estimate=pl.CostEstimate(
            flops=cost,
            bytes_accessed=2 * sum(a.size * a.dtype.itemsize for a in args),
            transcendentals=0,
        ),
    )(*scalars, *args)


class Tile:
    def __init__(self, axis):
        self.axis = axis
        devices = lax.axis_size(axis)
        if devices == STEPS:
            self.video = [(p ^ 1, p) for p in range(devices)]
            self.partner = [(p ^ 2, p) for p in range(devices)]
        else:
            self.video = [((p + 1) % devices, p) for p in range(devices)]
            self.partner = [((p - 2) % devices, p) for p in range(devices)]

    def bring_video(self, block):
        return lax.ppermute(block, self.axis, self.video)

    def bring_partner(self, block):
        return lax.ppermute(block, self.axis, self.partner)

    def return_video(self, block):
        return lax.ppermute(block, self.axis, [(b, a) for a, b in self.video])

    def return_partner(self, block):
        return lax.ppermute(block, self.axis, [(b, a) for a, b in self.partner])


def per_device(
    video, video_ids, imu, imu_ids, audio, audio_ids,
    imu_log_scale, imu_bias, audio_log_scale, audio_bias,
):
    rows, width = video.shape
    line, square, narrow = ((1, rows), F32), ((rows, width), F32), ((rows, width), BF16)
    packed = ((rows + TAG_ROWS, width), BF16)
    of_imu, of_audio = (imu_log_scale, imu_bias), (audio_log_scale, audio_bias)
    along_row, along_col = Tile("row"), Tile("col")

    video, imu, audio = pack((video, imu, audio), (video_ids, imu_ids, audio_ids))
    col_video = along_col.bring_video(video)
    col_audio = along_col.bring_partner(audio)
    row_imu = along_row.bring_partner(imu)
    row_video = along_row.bring_video(video)

    def near(scalars, other_video, partner, grad, cost):
        args = (other_video, partner, grad)
        return call(near_kernel, [line, square, square], scalars, args, rows, 1, cost)

    def far(scalars, *args, cost):
        return call(far_kernel, [line, square, packed, narrow], scalars, args, rows, 2, cost)

    def summed(*args, cost):
        return call(sum_kernel, [square, square, line], (), args, rows, 0, cost)

    loss, video_grad, imu_grad, audio_grad = call(
        own_kernel, [line, square, square, square], of_imu + of_audio, (video, imu, audio), rows
    )
    col_loss, col_grad, audio_grad = near(of_audio, col_video, audio, audio_grad, COL_COST)
    loss, video_grad, col_grad, audio_sums = far(
        of_audio, video, col_video, col_audio, loss, video_grad, col_loss, col_grad, cost=COL_COST
    )
    got_audio = along_col.return_partner(audio_sums)
    got_col = along_col.return_video(col_grad)
    row_loss, row_grad, imu_grad = near(of_imu, row_video, imu, imu_grad, ROW_COST)
    loss, video_grad, row_grad, imu_sums = far(
        of_imu, video, row_video, row_imu, loss, video_grad, row_loss, row_grad, cost=ROW_COST
    )
    got_imu = along_row.return_partner(imu_sums)
    got_row = along_row.return_video(row_grad)

    video_grad, audio_grad, loss = summed(
        got_col, got_audio, video_grad, audio_grad, loss, cost=SUM_COST
    )
    video_grad, imu_grad, loss = summed(
        got_row, got_imu, video_grad, imu_grad, loss, cost=ROW_COST
    )
    return (video_grad, imu_grad, audio_grad, loss[0] / (2.0 * STEPS * rows))


def solution(mesh):
    rows, vector = P(("row", "col"), None), P(("row", "col"))
    return jax.shard_map(
        per_device,
        mesh=mesh,
        in_specs=(rows, vector, rows, vector, rows, vector, P(), P(), P(), P()),
        out_specs=(rows, rows, rows, vector),
        check_vma=False,
    )
```

```python
import jax
import jax.numpy as jnp
from jax import lax
from jax.experimental import pallas as pl
from jax.experimental.pallas import tpu as pltpu
from jax.sharding import PartitionSpec as P

STEPS = 4
SLAB = 64
COLUMNS = 512
SUM_BLOCKS = 4
TAG_ROWS = 16
TAG_BASE = 256
OWN_COST = COL_COST = ROW_COST = 500_000_000
SUM_COST = 40_000_000_000

F32 = jnp.float32
BF16 = jnp.bfloat16


def pack_kernel(*refs):
    blocks, ids, packed = refs[:2], refs[2:4], refs[4:6]
    tags, (block_done, tags_done) = refs[6:8], refs[8:]
    rows, width = blocks[0].shape
    copies = [
        pltpu.make_async_copy(block, out.at[:rows, :], block_done.at[k])
        for k, (block, out) in enumerate(zip(blocks, packed))
    ]
    tag_copies = [
        pltpu.make_async_copy(source, tags[k], tags_done.at[k]) for k, source in enumerate(ids)
    ]
    for copy in tag_copies + copies:
        copy.start()
    for copy in tag_copies:
        copy.wait()
    for k, out in enumerate(packed):
        tag = tags[k][...].reshape(1, rows)
        high = tag // TAG_BASE
        low = tag - high * TAG_BASE
        both = jnp.concatenate([high, low, jnp.zeros((TAG_ROWS - 2, rows), jnp.int32)], axis=0)
        out[rows:, :rows] = both.astype(F32).astype(BF16)
        out[rows:, rows:] = jnp.zeros((TAG_ROWS, width - rows), BF16)
    for copy in copies:
        copy.wait()


def pack(blocks, ids):
    rows, width = blocks[0].shape
    hbm, vmem = pl.BlockSpec(memory_space=pltpu.HBM), pl.BlockSpec(memory_space=pltpu.VMEM)
    return pl.pallas_call(
        pack_kernel,
        out_shape=[jax.ShapeDtypeStruct((rows + TAG_ROWS, width), BF16)] * 2,
        in_specs=[hbm] * 4,
        out_specs=[vmem] * 2,
        scratch_shapes=[
            *[pltpu.VMEM((rows,), jnp.int32)] * 2,
            pltpu.SemaphoreType.DMA((2,)),
            pltpu.SemaphoreType.DMA((2,)),
        ],
        compiler_params=pltpu.CompilerParams(vmem_limit_bytes=60 * 2**20),
    )(*blocks, *ids)


def tags_of(block):
    if isinstance(block, tuple):
        tags = block[1][...]
        return tags.reshape(1, tags.shape[0]).astype(F32)
    rows = block.shape[0] - TAG_ROWS
    tags = block[rows:, :rows].astype(F32)
    return tags[0:1] * TAG_BASE + tags[1:2]


def rows_of(block):
    return block[0] if isinstance(block, tuple) else block


def meet(video, partner, scalars, products, weights):
    rows = weights.shape[0]
    log_scale, offset = scalars[0][0], scalars[1][0]
    scale = jnp.exp(jnp.full((1, rows), log_scale, F32))
    products[...] = lax.dot_general(
        rows_of(partner)[:rows, :], video[:rows, :], (((1,), (1,)), ((), ())), preferred_element_type=F32
    )
    video_tags = tags_of(video)
    partner_tags = jnp.transpose(jnp.broadcast_to(tags_of(partner), (8, rows)))[:, :1]
    total = jnp.zeros((8, rows), F32)
    for start in range(0, rows, SLAB):
        part = slice(start, start + SLAB)
        logits = scale * products[part, :] + offset
        same = partner_tags[part, :] == video_tags
        flipped = -logits
        z = jnp.where(same, flipped, logits)
        e = jnp.exp(jnp.minimum(logits, flipped))
        inverse = 1.0 / (1.0 + e)
        sigmoid = jnp.where(z >= 0.0, inverse, e * inverse)
        weights[part, :] = (jnp.where(same, -scale, scale) * sigmoid).astype(BF16)
        log1p = jnp.where(e < 0.005, e * (1.0 - 0.5 * e), jnp.log(1.0 + e))
        losses = jnp.maximum(z, 0.0) + log1p
        total = total + jnp.sum(losses.reshape(SLAB // 8, 8, rows), axis=0)
    return jnp.sum(total, axis=0, keepdims=True)


def column_parts(ref):
    return [slice(c, c + COLUMNS) for c in range(0, ref.shape[1], COLUMNS)]


def to_video(weights, partner, part):
    rows = weights.shape[0]
    return lax.dot_general(
        weights[...], rows_of(partner)[:rows, part], (((0,), (0,)), ((), ())), preferred_element_type=F32
    )


def to_partner(weights, video, part):
    return jnp.dot(weights[...], video[: weights.shape[0], part], preferred_element_type=F32)


def own_kernel(
    imu_log_scale, imu_bias, audio_log_scale, audio_bias, video, imu, audio, audio_ids,
    loss, video_grad, imu_grad, audio_grad, products, weights,
):
    audio = (audio, audio_ids)
    loss[...] = meet(video, audio, (audio_log_scale, audio_bias), products, weights)
    for part in column_parts(video):
        video_grad[:, part] = to_video(weights, audio, part)
        audio_grad[:, part] = to_partner(weights, video, part)
    loss[...] += meet(video, imu, (imu_log_scale, imu_bias), products, weights)
    for part in column_parts(video):
        video_grad[:, part] += to_video(weights, imu, part)
        imu_grad[:, part] = to_partner(weights, video, part)


def put_losses(losses, packed):
    rows = losses.shape[1]
    terms = []
    for _ in range(3):
        terms.append(losses.astype(BF16).astype(F32))
        losses = losses - terms[-1]
    terms.append(jnp.zeros((TAG_ROWS - 3, rows), F32))
    packed[rows:, :rows] = jnp.concatenate(terms, axis=0).astype(BF16)
    packed[rows:, rows:] = jnp.zeros((TAG_ROWS, packed.shape[1] - rows), BF16)


def row_near_kernel(
    log_scale, bias, other_video, imu, grad_in, other_loss, other_grad, grad, products, weights
):
    other_loss[...] = meet(other_video, imu, (log_scale, bias), products, weights)
    for part in column_parts(imu):
        other_grad[:, part] = to_video(weights, imu, part)
        grad[:, part] = grad_in[:, part] + to_partner(weights, other_video, part)


def row_far_kernel(
    log_scale, bias, video, other_video, imu, loss_in, video_in, other_loss_in, other_in,
    loss, video_grad, other_grad, sums, products, weights, other_weights,
):
    scalars = (log_scale, bias)
    rows = sums.shape[0]
    of_other = meet(other_video, imu, scalars, products, other_weights)
    put_losses(other_loss_in[...] + of_other, other_grad)
    loss[...] = loss_in[...] + meet(video, imu, scalars, products, weights)
    for part in column_parts(video):
        both = to_partner(weights, video, part) + to_partner(other_weights, other_video, part)
        sums[:, part] = both.astype(BF16)
        other_sum = other_in[:, part] + to_video(other_weights, imu, part)
        other_grad[:rows, part] = other_sum.astype(BF16)
        video_grad[:, part] = video_in[:, part] + to_video(weights, imu, part)


def col_own_kernel(
    log_scale, bias, video, audio, audio_ids, loss_in, video_in,
    loss, video_grad, sums, products, weights,
):
    audio = (audio, audio_ids)
    loss[...] = loss_in[...] + meet(video, audio, (log_scale, bias), products, weights)
    for part in column_parts(video):
        video_grad[:, part] = video_in[:, part] + to_video(weights, audio, part)
        sums[:, part] = to_partner(weights, video, part)


def col_far_kernel(
    log_scale, bias, other_video, audio, audio_ids, sums_in,
    other_loss, other_grad, sums, products, weights,
):
    audio = (audio, audio_ids)
    other_loss[...] = meet(other_video, audio, (log_scale, bias), products, weights)
    for part in column_parts(other_video):
        sums[:, part] = (sums_in[:, part] + to_partner(weights, other_video, part)).astype(BF16)
        other_grad[:, part] = to_video(weights, audio, part)


def col_near_kernel(
    log_scale, bias, other_video, audio, audio_ids, other_loss_in, other_in, grad_in,
    other_grad, grad, products, weights,
):
    audio = (audio, audio_ids)
    rows = grad.shape[0]
    losses = meet(other_video, audio, (log_scale, bias), products, weights)
    put_losses(other_loss_in[...] + losses, other_grad)
    for part in column_parts(other_video):
        other_sum = other_in[:, part] + to_video(weights, audio, part)
        other_grad[:rows, part] = other_sum.astype(BF16)
        grad[:, part] = grad_in[:, part] + to_partner(weights, other_video, part)


def sum_kernel(got_video, got_losses, got_partner, video_in, partner_in, loss_in, *outs):
    video_grad, grad, loss = outs
    grad[...] = partner_in[...] + got_partner[...].astype(F32)
    video_grad[...] = video_in[...] + got_video[...].astype(F32)

    @pl.when(pl.program_id(0) == 0)
    def _():
        rows = loss_in.shape[1]
        came = got_losses[:, :rows].astype(F32)
        total = loss_in[...] + jnp.sum(came, axis=0, keepdims=True)
        if len(loss.shape) == 1:
            loss[...] = (total / (2.0 * STEPS * rows)).reshape(rows)
        else:
            loss[...] = total


def summed(got_video, got_partner, video_grad, grad, loss, last, cost):
    rows, width = grad.shape
    block = pl.BlockSpec((rows // SUM_BLOCKS, width), lambda i: (i, 0))
    below = pl.BlockSpec((TAG_ROWS, width), lambda i: (rows // TAG_ROWS, 0))
    line = pl.BlockSpec((1, rows), lambda i: (0, 0))
    square = jax.ShapeDtypeStruct((rows, width), F32)
    losses = jax.ShapeDtypeStruct((rows,) if last else (1, rows), F32)
    return pl.pallas_call(
        sum_kernel,
        grid=(SUM_BLOCKS,),
        out_shape=[square, square, losses],
        in_specs=[block, below, block, block, block, line],
        out_specs=[block, block, pl.BlockSpec((rows,), lambda i: (0,)) if last else line],
        compiler_params=pltpu.CompilerParams(vmem_limit_bytes=20 * 2**20),
        cost_estimate=pl.CostEstimate(flops=cost, bytes_accessed=0, transcendentals=0),
    )(got_video, got_video, got_partner, video_grad, grad, loss)


def call(kernel, outs, scalars, args, rows, weights=1, cost=OWN_COST):
    smem, vmem = pl.BlockSpec(memory_space=pltpu.SMEM), pl.BlockSpec(memory_space=pltpu.VMEM)
    scratch = [pltpu.VMEM((rows, rows), F32)] + [pltpu.VMEM((rows, rows), BF16)] * weights
    return pl.pallas_call(
        kernel,
        out_shape=[jax.ShapeDtypeStruct(*out) for out in outs],
        in_specs=[smem] * len(scalars) + [vmem] * len(args),
        out_specs=[vmem] * len(outs),
        scratch_shapes=scratch,
        compiler_params=pltpu.CompilerParams(vmem_limit_bytes=20 * 2**20),
        cost_estimate=pl.CostEstimate(
            flops=cost,
            bytes_accessed=2 * sum(a.size * a.dtype.itemsize for a in args),
            transcendentals=0,
        ),
    )(*scalars, *args)


class Tile:
    def __init__(self, axis):
        self.axis = axis
        devices = lax.axis_size(axis)
        if devices == STEPS:
            self.video = [(p ^ 1, p) for p in range(devices)]
            self.partner = [(p ^ 2, p) for p in range(devices)]
        else:
            self.video = [((p + 1) % devices, p) for p in range(devices)]
            self.partner = [((p - 2) % devices, p) for p in range(devices)]

    def bring_video(self, block):
        return lax.ppermute(block, self.axis, self.video)

    def bring_partner(self, block):
        return lax.ppermute(block, self.axis, self.partner)

    def return_video(self, block):
        return lax.ppermute(block, self.axis, [(b, a) for a, b in self.video])

    def return_partner(self, block):
        return lax.ppermute(block, self.axis, [(b, a) for a, b in self.partner])


def per_device(
    video, video_ids, imu, imu_ids, audio, audio_ids,
    imu_log_scale, imu_bias, audio_log_scale, audio_bias,
):
    rows, width = video.shape
    line, square, narrow = ((1, rows), F32), ((rows, width), F32), ((rows, width), BF16)
    packed = ((rows + TAG_ROWS, width), BF16)
    of_imu, of_audio = (imu_log_scale, imu_bias), (audio_log_scale, audio_bias)
    along_row, along_col = Tile("row"), Tile("col")

    col_audio = along_col.bring_partner(audio), along_col.bring_partner(audio_ids)
    audio = (audio, audio_ids)
    video, imu = pack((video, imu), (video_ids, imu_ids))
    col_video = along_col.bring_video(video)
    row_video = along_row.bring_video(video)
    row_imu = along_row.bring_partner(imu)

    loss, video_grad, imu_grad, audio_grad = call(
        own_kernel,
        [line, square, square, square],
        of_imu + of_audio,
        (video, imu, *audio),
        rows, 1, OWN_COST,
    )
    loss, video_grad, sums = call(
        col_own_kernel,
        [line, square, square],
        of_audio,
        (video, *col_audio, loss, video_grad),
        rows, 1, COL_COST,
    )
    row_loss, row_grad, imu_grad = call(
        row_near_kernel,
        [line, square, square],
        of_imu,
        (row_video, imu, imu_grad),
        rows, 1, ROW_COST,
    )
    col_loss, col_grad, sums = call(
        col_far_kernel,
        [line, square, narrow],
        of_audio,
        (col_video, *col_audio, sums),
        rows, 1, COL_COST,
    )
    got_audio = along_col.return_partner(sums)
    col_grad, audio_grad = call(
        col_near_kernel,
        [packed, square],
        of_audio,
        (col_video, *audio, col_loss, col_grad, audio_grad),
        rows, 1, COL_COST,
    )
    got_col = along_col.return_video(col_grad)
    loss, video_grad, row_grad, sums = call(
        row_far_kernel,
        [line, square, packed, narrow],
        of_imu,
        (video, row_video, row_imu, loss, video_grad, row_loss, row_grad),
        rows, 2, ROW_COST,
    )
    got_imu = along_row.return_partner(sums)
    got_row = along_row.return_video(row_grad)

    video_grad, audio_grad, loss = summed(
        got_col, got_audio, video_grad, audio_grad, loss, False, SUM_COST
    )
    video_grad, imu_grad, loss = summed(
        got_row, got_imu, video_grad, imu_grad, loss, True, ROW_COST
    )
    return (video_grad, imu_grad, audio_grad, loss)


def solution(mesh):
    rows, vector = P(("row", "col"), None), P(("row", "col"))
    return jax.shard_map(
        per_device,
        mesh=mesh,
        in_specs=(rows, vector, rows, vector, rows, vector, P(), P(), P(), P()),
        out_specs=(rows, rows, rows, vector),
        check_vma=False,
    )
```

```python
import jax
import jax.numpy as jnp
from jax import lax
from jax.experimental import pallas as pl
from jax.experimental.pallas import tpu as pltpu
from jax.sharding import PartitionSpec as P

STEPS = 4
SLAB = 16
COLUMNS = 512
SUM_BLOCKS = 4
TAG_ROWS = 16
TAG_BASE = 256
COSTS = {
    "own": 0.5e9, "row_near": 0.5e9, "col_own": 0.5e9, "row_far": 0.5e9, "col_far": 0.5e9,
    "col_near": 0.5e9, "row_sum": 0.5e9, "audio_sum": 20e9, "video_sum": 20e9,
}

F32 = jnp.float32
BF16 = jnp.bfloat16


def pack_kernel(*refs):
    blocks, ids, packed = refs[:2], refs[2:4], refs[4:6]
    tags, (block_done, tags_done) = refs[6:8], refs[8:]
    rows, width = blocks[0].shape
    copies = [
        pltpu.make_async_copy(block, out.at[:rows, :], block_done.at[k])
        for k, (block, out) in enumerate(zip(blocks, packed))
    ]
    tag_copies = [
        pltpu.make_async_copy(source, tags[k], tags_done.at[k]) for k, source in enumerate(ids)
    ]
    for copy in tag_copies + copies:
        copy.start()
    for copy in tag_copies:
        copy.wait()
    for k, out in enumerate(packed):
        tag = tags[k][...].reshape(1, rows)
        high = tag // TAG_BASE
        low = tag - high * TAG_BASE
        both = jnp.concatenate([high, low, jnp.zeros((TAG_ROWS - 2, rows), jnp.int32)], axis=0)
        out[rows:, :rows] = both.astype(F32).astype(BF16)
        out[rows:, rows:] = jnp.zeros((TAG_ROWS, width - rows), BF16)
    for copy in copies:
        copy.wait()


def pack(blocks, ids):
    rows, width = blocks[0].shape
    hbm, vmem = pl.BlockSpec(memory_space=pltpu.HBM), pl.BlockSpec(memory_space=pltpu.VMEM)
    return pl.pallas_call(
        pack_kernel,
        out_shape=[jax.ShapeDtypeStruct((rows + TAG_ROWS, width), BF16)] * 2,
        in_specs=[hbm] * 4,
        out_specs=[vmem] * 2,
        scratch_shapes=[
            *[pltpu.VMEM((rows,), jnp.int32)] * 2,
            pltpu.SemaphoreType.DMA((2,)),
            pltpu.SemaphoreType.DMA((2,)),
        ],
        compiler_params=pltpu.CompilerParams(vmem_limit_bytes=60 * 2**20),
    )(*blocks, *ids)


def tags_of(block):
    if isinstance(block, tuple):
        tags = block[1][...]
        return tags.reshape(1, tags.shape[0]).astype(F32)
    rows = block.shape[0] - TAG_ROWS
    tags = block[rows:, :rows].astype(F32)
    return tags[0:1] * TAG_BASE + tags[1:2]


def rows_of(block):
    return block[0] if isinstance(block, tuple) else block


def meet(video, partner, scalars, products, weights):
    rows = weights.shape[0]
    log_scale, offset = scalars[0][0], scalars[1][0]
    scale = jnp.exp(jnp.full((1, rows), log_scale, F32))
    products[...] = lax.dot_general(
        rows_of(partner)[:rows, :], video[:rows, :], (((1,), (1,)), ((), ())), preferred_element_type=F32
    )
    video_tags = tags_of(video)
    partner_tags = jnp.transpose(jnp.broadcast_to(tags_of(partner), (8, rows)))[:, :1]
    total = jnp.zeros((8, rows), F32)
    for start in range(0, rows, SLAB):
        part = slice(start, start + SLAB)
        logits = scale * products[part, :] + offset
        same = partner_tags[part, :] == video_tags
        flipped = -logits
        z = jnp.where(same, flipped, logits)
        e = jnp.exp(jnp.minimum(logits, flipped))
        inverse = 1.0 / (1.0 + e)
        sigmoid = jnp.where(z >= 0.0, inverse, e * inverse)
        weights[part, :] = (jnp.where(same, -scale, scale) * sigmoid).astype(BF16)
        log1p = jnp.where(e < 0.005, e * (1.0 - 0.5 * e), jnp.log(1.0 + e))
        losses = jnp.maximum(z, 0.0) + log1p
        total = total + jnp.sum(losses.reshape(SLAB // 8, 8, rows), axis=0)
    return jnp.sum(total, axis=0, keepdims=True)


def column_parts(ref):
    return [slice(c, c + COLUMNS) for c in range(0, ref.shape[1], COLUMNS)]


def to_video(weights, partner, part):
    rows = weights.shape[0]
    return lax.dot_general(
        weights[...], rows_of(partner)[:rows, part], (((0,), (0,)), ((), ())), preferred_element_type=F32
    )


def to_partner(weights, video, part):
    return jnp.dot(weights[...], video[: weights.shape[0], part], preferred_element_type=F32)


def own_kernel(
    imu_log_scale, imu_bias, audio_log_scale, audio_bias, video, imu, audio, audio_ids,
    loss, video_grad, imu_grad, audio_grad, products, weights,
):
    audio = (audio, audio_ids)
    loss[...] = meet(video, audio, (audio_log_scale, audio_bias), products, weights)
    for part in column_parts(video):
        video_grad[:, part] = to_video(weights, audio, part)
        audio_grad[:, part] = to_partner(weights, video, part)
    loss[...] += meet(video, imu, (imu_log_scale, imu_bias), products, weights)
    for part in column_parts(video):
        video_grad[:, part] += to_video(weights, imu, part)
        imu_grad[:, part] = to_partner(weights, video, part)


def put_losses(losses, packed):
    rows = losses.shape[1]
    terms = []
    for _ in range(3):
        terms.append(losses.astype(BF16).astype(F32))
        losses = losses - terms[-1]
    terms.append(jnp.zeros((TAG_ROWS - 3, rows), F32))
    packed[rows:, :rows] = jnp.concatenate(terms, axis=0).astype(BF16)
    packed[rows:, rows:] = jnp.zeros((TAG_ROWS, packed.shape[1] - rows), BF16)


def row_near_kernel(
    log_scale, bias, other_video, imu, grad_in, loss_in,
    other_loss, other_grad, grad, loss, products, weights,
):
    loss[...] = loss_in[...]
    other_loss[...] = meet(other_video, imu, (log_scale, bias), products, weights)
    for part in column_parts(imu):
        other_grad[:, part] = to_video(weights, imu, part)
        grad[:, part] = grad_in[:, part] + to_partner(weights, other_video, part)


def row_far_kernel(
    log_scale, bias, video, other_video, imu, loss_in, video_in, other_loss_in, other_in,
    loss, video_grad, other_grad, sums, products, weights, other_weights,
):
    scalars = (log_scale, bias)
    rows = sums.shape[0]
    of_other = meet(other_video, imu, scalars, products, other_weights)
    put_losses(other_loss_in[...] + of_other, other_grad)
    loss[...] = loss_in[...] + meet(video, imu, scalars, products, weights)
    for part in column_parts(video):
        both = to_partner(weights, video, part) + to_partner(other_weights, other_video, part)
        sums[:, part] = both.astype(BF16)
        other_sum = other_in[:, part] + to_video(other_weights, imu, part)
        other_grad[:rows, part] = other_sum.astype(BF16)
        video_grad[:, part] = video_in[:, part] + to_video(weights, imu, part)


def col_own_kernel(
    log_scale, bias, video, audio, audio_ids, loss_in, video_in,
    loss, video_grad, sums, products, weights,
):
    audio = (audio, audio_ids)
    loss[...] = loss_in[...] + meet(video, audio, (log_scale, bias), products, weights)
    for part in column_parts(video):
        video_grad[:, part] = video_in[:, part] + to_video(weights, audio, part)
        sums[:, part] = to_partner(weights, video, part)


def col_far_kernel(
    log_scale, bias, other_video, audio, audio_ids, sums_in, loss_in,
    other_loss, other_grad, sums, loss, products, weights,
):
    loss[...] = loss_in[...]
    audio = (audio, audio_ids)
    other_loss[...] = meet(other_video, audio, (log_scale, bias), products, weights)
    for part in column_parts(other_video):
        sums[:, part] = (sums_in[:, part] + to_partner(weights, other_video, part)).astype(BF16)
        other_grad[:, part] = to_video(weights, audio, part)


def col_near_kernel(
    log_scale, bias, other_video, audio, audio_ids, other_loss_in, other_in, grad_in, loss_in,
    other_grad, grad, loss, products, weights,
):
    loss[...] = loss_in[...]
    audio = (audio, audio_ids)
    rows = grad.shape[0]
    losses = meet(other_video, audio, (log_scale, bias), products, weights)
    put_losses(other_loss_in[...] + losses, other_grad)
    for part in column_parts(other_video):
        other_sum = other_in[:, part] + to_video(weights, audio, part)
        other_grad[:rows, part] = other_sum.astype(BF16)
        grad[:, part] = grad_in[:, part] + to_partner(weights, other_video, part)


def added(parts, out, buffer, done):
    rows = out.shape[0] // SUM_BLOCKS
    copies = []
    for k in range(SUM_BLOCKS):
        block = slice(k * rows, (k + 1) * rows)
        total = parts[0][block, :]
        for part in parts[1:]:
            total = total + part[block, :].astype(F32)
        buffer[block, :] = total
        copy = pltpu.make_async_copy(buffer.at[block, :], out.at[block, :], done.at[k])
        copy.start()
        copies.append(copy)
    return copies


def losses_in(packed):
    rows = packed.shape[0] - TAG_ROWS
    return jnp.sum(packed[rows:, :rows].astype(F32), axis=0, keepdims=True)


def audio_sum_kernel(got_audio, audio_in, loss_in, audio_grad, loss, buffer, done):
    copies = added((audio_in, got_audio), audio_grad, buffer, done)
    loss[...] = loss_in[...]
    for copy in copies:
        copy.wait()


def video_sum_kernel(got_video, video_in, loss_in, video_grad, loss):
    rows = video_grad.shape[0]
    video_grad[...] = video_in[...] + got_video[:rows, :].astype(F32)
    loss[...] = loss_in[...] + losses_in(got_video)


def row_sum_kernel(
    got_video, got_imu, video_in, imu_in, loss_in, video_grad, imu_grad, loss,
    video_buffer, video_done, imu_buffer, imu_done,
):
    copies = added((video_in, got_video), video_grad, video_buffer, video_done)
    copies += added((imu_in, got_imu), imu_grad, imu_buffer, imu_done)
    rows = video_in.shape[0]
    total = loss_in[...] + losses_in(got_video)
    loss[...] = (total / (2.0 * STEPS * rows)).reshape(rows)
    for copy in copies:
        copy.wait()


def summed(kernel, outs, spaces, args, cost):
    vmem = pl.BlockSpec(memory_space=pltpu.VMEM)
    return pl.pallas_call(
        kernel,
        out_shape=[jax.ShapeDtypeStruct(*out) for out in outs],
        in_specs=[vmem] * len(args),
        out_specs=[pl.BlockSpec(memory_space=space) for space in spaces],
        scratch_shapes=[pltpu.VMEM(outs[0][0], F32), pltpu.SemaphoreType.DMA((SUM_BLOCKS,))]
        * sum(space == pltpu.HBM for space in spaces),
        compiler_params=pltpu.CompilerParams(vmem_limit_bytes=20 * 2**20),
        cost_estimate=pl.CostEstimate(flops=int(cost), bytes_accessed=0, transcendentals=0),
    )(*args)


def call(kernel, outs, scalars, args, rows, weights=1, cost=0):
    smem, vmem = pl.BlockSpec(memory_space=pltpu.SMEM), pl.BlockSpec(memory_space=pltpu.VMEM)
    scratch = [pltpu.VMEM((rows, rows), F32)] + [pltpu.VMEM((rows, rows), BF16)] * weights
    return pl.pallas_call(
        kernel,
        out_shape=[jax.ShapeDtypeStruct(*out) for out in outs],
        in_specs=[smem] * len(scalars) + [vmem] * len(args),
        out_specs=[vmem] * len(outs),
        scratch_shapes=scratch,
        compiler_params=pltpu.CompilerParams(vmem_limit_bytes=20 * 2**20),
        cost_estimate=pl.CostEstimate(
            flops=int(cost),
            bytes_accessed=2 * sum(a.size * a.dtype.itemsize for a in args),
            transcendentals=0,
        ),
    )(*scalars, *args)


class Tile:
    def __init__(self, axis):
        self.axis = axis
        devices = lax.axis_size(axis)
        if devices == STEPS:
            self.video = [(p ^ 1, p) for p in range(devices)]
            self.partner = [(p ^ 2, p) for p in range(devices)]
        else:
            self.video = [((p + 1) % devices, p) for p in range(devices)]
            self.partner = [((p - 2) % devices, p) for p in range(devices)]

    def bring_video(self, block):
        return lax.ppermute(block, self.axis, self.video)

    def bring_partner(self, block):
        return lax.ppermute(block, self.axis, self.partner)

    def return_video(self, block):
        return lax.ppermute(block, self.axis, [(b, a) for a, b in self.video])

    def return_partner(self, block):
        return lax.ppermute(block, self.axis, [(b, a) for a, b in self.partner])


def per_device(
    video, video_ids, imu, imu_ids, audio, audio_ids,
    imu_log_scale, imu_bias, audio_log_scale, audio_bias,
):
    rows, width = video.shape
    line, square, narrow = ((1, rows), F32), ((rows, width), F32), ((rows, width), BF16)
    packed = ((rows + TAG_ROWS, width), BF16)
    of_imu, of_audio = (imu_log_scale, imu_bias), (audio_log_scale, audio_bias)
    along_row, along_col = Tile("row"), Tile("col")

    col_audio = along_col.bring_partner(audio), along_col.bring_partner(audio_ids)
    audio = (audio, audio_ids)
    video, imu = pack((video, imu), (video_ids, imu_ids))
    col_video = along_col.bring_video(video)
    row_video = along_row.bring_video(video)
    row_imu = along_row.bring_partner(imu)

    loss, video_grad, imu_grad, audio_grad = call(
        own_kernel,
        [line, square, square, square],
        of_imu + of_audio,
        (video, imu, *audio),
        rows, 1, COSTS["own"],
    )
    loss, video_grad, sums = call(
        col_own_kernel,
        [line, square, square],
        of_audio,
        (video, *col_audio, loss, video_grad),
        rows, 1, COSTS["col_own"],
    )
    row_loss, row_grad, imu_grad, loss = call(
        row_near_kernel,
        [line, square, square, line],
        of_imu,
        (row_video, imu, imu_grad, loss),
        rows, 1, COSTS["row_near"],
    )
    col_loss, col_grad, sums, loss = call(
        col_far_kernel,
        [line, square, narrow, line],
        of_audio,
        (col_video, *col_audio, sums, loss),
        rows, 1, COSTS["col_far"],
    )
    got_audio = along_col.return_partner(sums)
    col_grad, audio_grad, loss = call(
        col_near_kernel,
        [packed, square, line],
        of_audio,
        (col_video, *audio, col_loss, col_grad, audio_grad, loss),
        rows, 1, COSTS["col_near"],
    )
    got_col = along_col.return_video(col_grad)

    loss, video_grad, row_grad, row_sums = call(
        row_far_kernel,
        [line, square, packed, narrow],
        of_imu,
        (video, row_video, row_imu, loss, video_grad, row_loss, row_grad),
        rows, 2, COSTS["row_far"],
    )
    got_row = along_row.return_video(row_grad)
    got_imu = along_row.return_partner(row_sums)

    hbm, vmem = pltpu.HBM, pltpu.VMEM
    audio_grad, loss = summed(
        audio_sum_kernel,
        [square, line],
        [hbm, vmem],
        (got_audio, audio_grad, loss),
        COSTS["audio_sum"],
    )
    video_grad, loss = summed(
        video_sum_kernel,
        [square, line],
        [vmem, vmem],
        (got_col, video_grad, loss),
        COSTS["video_sum"],
    )
    video_grad, imu_grad, loss = summed(
        row_sum_kernel,
        [square, square, ((rows,), F32)],
        [hbm, hbm, vmem],
        (got_row, got_imu, video_grad, imu_grad, loss),
        COSTS["row_sum"],
    )
    return (video_grad, imu_grad, audio_grad, loss)


def solution(mesh):
    rows, vector = P(("row", "col"), None), P(("row", "col"))
    return jax.shard_map(
        per_device,
        mesh=mesh,
        in_specs=(rows, vector, rows, vector, rows, vector, P(), P(), P(), P()),
        out_specs=(rows, rows, rows, vector),
        check_vma=False,
    )
```

```python
import jax
import jax.numpy as jnp
from jax import lax
from jax.experimental import pallas as pl
from jax.experimental.pallas import tpu as pltpu
from jax.sharding import PartitionSpec as P

STEPS = 4
SLAB = 16
COLUMNS = 512
SUM_BLOCKS = 4
TAG_ROWS = 16
TAG_BASE = 256
COSTS = {
    "own": 0.5e9, "col_own": 0.5e9, "row": 0.5e9, "col_far": 0.5e9,
    "col_near": 0.5e9, "row_sum": 0.5e9, "audio_sum": 5e9, "video_sum": 20e9,
}

F32 = jnp.float32
BF16 = jnp.bfloat16


def pack_kernel(*refs):
    blocks, ids, packed = refs[:2], refs[2:4], refs[4:6]
    tags, (block_done, tags_done) = refs[6:8], refs[8:]
    rows, width = blocks[0].shape
    copies = [
        pltpu.make_async_copy(block, out.at[:rows, :], block_done.at[k])
        for k, (block, out) in enumerate(zip(blocks, packed))
    ]
    tag_copies = [
        pltpu.make_async_copy(source, tags[k], tags_done.at[k]) for k, source in enumerate(ids)
    ]
    for copy in tag_copies + copies:
        copy.start()
    for copy in tag_copies:
        copy.wait()
    for k, out in enumerate(packed):
        tag = tags[k][...].reshape(1, rows)
        high = tag // TAG_BASE
        low = tag - high * TAG_BASE
        both = jnp.concatenate([high, low, jnp.zeros((TAG_ROWS - 2, rows), jnp.int32)], axis=0)
        out[rows:, :rows] = both.astype(F32).astype(BF16)
        out[rows:, rows:] = jnp.zeros((TAG_ROWS, width - rows), BF16)
    for copy in copies:
        copy.wait()


def pack(blocks, ids):
    rows, width = blocks[0].shape
    hbm, vmem = pl.BlockSpec(memory_space=pltpu.HBM), pl.BlockSpec(memory_space=pltpu.VMEM)
    return pl.pallas_call(
        pack_kernel,
        out_shape=[pltpu.VMEM((rows + TAG_ROWS, width), BF16)] * 2,
        in_specs=[hbm] * 4,
        out_specs=[vmem] * 2,
        scratch_shapes=[
            *[pltpu.VMEM((rows,), jnp.int32)] * 2,
            pltpu.SemaphoreType.DMA((2,)),
            pltpu.SemaphoreType.DMA((2,)),
        ],
        compiler_params=pltpu.CompilerParams(vmem_limit_bytes=56 * 2**20),
    )(*blocks, *ids)


def tags_of(block):
    if isinstance(block, tuple):
        tags = block[1][...]
        return tags.reshape(1, tags.shape[0]).astype(F32)
    rows = block.shape[0] - TAG_ROWS
    tags = block[rows:, :rows].astype(F32)
    return tags[0:1] * TAG_BASE + tags[1:2]


def rows_of(block):
    return block[0] if isinstance(block, tuple) else block


def meet(video, partner, scalars, products, weights):
    rows = weights.shape[0]
    log_scale, offset = scalars[0][0], scalars[1][0]
    scale = jnp.exp(jnp.full((1, rows), log_scale, F32))
    products[...] = lax.dot_general(
        rows_of(partner)[:rows, :], video[:rows, :], (((1,), (1,)), ((), ())), preferred_element_type=F32
    )
    video_tags = tags_of(video)
    partner_tags = jnp.transpose(jnp.broadcast_to(tags_of(partner), (8, rows)))[:, :1]
    total = jnp.zeros((8, rows), F32)
    for start in range(0, rows, SLAB):
        part = slice(start, start + SLAB)
        logits = scale * products[part, :] + offset
        same = partner_tags[part, :] == video_tags
        flipped = -logits
        z = jnp.where(same, flipped, logits)
        e = jnp.exp(jnp.minimum(logits, flipped))
        inverse = 1.0 / (1.0 + e)
        sigmoid = jnp.where(z >= 0.0, inverse, e * inverse)
        weights[part, :] = (jnp.where(same, -scale, scale) * sigmoid).astype(BF16)
        log1p = jnp.where(e < 0.005, e * (1.0 - 0.5 * e), jnp.log(1.0 + e))
        losses = jnp.maximum(z, 0.0) + log1p
        total = total + jnp.sum(losses.reshape(SLAB // 8, 8, rows), axis=0)
    return jnp.sum(total, axis=0, keepdims=True)


def column_parts(ref):
    return [slice(c, c + COLUMNS) for c in range(0, ref.shape[1], COLUMNS)]


def to_video(weights, partner, part):
    rows = weights.shape[0]
    return lax.dot_general(
        weights[...], rows_of(partner)[:rows, part], (((0,), (0,)), ((), ())), preferred_element_type=F32
    )


def to_partner(weights, video, part):
    return jnp.dot(weights[...], video[: weights.shape[0], part], preferred_element_type=F32)


def own_kernel(
    imu_log_scale, imu_bias, audio_log_scale, audio_bias, video, imu, audio, audio_ids,
    loss, video_grad, imu_grad, audio_grad, video_on, imu_on, products, weights,
):
    video_on[...] = video[...]
    imu_on[...] = imu[...]
    audio = (audio, audio_ids)
    loss[...] = meet(video, audio, (audio_log_scale, audio_bias), products, weights)
    for part in column_parts(video):
        video_grad[:, part] = to_video(weights, audio, part)
        audio_grad[:, part] = to_partner(weights, video, part)
    loss[...] += meet(video, imu, (imu_log_scale, imu_bias), products, weights)
    for part in column_parts(video):
        video_grad[:, part] += to_video(weights, imu, part)
        imu_grad[:, part] = to_partner(weights, video, part)


def put_losses(losses, packed):
    rows = losses.shape[1]
    terms = []
    for _ in range(3):
        terms.append(losses.astype(BF16).astype(F32))
        losses = losses - terms[-1]
    terms.append(jnp.zeros((TAG_ROWS - 3, rows), F32))
    packed[rows:, :rows] = jnp.concatenate(terms, axis=0).astype(BF16)
    packed[rows:, rows:] = jnp.zeros((TAG_ROWS, packed.shape[1] - rows), BF16)


def row_kernel(
    log_scale, bias, video, other_video, imu, other_imu, loss_in, video_in, grad_in,
    loss, video_grad, grad, other_grad, sums, products, weights, other_weights, near_weights,
):
    scalars = (log_scale, bias)
    rows = sums.shape[0]
    losses = meet(other_video, imu, scalars, products, near_weights)
    losses = losses + meet(other_video, other_imu, scalars, products, other_weights)
    put_losses(losses, other_grad)
    loss[...] = loss_in[...] + meet(video, other_imu, scalars, products, weights)
    for part in column_parts(video):
        other_sum = to_video(near_weights, imu, part) + to_video(other_weights, other_imu, part)
        other_grad[:rows, part] = other_sum.astype(BF16)
        both = to_partner(weights, video, part) + to_partner(other_weights, other_video, part)
        sums[:, part] = both.astype(BF16)
        grad[:, part] = grad_in[:, part] + to_partner(near_weights, other_video, part)
        video_grad[:, part] = video_in[:, part] + to_video(weights, other_imu, part)


def col_own_kernel(
    log_scale, bias, video, audio, audio_ids, loss_in, video_in,
    loss, video_grad, sums, products, weights,
):
    audio = (audio, audio_ids)
    loss[...] = loss_in[...] + meet(video, audio, (log_scale, bias), products, weights)
    for part in column_parts(video):
        video_grad[:, part] = video_in[:, part] + to_video(weights, audio, part)
        sums[:, part] = to_partner(weights, video, part)


def col_far_kernel(
    log_scale, bias, other_video, audio, audio_ids, sums_in, loss_in,
    other_loss, other_grad, sums, loss, products, weights,
):
    loss[...] = loss_in[...]
    audio = (audio, audio_ids)
    other_loss[...] = meet(other_video, audio, (log_scale, bias), products, weights)
    for part in column_parts(other_video):
        sums[:, part] = (sums_in[:, part] + to_partner(weights, other_video, part)).astype(BF16)
        other_grad[:, part] = to_video(weights, audio, part)


def col_near_kernel(
    log_scale, bias, other_video, audio, audio_ids, other_loss_in, other_in, grad_in, loss_in,
    other_grad, grad, loss, products, weights,
):
    loss[...] = loss_in[...]
    audio = (audio, audio_ids)
    rows = grad.shape[0]
    losses = meet(other_video, audio, (log_scale, bias), products, weights)
    put_losses(other_loss_in[...] + losses, other_grad)
    for part in column_parts(other_video):
        other_sum = other_in[:, part] + to_video(weights, audio, part)
        other_grad[:rows, part] = other_sum.astype(BF16)
        grad[:, part] = grad_in[:, part] + to_partner(weights, other_video, part)


def added(parts, out, buffer, done):
    rows = out.shape[0] // SUM_BLOCKS
    copies = []
    for k in range(SUM_BLOCKS):
        block = slice(k * rows, (k + 1) * rows)
        total = parts[0][block, :]
        for part in parts[1:]:
            total = total + part[block, :].astype(F32)
        buffer[block, :] = total
        copy = pltpu.make_async_copy(buffer.at[block, :], out.at[block, :], done.at[k])
        copy.start()
        copies.append(copy)
    return copies


def losses_in(packed):
    rows = packed.shape[0] - TAG_ROWS
    return jnp.sum(packed[rows:, :rows].astype(F32), axis=0, keepdims=True)


def audio_sum_kernel(got_audio, audio_in, loss_in, audio_grad, loss, buffer, done):
    copies = added((audio_in, got_audio), audio_grad, buffer, done)
    loss[...] = loss_in[...]
    for copy in copies:
        copy.wait()


def video_sum_kernel(got_video, video_in, loss_in, video_grad, loss):
    rows = video_grad.shape[0]
    video_grad[...] = video_in[...] + got_video[:rows, :].astype(F32)
    loss[...] = loss_in[...] + losses_in(got_video)


def row_sum_kernel(
    got_video, got_imu, video_in, imu_in, loss_in, video_grad, imu_grad, loss,
    video_buffer, video_done, imu_buffer, imu_done,
):
    copies = added((video_in, got_video), video_grad, video_buffer, video_done)
    copies += added((imu_in, got_imu), imu_grad, imu_buffer, imu_done)
    rows = video_in.shape[0]
    total = loss_in[...] + losses_in(got_video)
    loss[...] = (total / (2.0 * STEPS * rows)).reshape(rows)
    for copy in copies:
        copy.wait()


def summed(kernel, outs, spaces, args, cost):
    vmem = pl.BlockSpec(memory_space=pltpu.VMEM)
    return pl.pallas_call(
        kernel,
        out_shape=[jax.ShapeDtypeStruct(*out) for out in outs],
        in_specs=[vmem] * len(args),
        out_specs=[pl.BlockSpec(memory_space=space) for space in spaces],
        scratch_shapes=[pltpu.VMEM(outs[0][0], F32), pltpu.SemaphoreType.DMA((SUM_BLOCKS,))]
        * sum(space == pltpu.HBM for space in spaces),
        compiler_params=pltpu.CompilerParams(vmem_limit_bytes=20 * 2**20),
        cost_estimate=pl.CostEstimate(flops=int(cost), bytes_accessed=0, transcendentals=0),
    )(*args)


def call(kernel, outs, scalars, args, rows, weights=1, cost=0):
    smem, vmem = pl.BlockSpec(memory_space=pltpu.SMEM), pl.BlockSpec(memory_space=pltpu.VMEM)
    scratch = [pltpu.VMEM((rows, rows), F32)] + [pltpu.VMEM((rows, rows), BF16)] * weights
    return pl.pallas_call(
        kernel,
        out_shape=[jax.ShapeDtypeStruct(*out) for out in outs],
        in_specs=[smem] * len(scalars) + [vmem] * len(args),
        out_specs=[vmem] * len(outs),
        scratch_shapes=scratch,
        compiler_params=pltpu.CompilerParams(vmem_limit_bytes=20 * 2**20),
        cost_estimate=pl.CostEstimate(
            flops=int(cost),
            bytes_accessed=2 * sum(a.size * a.dtype.itemsize for a in args),
            transcendentals=0,
        ),
    )(*scalars, *args)


class Tile:
    def __init__(self, axis):
        self.axis = axis
        devices = lax.axis_size(axis)
        if devices == STEPS:
            self.video = [(p ^ 1, p) for p in range(devices)]
            self.partner = [(p ^ 2, p) for p in range(devices)]
        else:
            self.video = [((p + 1) % devices, p) for p in range(devices)]
            self.partner = [((p - 2) % devices, p) for p in range(devices)]

    def bring_video(self, block):
        return lax.ppermute(block, self.axis, self.video)

    def bring_partner(self, block):
        return lax.ppermute(block, self.axis, self.partner)

    def return_video(self, block):
        return lax.ppermute(block, self.axis, [(b, a) for a, b in self.video])

    def return_partner(self, block):
        return lax.ppermute(block, self.axis, [(b, a) for a, b in self.partner])


def per_device(
    video, video_ids, imu, imu_ids, audio, audio_ids,
    imu_log_scale, imu_bias, audio_log_scale, audio_bias,
):
    rows, width = video.shape
    line, square, narrow = ((1, rows), F32), ((rows, width), F32), ((rows, width), BF16)
    packed = ((rows + TAG_ROWS, width), BF16)
    of_imu, of_audio = (imu_log_scale, imu_bias), (audio_log_scale, audio_bias)
    along_row, along_col = Tile("row"), Tile("col")

    col_audio = along_col.bring_partner(audio), along_col.bring_partner(audio_ids)
    audio = (audio, audio_ids)
    video, imu = pack((video, imu), (video_ids, imu_ids))
    col_video = along_col.bring_video(video)

    loss, video_grad, imu_grad, audio_grad, video_on, imu_on = call(
        own_kernel,
        [line, square, square, square, packed, packed],
        of_imu + of_audio,
        (video, imu, *audio),
        rows, 1, COSTS["own"],
    )
    row_video = along_row.bring_video(video_on)
    row_imu = along_row.bring_partner(imu_on)
    loss, video_grad, sums = call(
        col_own_kernel,
        [line, square, square],
        of_audio,
        (video, *col_audio, loss, video_grad),
        rows, 1, COSTS["col_own"],
    )
    col_loss, col_grad, sums, loss = call(
        col_far_kernel,
        [line, square, narrow, line],
        of_audio,
        (col_video, *col_audio, sums, loss),
        rows, 1, COSTS["col_far"],
    )
    got_audio = along_col.return_partner(sums)
    col_grad, audio_grad, loss = call(
        col_near_kernel,
        [packed, square, line],
        of_audio,
        (col_video, *audio, col_loss, col_grad, audio_grad, loss),
        rows, 1, COSTS["col_near"],
    )
    got_col = along_col.return_video(col_grad)

    loss, video_grad, imu_grad, row_grad, row_sums = call(
        row_kernel,
        [line, square, square, packed, narrow],
        of_imu,
        (video, row_video, imu, row_imu, loss, video_grad, imu_grad),
        rows, 3, COSTS["row"],
    )
    got_row = along_row.return_video(row_grad)
    got_imu = along_row.return_partner(row_sums)

    hbm, vmem = pltpu.HBM, pltpu.VMEM
    audio_grad, loss = summed(
        audio_sum_kernel,
        [square, line],
        [hbm, vmem],
        (got_audio, audio_grad, loss),
        COSTS["audio_sum"],
    )
    video_grad, loss = summed(
        video_sum_kernel,
        [square, line],
        [vmem, vmem],
        (got_col, video_grad, loss),
        COSTS["video_sum"],
    )
    video_grad, imu_grad, loss = summed(
        row_sum_kernel,
        [square, square, ((rows,), F32)],
        [hbm, hbm, vmem],
        (got_row, got_imu, video_grad, imu_grad, loss),
        COSTS["row_sum"],
    )
    return (video_grad, imu_grad, audio_grad, loss)


def solution(mesh):
    rows, vector = P(("row", "col"), None), P(("row", "col"))
    return jax.shard_map(
        per_device,
        mesh=mesh,
        in_specs=(rows, vector, rows, vector, rows, vector, P(), P(), P(), P()),
        out_specs=(rows, rows, rows, vector),
        check_vma=False,
    )
```

```python
import jax
import jax.numpy as jnp
from jax import lax
from jax.experimental import pallas as pl
from jax.experimental.pallas import tpu as pltpu
from jax.sharding import PartitionSpec as P

STEPS = 4
SLAB = 16
COLUMNS = 512
SUM_BLOCKS = 4
TAG_ROWS = 16
TAG_BASE = 256
COSTS = {
    "own": 0.5e9, "own_far": 0.5e9, "far": 0.5e9, "near": 0.5e9, "row": 0.5e9, "late": 0.01e9,
    "audio_sum": 5e9, "video_sum": 20e9, "row_sum": 0.5e9,
}

F32 = jnp.float32
BF16 = jnp.bfloat16


def pack_kernel(*refs):
    blocks, ids, packed = refs[:2], refs[2:4], refs[4:6]
    tags, (block_done, tags_done) = refs[6:8], refs[8:]
    rows, width = blocks[0].shape
    copies = [
        pltpu.make_async_copy(block, out.at[:rows, :], block_done.at[k])
        for k, (block, out) in enumerate(zip(blocks, packed))
    ]
    tag_copies = [
        pltpu.make_async_copy(source, tags[k], tags_done.at[k]) for k, source in enumerate(ids)
    ]
    for copy in tag_copies + copies:
        copy.start()
    for copy in tag_copies:
        copy.wait()
    for k, out in enumerate(packed):
        tag = tags[k][...].reshape(1, rows)
        high = tag // TAG_BASE
        low = tag - high * TAG_BASE
        both = jnp.concatenate([high, low, jnp.zeros((TAG_ROWS - 2, rows), jnp.int32)], axis=0)
        out[rows:, :rows] = both.astype(F32).astype(BF16)
        out[rows:, rows:] = jnp.zeros((TAG_ROWS, width - rows), BF16)
    for copy in copies:
        copy.wait()


def pack(blocks, ids):
    rows, width = blocks[0].shape
    hbm, vmem = pl.BlockSpec(memory_space=pltpu.HBM), pl.BlockSpec(memory_space=pltpu.VMEM)
    return pl.pallas_call(
        pack_kernel,
        out_shape=[pltpu.VMEM((rows + TAG_ROWS, width), BF16)] * 2,
        in_specs=[hbm] * 4,
        out_specs=[vmem] * 2,
        scratch_shapes=[
            *[pltpu.VMEM((rows,), jnp.int32)] * 2,
            pltpu.SemaphoreType.DMA((2,)),
            pltpu.SemaphoreType.DMA((2,)),
        ],
        compiler_params=pltpu.CompilerParams(vmem_limit_bytes=56 * 2**20),
    )(*blocks, *ids)


def tags_of(block):
    if isinstance(block, tuple):
        tags = block[1][...]
        return tags.reshape(1, tags.shape[0]).astype(F32)
    rows = block.shape[0] - TAG_ROWS
    tags = block[rows:, :rows].astype(F32)
    return tags[0:1] * TAG_BASE + tags[1:2]


def rows_of(block):
    return block[0] if isinstance(block, tuple) else block


def meet(video, partner, scalars, products, weights):
    rows = weights.shape[0]
    log_scale, offset = scalars[0][0], scalars[1][0]
    scale = jnp.exp(jnp.full((1, rows), log_scale, F32))
    products[...] = lax.dot_general(
        rows_of(partner)[:rows, :], video[:rows, :], (((1,), (1,)), ((), ())), preferred_element_type=F32
    )
    video_tags = tags_of(video)
    partner_tags = jnp.transpose(jnp.broadcast_to(tags_of(partner), (8, rows)))[:, :1]
    total = jnp.zeros((8, rows), F32)
    for start in range(0, rows, SLAB):
        part = slice(start, start + SLAB)
        logits = scale * products[part, :] + offset
        same = partner_tags[part, :] == video_tags
        flipped = -logits
        z = jnp.where(same, flipped, logits)
        e = jnp.exp(jnp.minimum(logits, flipped))
        inverse = 1.0 / (1.0 + e)
        sigmoid = jnp.where(z >= 0.0, inverse, e * inverse)
        weights[part, :] = (jnp.where(same, -scale, scale) * sigmoid).astype(BF16)
        log1p = jnp.where(e < 0.005, e * (1.0 - 0.5 * e), jnp.log(1.0 + e))
        losses = jnp.maximum(z, 0.0) + log1p
        total = total + jnp.sum(losses.reshape(SLAB // 8, 8, rows), axis=0)
    return jnp.sum(total, axis=0, keepdims=True)


def column_parts(ref):
    return [slice(c, c + COLUMNS) for c in range(0, ref.shape[1], COLUMNS)]


def to_video(weights, partner, part):
    rows = weights.shape[0]
    return lax.dot_general(
        weights[...], rows_of(partner)[:rows, part], (((0,), (0,)), ((), ())), preferred_element_type=F32
    )


def to_partner(weights, video, part):
    return jnp.dot(weights[...], video[: weights.shape[0], part], preferred_element_type=F32)


def own_kernel(
    imu_log_scale, imu_bias, audio_log_scale, audio_bias, video, imu, audio, audio_ids,
    loss, video_grad, imu_grad, audio_grad, video_on, imu_on, products, weights,
):
    video_on[...] = video[...]
    imu_on[...] = imu[...]
    audio = (audio, audio_ids)
    loss[...] = meet(video, audio, (audio_log_scale, audio_bias), products, weights)
    for part in column_parts(video):
        video_grad[:, part] = to_video(weights, audio, part)
        audio_grad[:, part] = to_partner(weights, video, part)
    loss[...] += meet(video, imu, (imu_log_scale, imu_bias), products, weights)
    for part in column_parts(video):
        video_grad[:, part] += to_video(weights, imu, part)
        imu_grad[:, part] = to_partner(weights, video, part)


def put_losses(losses, packed):
    rows = losses.shape[1]
    terms = []
    for _ in range(3):
        terms.append(losses.astype(BF16).astype(F32))
        losses = losses - terms[-1]
    terms.append(jnp.zeros((TAG_ROWS - 3, rows), F32))
    packed[rows:, :rows] = jnp.concatenate(terms, axis=0).astype(BF16)
    packed[rows:, rows:] = jnp.zeros((TAG_ROWS, packed.shape[1] - rows), BF16)


def own_far_kernel(
    log_scale, bias, video, audio, audio_ids, loss_in, loss, weights, products
):
    scalars = (log_scale, bias)
    loss[...] = loss_in[...] + meet(video, (audio, audio_ids), scalars, products, weights)


def far_kernel(
    log_scale, bias, video, other_video, audio, audio_ids, own_weights, loss_in,
    loss, other_loss, sums, weights, products,
):
    loss[...] = loss_in[...]
    other_loss[...] = meet(other_video, (audio, audio_ids), (log_scale, bias), products, weights)
    for part in column_parts(video):
        both = to_partner(own_weights, video, part) + to_partner(weights, other_video, part)
        sums[:, part] = both.astype(BF16)


def near_kernel(
    log_scale, bias, other_video, audio, audio_ids, far_audio, far_weights, other_loss_in, loss_in,
    other_grad, weights, loss, products,
):
    audio = (audio, audio_ids)
    rows = weights.shape[0]
    loss[...] = loss_in[...]
    losses = meet(other_video, audio, (log_scale, bias), products, weights)
    put_losses(other_loss_in[...] + losses, other_grad)
    for part in column_parts(other_video):
        both = to_video(weights, audio, part) + to_video(far_weights, far_audio, part)
        other_grad[:rows, part] = both.astype(BF16)


def row_kernel(
    log_scale, bias, video, other_video, imu, other_imu, loss_in,
    loss, other_grad, sums, weights, near_weights, products, other_weights,
):
    scalars = (log_scale, bias)
    rows = sums.shape[0]
    losses = meet(other_video, imu, scalars, products, near_weights)
    losses = losses + meet(other_video, other_imu, scalars, products, other_weights)
    put_losses(losses, other_grad)
    loss[...] = loss_in[...] + meet(video, other_imu, scalars, products, weights)
    for part in column_parts(video):
        other_sum = to_video(near_weights, imu, part) + to_video(other_weights, other_imu, part)
        other_grad[:rows, part] = other_sum.astype(BF16)
        both = to_partner(weights, video, part) + to_partner(other_weights, other_video, part)
        sums[:, part] = both.astype(BF16)


def late_kernel(
    far_audio, far_weights, col_video, near_weights, row_imu, row_weights, row_video,
    row_near_weights, video_in, audio_in, imu_in, loss_in,
    video_grad, audio_grad, imu_grad, loss,
):
    loss[...] = loss_in[...]
    for part in column_parts(video_grad):
        video_sum = to_video(far_weights, far_audio, part) + to_video(row_weights, row_imu, part)
        video_grad[:, part] = video_in[:, part] + video_sum
        audio_grad[:, part] = audio_in[:, part] + to_partner(near_weights, col_video, part)
        imu_grad[:, part] = imu_in[:, part] + to_partner(row_near_weights, row_video, part)


def added(parts, out, buffer, done):
    rows = out.shape[0] // SUM_BLOCKS
    copies = []
    for k in range(SUM_BLOCKS):
        block = slice(k * rows, (k + 1) * rows)
        total = parts[0][block, :]
        for part in parts[1:]:
            total = total + part[block, :].astype(F32)
        buffer[block, :] = total
        copy = pltpu.make_async_copy(buffer.at[block, :], out.at[block, :], done.at[k])
        copy.start()
        copies.append(copy)
    return copies


def losses_in(packed):
    rows = packed.shape[0] - TAG_ROWS
    return jnp.sum(packed[rows:, :rows].astype(F32), axis=0, keepdims=True)


def audio_sum_kernel(got_audio, audio_in, loss_in, audio_grad, loss, buffer, done):
    copies = added((audio_in, got_audio), audio_grad, buffer, done)
    loss[...] = loss_in[...]
    for copy in copies:
        copy.wait()


def video_sum_kernel(got_video, video_in, loss_in, video_grad, loss):
    rows = video_grad.shape[0]
    video_grad[...] = video_in[...] + got_video[:rows, :].astype(F32)
    loss[...] = loss_in[...] + losses_in(got_video)


def row_sum_kernel(
    got_video, got_imu, video_in, imu_in, loss_in, video_grad, imu_grad, loss,
    video_buffer, video_done, imu_buffer, imu_done,
):
    copies = added((video_in, got_video), video_grad, video_buffer, video_done)
    copies += added((imu_in, got_imu), imu_grad, imu_buffer, imu_done)
    rows = video_in.shape[0]
    total = loss_in[...] + losses_in(got_video)
    loss[...] = (total / (2.0 * STEPS * rows)).reshape(rows)
    for copy in copies:
        copy.wait()


def summed(kernel, outs, spaces, args, cost):
    vmem = pl.BlockSpec(memory_space=pltpu.VMEM)
    return pl.pallas_call(
        kernel,
        out_shape=[jax.ShapeDtypeStruct(*out) for out in outs],
        in_specs=[vmem] * len(args),
        out_specs=[pl.BlockSpec(memory_space=space) for space in spaces],
        scratch_shapes=[pltpu.VMEM(outs[0][0], F32), pltpu.SemaphoreType.DMA((SUM_BLOCKS,))]
        * sum(space == pltpu.HBM for space in spaces),
        compiler_params=pltpu.CompilerParams(vmem_limit_bytes=20 * 2**20),
        cost_estimate=pl.CostEstimate(flops=int(cost), bytes_accessed=0, transcendentals=0),
    )(*args)


def call(kernel, outs, scalars, args, rows, weights=1, cost=0, meets=True):
    smem, vmem = pl.BlockSpec(memory_space=pltpu.SMEM), pl.BlockSpec(memory_space=pltpu.VMEM)
    scratch = [pltpu.VMEM((rows, rows), F32)] + [pltpu.VMEM((rows, rows), BF16)] * weights
    scratch = scratch if meets else []
    return pl.pallas_call(
        kernel,
        out_shape=[jax.ShapeDtypeStruct(*out) for out in outs],
        in_specs=[smem] * len(scalars) + [vmem] * len(args),
        out_specs=[vmem] * len(outs),
        scratch_shapes=scratch,
        compiler_params=pltpu.CompilerParams(vmem_limit_bytes=20 * 2**20),
        cost_estimate=pl.CostEstimate(
            flops=int(cost),
            bytes_accessed=2 * sum(a.size * a.dtype.itemsize for a in args),
            transcendentals=0,
        ),
    )(*scalars, *args)


class Tile:
    def __init__(self, axis):
        self.axis = axis
        devices = lax.axis_size(axis)
        if devices == STEPS:
            self.video = [(p ^ 1, p) for p in range(devices)]
            self.partner = [(p ^ 2, p) for p in range(devices)]
        else:
            self.video = [((p + 1) % devices, p) for p in range(devices)]
            self.partner = [((p - 2) % devices, p) for p in range(devices)]

    def bring_video(self, block):
        return lax.ppermute(block, self.axis, self.video)

    def bring_partner(self, block):
        return lax.ppermute(block, self.axis, self.partner)

    def return_video(self, block):
        return lax.ppermute(block, self.axis, [(b, a) for a, b in self.video])

    def return_partner(self, block):
        return lax.ppermute(block, self.axis, [(b, a) for a, b in self.partner])


def per_device(
    video, video_ids, imu, imu_ids, audio, audio_ids,
    imu_log_scale, imu_bias, audio_log_scale, audio_bias,
):
    rows, width = video.shape
    line, square, narrow = ((1, rows), F32), ((rows, width), F32), ((rows, width), BF16)
    packed = ((rows + TAG_ROWS, width), BF16)
    of_imu, of_audio = (imu_log_scale, imu_bias), (audio_log_scale, audio_bias)
    along_row, along_col = Tile("row"), Tile("col")

    col_audio = along_col.bring_partner(audio), along_col.bring_partner(audio_ids)
    audio = (audio, audio_ids)
    video, imu = pack((video, imu), (video_ids, imu_ids))
    col_video = along_col.bring_video(video)

    loss, video_grad, imu_grad, audio_grad, video_on, imu_on = call(
        own_kernel,
        [line, square, square, square, packed, packed],
        of_imu + of_audio,
        (video, imu, *audio),
        rows, 1, COSTS["own"],
    )
    row_video = along_row.bring_video(video_on)
    row_imu = along_row.bring_partner(imu_on)
    tile = ((rows, rows), BF16)
    loss, far_weights = call(
        own_far_kernel,
        [line, tile],
        of_audio,
        (video, *col_audio, loss),
        rows, 0, COSTS["own_far"],
    )
    loss, col_loss, sums, far_col_weights = call(
        far_kernel,
        [line, line, narrow, tile],
        of_audio,
        (video, col_video, *col_audio, far_weights, loss),
        rows, 0, COSTS["far"],
    )
    got_audio = along_col.return_partner(sums)
    col_grad, near_weights, loss = call(
        near_kernel,
        [packed, tile, line],
        of_audio,
        (col_video, *audio, col_audio[0], far_col_weights, col_loss, loss),
        rows, 0, COSTS["near"],
    )
    got_col = along_col.return_video(col_grad)
    loss, row_grad, sums, row_weights, row_near_weights = call(
        row_kernel,
        [line, packed, narrow, tile, tile],
        of_imu,
        (video, row_video, imu, row_imu, loss),
        rows, 1, COSTS["row"],
    )
    got_row = along_row.return_video(row_grad)
    got_imu = along_row.return_partner(sums)
    video_grad, audio_grad, imu_grad, loss = call(
        late_kernel,
        [square, square, square, line],
        (),
        (
            col_audio[0], far_weights, col_video, near_weights, row_imu, row_weights, row_video,
            row_near_weights, video_grad, audio_grad, imu_grad, loss,
        ),
        rows, 0, COSTS["late"], False,
    )

    hbm, vmem = pltpu.HBM, pltpu.VMEM
    audio_grad, loss = summed(
        audio_sum_kernel,
        [square, line],
        [hbm, vmem],
        (got_audio, audio_grad, loss),
        COSTS["audio_sum"],
    )
    video_grad, loss = summed(
        video_sum_kernel,
        [square, line],
        [vmem, vmem],
        (got_col, video_grad, loss),
        COSTS["video_sum"],
    )
    video_grad, imu_grad, loss = summed(
        row_sum_kernel,
        [square, square, ((rows,), F32)],
        [hbm, hbm, vmem],
        (got_row, got_imu, video_grad, imu_grad, loss),
        COSTS["row_sum"],
    )
    return (video_grad, imu_grad, audio_grad, loss)


def solution(mesh):
    rows, vector = P(("row", "col"), None), P(("row", "col"))
    return jax.shard_map(
        per_device,
        mesh=mesh,
        in_specs=(rows, vector, rows, vector, rows, vector, P(), P(), P(), P()),
        out_specs=(rows, rows, rows, vector),
        check_vma=False,
    )
```

```python
import jax
import jax.numpy as jnp
from jax import lax
from jax.experimental import pallas as pl
from jax.experimental.pallas import tpu as pltpu
from jax.sharding import PartitionSpec as P

STEPS = 4
SLAB = 16
COLUMNS = 512
SUM_BLOCKS = 4
TAG_ROWS = 16
TAG_BASE = 256
COSTS = {
    "own": 0.5e9, "own_far": 0.5e9, "far": 0.5e9, "near": 0.5e9, "row": 0.5e9, "late": 0.01e9,
    "audio_sum": 5e9, "imu_sum": 0.01e9, "col_sum": 20e9, "row_sum": 0.5e9,
}

F32 = jnp.float32
BF16 = jnp.bfloat16


def pack_kernel(*refs):
    blocks, ids, packed = refs[:2], refs[2:4], refs[4:6]
    tags, (block_done, tags_done) = refs[6:8], refs[8:]
    rows, width = blocks[0].shape
    copies = [
        pltpu.make_async_copy(block, out.at[:rows, :], block_done.at[k])
        for k, (block, out) in enumerate(zip(blocks, packed))
    ]
    tag_copies = [
        pltpu.make_async_copy(source, tags[k], tags_done.at[k]) for k, source in enumerate(ids)
    ]
    for copy in tag_copies + copies:
        copy.start()
    for copy in tag_copies:
        copy.wait()
    for k, out in enumerate(packed):
        tag = tags[k][...].reshape(1, rows)
        high = tag // TAG_BASE
        low = tag - high * TAG_BASE
        both = jnp.concatenate([high, low, jnp.zeros((TAG_ROWS - 2, rows), jnp.int32)], axis=0)
        out[rows:, :rows] = both.astype(F32).astype(BF16)
        out[rows:, rows:] = jnp.zeros((TAG_ROWS, width - rows), BF16)
    for copy in copies:
        copy.wait()


def pack(blocks, ids):
    rows, width = blocks[0].shape
    hbm, vmem = pl.BlockSpec(memory_space=pltpu.HBM), pl.BlockSpec(memory_space=pltpu.VMEM)
    return pl.pallas_call(
        pack_kernel,
        out_shape=[pltpu.VMEM((rows + TAG_ROWS, width), BF16)] * 2,
        in_specs=[hbm] * 4,
        out_specs=[vmem] * 2,
        scratch_shapes=[
            *[pltpu.VMEM((rows,), jnp.int32)] * 2,
            pltpu.SemaphoreType.DMA((2,)),
            pltpu.SemaphoreType.DMA((2,)),
        ],
        compiler_params=pltpu.CompilerParams(vmem_limit_bytes=56 * 2**20),
    )(*blocks, *ids)


def tags_of(block):
    if isinstance(block, tuple):
        tags = block[1][...]
        return tags.reshape(1, tags.shape[0]).astype(F32)
    rows = block.shape[0] - TAG_ROWS
    tags = block[rows:, :rows].astype(F32)
    return tags[0:1] * TAG_BASE + tags[1:2]


def rows_of(block):
    return block[0] if isinstance(block, tuple) else block


def meet(video, partner, scalars, products, weights):
    rows = weights.shape[0]
    log_scale, offset = scalars[0][0], scalars[1][0]
    scale = jnp.exp(jnp.full((1, rows), log_scale, F32))
    products[...] = lax.dot_general(
        rows_of(partner)[:rows, :], video[:rows, :], (((1,), (1,)), ((), ())), preferred_element_type=F32
    )
    video_tags = tags_of(video)
    partner_tags = jnp.transpose(jnp.broadcast_to(tags_of(partner), (8, rows)))[:, :1]
    total = jnp.zeros((8, rows), F32)
    for start in range(0, rows, SLAB):
        part = slice(start, start + SLAB)
        logits = scale * products[part, :] + offset
        same = partner_tags[part, :] == video_tags
        flipped = -logits
        z = jnp.where(same, flipped, logits)
        e = jnp.exp(jnp.minimum(logits, flipped))
        inverse = 1.0 / (1.0 + e)
        sigmoid = jnp.where(z >= 0.0, inverse, e * inverse)
        weights[part, :] = (jnp.where(same, -scale, scale) * sigmoid).astype(BF16)
        log1p = jnp.where(e < 0.005, e * (1.0 - 0.5 * e), jnp.log(1.0 + e))
        losses = jnp.maximum(z, 0.0) + log1p
        total = total + jnp.sum(losses.reshape(SLAB // 8, 8, rows), axis=0)
    return jnp.sum(total, axis=0, keepdims=True)


def column_parts(ref):
    return [slice(c, c + COLUMNS) for c in range(0, ref.shape[1], COLUMNS)]


def to_video(weights, partner, part):
    rows = weights.shape[0]
    return lax.dot_general(
        weights[...], rows_of(partner)[:rows, part], (((0,), (0,)), ((), ())), preferred_element_type=F32
    )


def to_partner(weights, video, part):
    return jnp.dot(weights[...], video[: weights.shape[0], part], preferred_element_type=F32)


def own_kernel(
    imu_log_scale, imu_bias, audio_log_scale, audio_bias, video, imu, audio, audio_ids,
    loss, video_grad, imu_grad, audio_grad, video_on, imu_on, products, weights,
):
    video_on[...] = video[...]
    imu_on[...] = imu[...]
    audio = (audio, audio_ids)
    loss[...] = meet(video, audio, (audio_log_scale, audio_bias), products, weights)
    for part in column_parts(video):
        video_grad[:, part] = to_video(weights, audio, part)
        audio_grad[:, part] = to_partner(weights, video, part)
    loss[...] += meet(video, imu, (imu_log_scale, imu_bias), products, weights)
    for part in column_parts(video):
        video_grad[:, part] += to_video(weights, imu, part)
        imu_grad[:, part] = to_partner(weights, video, part)


def put_losses(losses, packed):
    rows = losses.shape[1]
    terms = []
    for _ in range(3):
        terms.append(losses.astype(BF16).astype(F32))
        losses = losses - terms[-1]
    terms.append(jnp.zeros((TAG_ROWS - 3, rows), F32))
    packed[rows:, :rows] = jnp.concatenate(terms, axis=0).astype(BF16)
    packed[rows:, rows:] = jnp.zeros((TAG_ROWS, packed.shape[1] - rows), BF16)


def own_far_kernel(
    log_scale, bias, video, audio, audio_ids, loss_in, loss, weights, products
):
    scalars = (log_scale, bias)
    loss[...] = loss_in[...] + meet(video, (audio, audio_ids), scalars, products, weights)


def far_kernel(
    log_scale, bias, video, other_video, audio, audio_ids, own_weights, loss_in,
    loss, other_loss, sums, weights, products,
):
    loss[...] = loss_in[...]
    other_loss[...] = meet(other_video, (audio, audio_ids), (log_scale, bias), products, weights)
    for part in column_parts(video):
        both = to_partner(own_weights, video, part) + to_partner(weights, other_video, part)
        sums[:, part] = both.astype(BF16)


def near_kernel(
    log_scale, bias, other_video, audio, audio_ids, far_audio, far_weights, other_loss_in, loss_in,
    other_grad, weights, loss, products,
):
    audio = (audio, audio_ids)
    rows = weights.shape[0]
    loss[...] = loss_in[...]
    losses = meet(other_video, audio, (log_scale, bias), products, weights)
    put_losses(other_loss_in[...] + losses, other_grad)
    for part in column_parts(other_video):
        both = to_video(weights, audio, part) + to_video(far_weights, far_audio, part)
        other_grad[:rows, part] = both.astype(BF16)


def row_kernel(
    log_scale, bias, video, other_video, imu, other_imu, loss_in,
    loss, other_grad, sums, weights, near_weights, products, other_weights,
):
    scalars = (log_scale, bias)
    rows = sums.shape[0]
    losses = meet(other_video, imu, scalars, products, near_weights)
    losses = losses + meet(other_video, other_imu, scalars, products, other_weights)
    put_losses(losses, other_grad)
    loss[...] = loss_in[...] + meet(video, other_imu, scalars, products, weights)
    for part in column_parts(video):
        other_sum = to_video(near_weights, imu, part) + to_video(other_weights, other_imu, part)
        other_grad[:rows, part] = other_sum.astype(BF16)
        both = to_partner(weights, video, part) + to_partner(other_weights, other_video, part)
        sums[:, part] = both.astype(BF16)


def late_kernel(
    far_audio, far_weights, col_video, near_weights, row_imu, row_weights, row_video,
    row_near_weights, video_in, audio_in, imu_in, loss_in,
    video_grad, audio_grad, imu_grad, loss,
):
    loss[...] = loss_in[...]
    for part in column_parts(video_grad):
        video_sum = to_video(far_weights, far_audio, part) + to_video(row_weights, row_imu, part)
        video_grad[:, part] = video_in[:, part] + video_sum
        audio_grad[:, part] = audio_in[:, part] + to_partner(near_weights, col_video, part)
        imu_grad[:, part] = imu_in[:, part] + to_partner(row_near_weights, row_video, part)


def added(parts, out, buffer, done):
    rows = out.shape[0] // SUM_BLOCKS
    copies = []
    for k in range(SUM_BLOCKS):
        block = slice(k * rows, (k + 1) * rows)
        total = parts[0][block, :]
        for part in parts[1:]:
            total = total + part[block, :].astype(F32)
        buffer[block, :] = total
        copy = pltpu.make_async_copy(buffer.at[block, :], out.at[block, :], done.at[k])
        copy.start()
        copies.append(copy)
    return copies


def losses_in(packed):
    rows = packed.shape[0] - TAG_ROWS
    return jnp.sum(packed[rows:, :rows].astype(F32), axis=0, keepdims=True)


def partner_sum_kernel(got, grad_in, loss_in, grad, loss, buffer, done):
    copies = added((grad_in, got), grad, buffer, done)
    loss[...] = loss_in[...]
    for copy in copies:
        copy.wait()


def col_sum_kernel(got_video, video_in, loss_in, video_grad, loss):
    rows = video_grad.shape[0]
    video_grad[...] = video_in[...] + got_video[:rows, :].astype(F32)
    loss[...] = loss_in[...] + losses_in(got_video)


def row_sum_kernel(got_video, video_in, loss_in, video_grad, loss, buffer, done):
    copies = added((video_in, got_video), video_grad, buffer, done)
    rows = video_in.shape[0]
    total = loss_in[...] + losses_in(got_video)
    loss[...] = (total / (2.0 * STEPS * rows)).reshape(rows)
    for copy in copies:
        copy.wait()


def summed(kernel, outs, spaces, args, cost):
    vmem = pl.BlockSpec(memory_space=pltpu.VMEM)
    return pl.pallas_call(
        kernel,
        out_shape=[jax.ShapeDtypeStruct(*out) for out in outs],
        in_specs=[vmem] * len(args),
        out_specs=[pl.BlockSpec(memory_space=space) for space in spaces],
        scratch_shapes=[pltpu.VMEM(outs[0][0], F32), pltpu.SemaphoreType.DMA((SUM_BLOCKS,))]
        * sum(space == pltpu.HBM for space in spaces),
        compiler_params=pltpu.CompilerParams(vmem_limit_bytes=20 * 2**20),
        cost_estimate=pl.CostEstimate(flops=int(cost), bytes_accessed=0, transcendentals=0),
    )(*args)


def call(kernel, outs, scalars, args, rows, weights=1, cost=0, meets=True):
    smem, vmem = pl.BlockSpec(memory_space=pltpu.SMEM), pl.BlockSpec(memory_space=pltpu.VMEM)
    scratch = [pltpu.VMEM((rows, rows), F32)] + [pltpu.VMEM((rows, rows), BF16)] * weights
    scratch = scratch if meets else []
    return pl.pallas_call(
        kernel,
        out_shape=[jax.ShapeDtypeStruct(*out) for out in outs],
        in_specs=[smem] * len(scalars) + [vmem] * len(args),
        out_specs=[vmem] * len(outs),
        scratch_shapes=scratch,
        compiler_params=pltpu.CompilerParams(vmem_limit_bytes=20 * 2**20),
        cost_estimate=pl.CostEstimate(
            flops=int(cost),
            bytes_accessed=2 * sum(a.size * a.dtype.itemsize for a in args),
            transcendentals=0,
        ),
    )(*scalars, *args)


class Tile:
    def __init__(self, axis):
        self.axis = axis
        devices = lax.axis_size(axis)
        if devices == STEPS:
            self.video = [(p ^ 1, p) for p in range(devices)]
            self.partner = [(p ^ 2, p) for p in range(devices)]
        else:
            self.video = [((p + 1) % devices, p) for p in range(devices)]
            self.partner = [((p - 2) % devices, p) for p in range(devices)]

    def bring_video(self, block):
        return lax.ppermute(block, self.axis, self.video)

    def bring_partner(self, block):
        return lax.ppermute(block, self.axis, self.partner)

    def return_video(self, block):
        return lax.ppermute(block, self.axis, [(b, a) for a, b in self.video])

    def return_partner(self, block):
        return lax.ppermute(block, self.axis, [(b, a) for a, b in self.partner])


def per_device(
    video, video_ids, imu, imu_ids, audio, audio_ids,
    imu_log_scale, imu_bias, audio_log_scale, audio_bias,
):
    rows, width = video.shape
    line, square, narrow = ((1, rows), F32), ((rows, width), F32), ((rows, width), BF16)
    packed = ((rows + TAG_ROWS, width), BF16)
    of_imu, of_audio = (imu_log_scale, imu_bias), (audio_log_scale, audio_bias)
    along_row, along_col = Tile("row"), Tile("col")

    col_audio = along_col.bring_partner(audio), along_col.bring_partner(audio_ids)
    audio = (audio, audio_ids)
    video, imu = pack((video, imu), (video_ids, imu_ids))
    col_video = along_col.bring_video(video)

    loss, video_grad, imu_grad, audio_grad, video_on, imu_on = call(
        own_kernel,
        [line, square, square, square, packed, packed],
        of_imu + of_audio,
        (video, imu, *audio),
        rows, 1, COSTS["own"],
    )
    row_video = along_row.bring_video(video_on)
    row_imu = along_row.bring_partner(imu_on)
    tile = ((rows, rows), BF16)
    loss, far_weights = call(
        own_far_kernel,
        [line, tile],
        of_audio,
        (video, *col_audio, loss),
        rows, 0, COSTS["own_far"],
    )
    loss, col_loss, sums, far_col_weights = call(
        far_kernel,
        [line, line, narrow, tile],
        of_audio,
        (video, col_video, *col_audio, far_weights, loss),
        rows, 0, COSTS["far"],
    )
    got_audio = along_col.return_partner(sums)
    col_grad, near_weights, loss = call(
        near_kernel,
        [packed, tile, line],
        of_audio,
        (col_video, *audio, col_audio[0], far_col_weights, col_loss, loss),
        rows, 0, COSTS["near"],
    )
    got_col = along_col.return_video(col_grad)
    loss, row_grad, sums, row_weights, row_near_weights = call(
        row_kernel,
        [line, packed, narrow, tile, tile],
        of_imu,
        (video, row_video, imu, row_imu, loss),
        rows, 1, COSTS["row"],
    )
    got_row = along_row.return_video(row_grad)
    got_imu = along_row.return_partner(sums)
    video_grad, audio_grad, imu_grad, loss = call(
        late_kernel,
        [square, square, square, line],
        (),
        (
            col_audio[0], far_weights, col_video, near_weights, row_imu, row_weights, row_video,
            row_near_weights, video_grad, audio_grad, imu_grad, loss,
        ),
        rows, 0, COSTS["late"], False,
    )

    hbm, vmem = pltpu.HBM, pltpu.VMEM
    audio_grad, loss = summed(
        partner_sum_kernel,
        [square, line],
        [hbm, vmem],
        (got_audio, audio_grad, loss),
        COSTS["audio_sum"],
    )
    imu_grad, loss = summed(
        partner_sum_kernel,
        [square, line],
        [hbm, vmem],
        (got_imu, imu_grad, loss),
        COSTS["imu_sum"],
    )
    video_grad, loss = summed(
        col_sum_kernel,
        [square, line],
        [vmem, vmem],
        (got_col, video_grad, loss),
        COSTS["col_sum"],
    )
    video_grad, loss = summed(
        row_sum_kernel,
        [square, ((rows,), F32)],
        [hbm, vmem],
        (got_row, video_grad, loss),
        COSTS["row_sum"],
    )
    return (video_grad, imu_grad, audio_grad, loss)


def solution(mesh):
    rows, vector = P(("row", "col"), None), P(("row", "col"))
    return jax.shard_map(
        per_device,
        mesh=mesh,
        in_specs=(rows, vector, rows, vector, rows, vector, P(), P(), P(), P()),
        out_specs=(rows, rows, rows, vector),
        check_vma=False,
    )
```

```python
import jax
import jax.numpy as jnp
from jax import lax
from jax.experimental import pallas as pl
from jax.experimental.pallas import tpu as pltpu
from jax.sharding import PartitionSpec as P

STEPS = 4
SLAB = 16
COLUMNS = 512
SUM_BLOCKS = 4
TAG_ROWS = 16
TAG_BASE = 256
COSTS = {
    "own": 0.5e9, "own_far": 0.5e9, "far": 0.5e9, "near": 0.5e9, "row": 0.5e9, "late": 0.01e9,
    "audio_sum": 5e9, "imu_sum": 0.01e9, "col_sum": 20e9, "row_sum": 0.5e9,
}

F32 = jnp.float32
BF16 = jnp.bfloat16


def pack_kernel(*refs):
    blocks, ids, packed = refs[:2], refs[2:4], refs[4:6]
    tags, (block_done, tags_done) = refs[6:8], refs[8:]
    rows, width = blocks[0].shape
    copies = [
        pltpu.make_async_copy(block, out.at[:rows, :], block_done.at[k])
        for k, (block, out) in enumerate(zip(blocks, packed))
    ]
    tag_copies = [
        pltpu.make_async_copy(source, tags[k], tags_done.at[k]) for k, source in enumerate(ids)
    ]
    for copy in tag_copies + copies:
        copy.start()
    for copy in tag_copies:
        copy.wait()
    for k, out in enumerate(packed):
        tag = tags[k][...].reshape(1, rows)
        high = tag // TAG_BASE
        low = tag - high * TAG_BASE
        both = jnp.concatenate([high, low, jnp.zeros((TAG_ROWS - 2, rows), jnp.int32)], axis=0)
        out[rows:, :rows] = both.astype(F32).astype(BF16)
        out[rows:, rows:] = jnp.zeros((TAG_ROWS, width - rows), BF16)
    for copy in copies:
        copy.wait()


def pack(blocks, ids):
    rows, width = blocks[0].shape
    hbm, vmem = pl.BlockSpec(memory_space=pltpu.HBM), pl.BlockSpec(memory_space=pltpu.VMEM)
    return pl.pallas_call(
        pack_kernel,
        out_shape=[pltpu.VMEM((rows + TAG_ROWS, width), BF16)] * 2,
        in_specs=[hbm] * 4,
        out_specs=[vmem] * 2,
        scratch_shapes=[
            *[pltpu.VMEM((rows,), jnp.int32)] * 2,
            pltpu.SemaphoreType.DMA((2,)),
            pltpu.SemaphoreType.DMA((2,)),
        ],
        compiler_params=pltpu.CompilerParams(vmem_limit_bytes=56 * 2**20),
    )(*blocks, *ids)


def tags_of(block):
    if isinstance(block, tuple):
        tags = block[1][...]
        return tags.reshape(1, tags.shape[0]).astype(F32)
    rows = block.shape[0] - TAG_ROWS
    tags = block[rows:, :rows].astype(F32)
    return tags[0:1] * TAG_BASE + tags[1:2]


def rows_of(block):
    return block[0] if isinstance(block, tuple) else block


def meet(video, partner, scalars, products, weights):
    rows = weights.shape[0]
    log_scale, offset = scalars[0][0], scalars[1][0]
    scale = jnp.exp(jnp.full((1, rows), log_scale, F32))
    products[...] = lax.dot_general(
        rows_of(partner)[:rows, :], video[:rows, :], (((1,), (1,)), ((), ())), preferred_element_type=F32
    )
    video_tags = tags_of(video)
    partner_tags = jnp.transpose(jnp.broadcast_to(tags_of(partner), (8, rows)))[:, :1]
    total = jnp.zeros((8, rows), F32)
    for start in range(0, rows, SLAB):
        part = slice(start, start + SLAB)
        logits = scale * products[part, :] + offset
        same = partner_tags[part, :] == video_tags
        flipped = -logits
        z = jnp.where(same, flipped, logits)
        e = jnp.exp(jnp.minimum(logits, flipped))
        inverse = 1.0 / (1.0 + e)
        sigmoid = jnp.where(z >= 0.0, inverse, e * inverse)
        weights[part, :] = (jnp.where(same, -scale, scale) * sigmoid).astype(BF16)
        log1p = jnp.where(e < 0.005, e * (1.0 - 0.5 * e), jnp.log(1.0 + e))
        losses = jnp.maximum(z, 0.0) + log1p
        total = total + jnp.sum(losses.reshape(SLAB // 8, 8, rows), axis=0)
    return jnp.sum(total, axis=0, keepdims=True)


def column_parts(ref):
    return [slice(c, c + COLUMNS) for c in range(0, ref.shape[1], COLUMNS)]


def to_video(weights, partner, part):
    rows = weights.shape[0]
    return lax.dot_general(
        weights[...], rows_of(partner)[:rows, part], (((0,), (0,)), ((), ())), preferred_element_type=F32
    )


def to_partner(weights, video, part):
    return jnp.dot(weights[...], video[: weights.shape[0], part], preferred_element_type=F32)


def own_kernel(
    imu_log_scale, imu_bias, audio_log_scale, audio_bias, video, imu, audio, audio_ids,
    loss, video_grad, imu_grad, audio_grad, video_on, imu_on, products, weights,
):
    video_on[...] = video[...]
    imu_on[...] = imu[...]
    audio = (audio, audio_ids)
    loss[...] = meet(video, audio, (audio_log_scale, audio_bias), products, weights)
    for part in column_parts(video):
        video_grad[:, part] = to_video(weights, audio, part)
        audio_grad[:, part] = to_partner(weights, video, part)
    loss[...] += meet(video, imu, (imu_log_scale, imu_bias), products, weights)
    for part in column_parts(video):
        video_grad[:, part] += to_video(weights, imu, part)
        imu_grad[:, part] = to_partner(weights, video, part)


def put_losses(losses, packed):
    rows = losses.shape[1]
    terms = []
    for _ in range(3):
        terms.append(losses.astype(BF16).astype(F32))
        losses = losses - terms[-1]
    terms.append(jnp.zeros((TAG_ROWS - 3, rows), F32))
    packed[rows:, :rows] = jnp.concatenate(terms, axis=0).astype(BF16)
    packed[rows:, rows:] = jnp.zeros((TAG_ROWS, packed.shape[1] - rows), BF16)


def own_far_kernel(
    log_scale, bias, video, audio, audio_ids, loss_in, loss, weights, products
):
    scalars = (log_scale, bias)
    loss[...] = loss_in[...] + meet(video, (audio, audio_ids), scalars, products, weights)


def far_kernel(
    log_scale, bias, video, other_video, audio, audio_ids, own_weights, loss_in,
    loss, other_loss, sums, weights, products,
):
    loss[...] = loss_in[...]
    other_loss[...] = meet(other_video, (audio, audio_ids), (log_scale, bias), products, weights)
    for part in column_parts(video):
        both = to_partner(own_weights, video, part) + to_partner(weights, other_video, part)
        sums[:, part] = both.astype(BF16)


def near_kernel(
    log_scale, bias, other_video, audio, audio_ids, far_audio, far_weights, other_loss_in, loss_in,
    other_grad, weights, loss, products,
):
    audio = (audio, audio_ids)
    rows = weights.shape[0]
    loss[...] = loss_in[...]
    losses = meet(other_video, audio, (log_scale, bias), products, weights)
    put_losses(other_loss_in[...] + losses, other_grad)
    for part in column_parts(other_video):
        both = to_video(weights, audio, part) + to_video(far_weights, far_audio, part)
        other_grad[:rows, part] = both.astype(BF16)


def row_kernel(
    log_scale, bias, video, other_video, imu, other_imu, loss_in,
    loss, other_grad, sums, weights, near_weights, products, other_weights,
):
    scalars = (log_scale, bias)
    rows = sums.shape[0]
    losses = meet(other_video, imu, scalars, products, near_weights)
    losses = losses + meet(other_video, other_imu, scalars, products, other_weights)
    put_losses(losses, other_grad)
    loss[...] = loss_in[...] + meet(video, other_imu, scalars, products, weights)
    for part in column_parts(video):
        other_sum = to_video(near_weights, imu, part) + to_video(other_weights, other_imu, part)
        other_grad[:rows, part] = other_sum.astype(BF16)
        both = to_partner(weights, video, part) + to_partner(other_weights, other_video, part)
        sums[:, part] = both.astype(BF16)


def late_kernel(
    far_audio, far_weights, col_video, near_weights, row_imu, row_weights, row_video,
    row_near_weights, video_in, audio_in, imu_in, loss_in,
    video_grad, audio_grad, imu_grad, loss,
):
    loss[...] = loss_in[...]
    for part in column_parts(video_grad):
        video_sum = to_video(far_weights, far_audio, part) + to_video(row_weights, row_imu, part)
        video_grad[:, part] = video_in[:, part] + video_sum
        audio_grad[:, part] = audio_in[:, part] + to_partner(near_weights, col_video, part)
        imu_grad[:, part] = imu_in[:, part] + to_partner(row_near_weights, row_video, part)


def added(parts, out, buffer, done):
    rows = out.shape[0] // SUM_BLOCKS
    copies = []
    for k in range(SUM_BLOCKS):
        block = slice(k * rows, (k + 1) * rows)
        total = parts[0][block, :]
        for part in parts[1:]:
            total = total + part[block, :].astype(F32)
        buffer[block, :] = total
        copy = pltpu.make_async_copy(buffer.at[block, :], out.at[block, :], done.at[k])
        copy.start()
        copies.append(copy)
    return copies


def losses_in(packed):
    rows = packed.shape[0] - TAG_ROWS
    return jnp.sum(packed[rows:, :rows].astype(F32), axis=0, keepdims=True)


def partner_sum_kernel(got, grad_in, loss_in, grad, loss, buffer, done):
    copies = added((grad_in, got), grad, buffer, done)
    loss[...] = loss_in[...]
    for copy in copies:
        copy.wait()


def col_sum_kernel(got_video, video_in, loss_in, video_grad, loss):
    rows = video_grad.shape[0]
    video_grad[...] = video_in[...] + got_video[:rows, :].astype(F32)
    loss[...] = loss_in[...] + losses_in(got_video)


def row_sum_kernel(
    got_video, video_in, loss_in, video_grad, loss, buffer, done, losses, losses_done
):
    rows = video_in.shape[0]
    total = loss_in[...] + losses_in(got_video)
    losses[...] = (total / (2.0 * STEPS * rows)).reshape(rows)
    copy = pltpu.make_async_copy(losses, loss, losses_done)
    copy.start()
    for part in added((video_in, got_video), video_grad, buffer, done):
        part.wait()
    copy.wait()


def summed(kernel, outs, spaces, args, cost):
    vmem = pl.BlockSpec(memory_space=pltpu.VMEM)
    return pl.pallas_call(
        kernel,
        out_shape=[jax.ShapeDtypeStruct(*out) for out in outs],
        in_specs=[vmem] * len(args),
        out_specs=[pl.BlockSpec(memory_space=space) for space in spaces],
        scratch_shapes=[
            scratch
            for (shape, _), space in zip(outs, spaces)
            if space == pltpu.HBM
            for scratch in (
                pltpu.VMEM(shape, F32),
                pltpu.SemaphoreType.DMA((SUM_BLOCKS,) if len(shape) == 2 else ()),
            )
        ],
        compiler_params=pltpu.CompilerParams(vmem_limit_bytes=20 * 2**20),
        cost_estimate=pl.CostEstimate(flops=int(cost), bytes_accessed=0, transcendentals=0),
    )(*args)


def call(kernel, outs, scalars, args, rows, weights=1, cost=0, meets=True):
    smem, vmem = pl.BlockSpec(memory_space=pltpu.SMEM), pl.BlockSpec(memory_space=pltpu.VMEM)
    scratch = [pltpu.VMEM((rows, rows), F32)] + [pltpu.VMEM((rows, rows), BF16)] * weights
    scratch = scratch if meets else []
    return pl.pallas_call(
        kernel,
        out_shape=[jax.ShapeDtypeStruct(*out) for out in outs],
        in_specs=[smem] * len(scalars) + [vmem] * len(args),
        out_specs=[vmem] * len(outs),
        scratch_shapes=scratch,
        compiler_params=pltpu.CompilerParams(vmem_limit_bytes=20 * 2**20),
        cost_estimate=pl.CostEstimate(
            flops=int(cost),
            bytes_accessed=2 * sum(a.size * a.dtype.itemsize for a in args),
            transcendentals=0,
        ),
    )(*scalars, *args)


class Tile:
    def __init__(self, axis):
        self.axis = axis
        devices = lax.axis_size(axis)
        if devices == STEPS:
            self.video = [(p ^ 1, p) for p in range(devices)]
            self.partner = [(p ^ 2, p) for p in range(devices)]
        else:
            self.video = [((p + 1) % devices, p) for p in range(devices)]
            self.partner = [((p - 2) % devices, p) for p in range(devices)]

    def bring_video(self, block):
        return lax.ppermute(block, self.axis, self.video)

    def bring_partner(self, block):
        return lax.ppermute(block, self.axis, self.partner)

    def return_video(self, block):
        return lax.ppermute(block, self.axis, [(b, a) for a, b in self.video])

    def return_partner(self, block):
        return lax.ppermute(block, self.axis, [(b, a) for a, b in self.partner])


def per_device(
    video, video_ids, imu, imu_ids, audio, audio_ids,
    imu_log_scale, imu_bias, audio_log_scale, audio_bias,
):
    rows, width = video.shape
    line, square, narrow = ((1, rows), F32), ((rows, width), F32), ((rows, width), BF16)
    packed = ((rows + TAG_ROWS, width), BF16)
    of_imu, of_audio = (imu_log_scale, imu_bias), (audio_log_scale, audio_bias)
    along_row, along_col = Tile("row"), Tile("col")

    col_audio = along_col.bring_partner(audio), along_col.bring_partner(audio_ids)
    audio = (audio, audio_ids)
    video, imu = pack((video, imu), (video_ids, imu_ids))
    col_video = along_col.bring_video(video)

    loss, video_grad, imu_grad, audio_grad, video_on, imu_on = call(
        own_kernel,
        [line, square, square, square, packed, packed],
        of_imu + of_audio,
        (video, imu, *audio),
        rows, 1, COSTS["own"],
    )
    row_video = along_row.bring_video(video_on)
    row_imu = along_row.bring_partner(imu_on)
    tile = ((rows, rows), BF16)
    loss, far_weights = call(
        own_far_kernel,
        [line, tile],
        of_audio,
        (video, *col_audio, loss),
        rows, 0, COSTS["own_far"],
    )
    loss, col_loss, sums, far_col_weights = call(
        far_kernel,
        [line, line, narrow, tile],
        of_audio,
        (video, col_video, *col_audio, far_weights, loss),
        rows, 0, COSTS["far"],
    )
    got_audio = along_col.return_partner(sums)
    col_grad, near_weights, loss = call(
        near_kernel,
        [packed, tile, line],
        of_audio,
        (col_video, *audio, col_audio[0], far_col_weights, col_loss, loss),
        rows, 0, COSTS["near"],
    )
    got_col = along_col.return_video(col_grad)
    loss, row_grad, sums, row_weights, row_near_weights = call(
        row_kernel,
        [line, packed, narrow, tile, tile],
        of_imu,
        (video, row_video, imu, row_imu, loss),
        rows, 1, COSTS["row"],
    )
    got_row = along_row.return_video(row_grad)
    got_imu = along_row.return_partner(sums)
    video_grad, audio_grad, imu_grad, loss = call(
        late_kernel,
        [square, square, square, line],
        (),
        (
            col_audio[0], far_weights, col_video, near_weights, row_imu, row_weights, row_video,
            row_near_weights, video_grad, audio_grad, imu_grad, loss,
        ),
        rows, 0, COSTS["late"], False,
    )

    hbm, vmem = pltpu.HBM, pltpu.VMEM
    audio_grad, loss = summed(
        partner_sum_kernel,
        [square, line],
        [hbm, vmem],
        (got_audio, audio_grad, loss),
        COSTS["audio_sum"],
    )
    imu_grad, loss = summed(
        partner_sum_kernel,
        [square, line],
        [hbm, vmem],
        (got_imu, imu_grad, loss),
        COSTS["imu_sum"],
    )
    video_grad, loss = summed(
        col_sum_kernel,
        [square, line],
        [vmem, vmem],
        (got_col, video_grad, loss),
        COSTS["col_sum"],
    )
    video_grad, loss = summed(
        row_sum_kernel,
        [square, ((rows,), F32)],
        [hbm, hbm],
        (got_row, video_grad, loss),
        COSTS["row_sum"],
    )
    return (video_grad, imu_grad, audio_grad, loss)


def solution(mesh):
    rows, vector = P(("row", "col"), None), P(("row", "col"))
    return jax.shard_map(
        per_device,
        mesh=mesh,
        in_specs=(rows, vector, rows, vector, rows, vector, P(), P(), P(), P()),
        out_specs=(rows, rows, rows, vector),
        check_vma=False,
    )
```

```python
import jax
import jax.numpy as jnp
from jax import lax
from jax.experimental import pallas as pl
from jax.experimental.pallas import tpu as pltpu
from jax.sharding import PartitionSpec as P

STEPS = 4
SLAB = 16
COLUMNS = 512
SUM_BLOCKS = 4
TAG_ROWS = 16
TAG_BASE = 256
COSTS = {
    "own": 0.5e9, "own_far": 0.5e9, "far": 0.5e9, "near": 0.5e9, "row": 0.5e9, "late": 0.01e9,
    "audio_sum": 5e9, "imu_sum": 0.01e9, "col_sum": 20e9, "row_sum": 0.5e9,
}

F32 = jnp.float32
BF16 = jnp.bfloat16


def pack_kernel(*refs):
    scalars, blocks, ids = refs[:4], refs[4:7], refs[7:10]
    outs, own = refs[10:13], refs[13:17]
    tags, at_hand, (block_done, tags_done, scalars_done) = refs[17:20], refs[20:24], refs[24:27]
    products, weights = refs[27:]
    rows, width = blocks[0].shape
    odd = lax.axis_index("row") % 2 == 1
    copies = [
        pltpu.make_async_copy(block, out.at[:rows, :], block_done.at[k])
        for k, (block, out) in enumerate(zip(blocks, outs))
    ]
    small = [
        pltpu.make_async_copy(source, tags[k], tags_done.at[k]) for k, source in enumerate(ids)
    ] + [
        pltpu.make_async_copy(source, at_hand[k], scalars_done.at[k])
        for k, source in enumerate(scalars)
    ]
    for copy in small + copies:
        copy.start()
    for copy in small:
        copy.wait()
    for k, out in enumerate(outs[:2]):
        tag = tags[k][...].reshape(1, rows)
        high = tag // TAG_BASE
        low = tag - high * TAG_BASE
        both = jnp.concatenate([high, low, jnp.zeros((TAG_ROWS - 2, rows), jnp.int32)], axis=0)
        out[rows:, :rows] = both.astype(F32).astype(BF16)
        out[rows:, rows:] = jnp.zeros((TAG_ROWS, width - rows), BF16)
    for copy in copies:
        copy.wait()

    @pl.when(odd)
    def _():
        own_meetings(at_hand, outs[0], outs[1], (outs[2], tags[2]), own, products, weights)


def pack(scalars, blocks, ids):
    rows, width = blocks[0].shape
    hbm, vmem = pl.BlockSpec(memory_space=pltpu.HBM), pl.BlockSpec(memory_space=pltpu.VMEM)
    packed, square = pltpu.VMEM((rows + TAG_ROWS, width), BF16), pltpu.VMEM((rows, width), F32)
    return pl.pallas_call(
        pack_kernel,
        out_shape=[packed] * 2 + [pltpu.VMEM((rows, width), BF16), pltpu.VMEM((1, rows), F32)]
        + [square] * 3,
        in_specs=[hbm] * 10,
        out_specs=[vmem] * 7,
        scratch_shapes=[
            *[pltpu.VMEM((rows,), jnp.int32)] * 3,
            *[pltpu.SMEM((1,), F32)] * 4,
            pltpu.SemaphoreType.DMA((3,)),
            pltpu.SemaphoreType.DMA((3,)),
            pltpu.SemaphoreType.DMA((4,)),
            pltpu.VMEM((rows, rows), F32),
            pltpu.VMEM((rows, rows), BF16),
        ],
        compiler_params=pltpu.CompilerParams(vmem_limit_bytes=52 * 2**20),
    )(*scalars, *blocks, *ids)


def tags_of(block):
    if isinstance(block, tuple):
        tags = block[1][...]
        return tags.reshape(1, tags.shape[0]).astype(F32)
    rows = block.shape[0] - TAG_ROWS
    tags = block[rows:, :rows].astype(F32)
    return tags[0:1] * TAG_BASE + tags[1:2]


def rows_of(block):
    return block[0] if isinstance(block, tuple) else block


def meet(video, partner, scalars, products, weights):
    rows = weights.shape[0]
    log_scale, offset = scalars[0][0], scalars[1][0]
    scale = jnp.exp(jnp.full((1, rows), log_scale, F32))
    products[...] = lax.dot_general(
        rows_of(partner)[:rows, :], video[:rows, :], (((1,), (1,)), ((), ())), preferred_element_type=F32
    )
    video_tags = tags_of(video)
    partner_tags = jnp.transpose(jnp.broadcast_to(tags_of(partner), (8, rows)))[:, :1]
    total = jnp.zeros((8, rows), F32)
    for start in range(0, rows, SLAB):
        part = slice(start, start + SLAB)
        logits = scale * products[part, :] + offset
        same = partner_tags[part, :] == video_tags
        flipped = -logits
        z = jnp.where(same, flipped, logits)
        e = jnp.exp(jnp.minimum(logits, flipped))
        inverse = 1.0 / (1.0 + e)
        sigmoid = jnp.where(z >= 0.0, inverse, e * inverse)
        weights[part, :] = (jnp.where(same, -scale, scale) * sigmoid).astype(BF16)
        log1p = jnp.where(e < 0.005, e * (1.0 - 0.5 * e), jnp.log(1.0 + e))
        losses = jnp.maximum(z, 0.0) + log1p
        total = total + jnp.sum(losses.reshape(SLAB // 8, 8, rows), axis=0)
    return jnp.sum(total, axis=0, keepdims=True)


def column_parts(ref):
    return [slice(c, c + COLUMNS) for c in range(0, ref.shape[1], COLUMNS)]


def to_video(weights, partner, part):
    rows = weights.shape[0]
    return lax.dot_general(
        weights[...], rows_of(partner)[:rows, part], (((0,), (0,)), ((), ())), preferred_element_type=F32
    )


def to_partner(weights, video, part):
    return jnp.dot(weights[...], video[: weights.shape[0], part], preferred_element_type=F32)


def own_meetings(scalars, video, imu, audio, outs, products, weights):
    loss, video_grad, imu_grad, audio_grad = outs
    loss[...] = meet(video, audio, scalars[2:], products, weights)
    for part in column_parts(video):
        video_grad[:, part] = to_video(weights, audio, part)
        audio_grad[:, part] = to_partner(weights, video, part)
    loss[...] += meet(video, imu, scalars[:2], products, weights)
    for part in column_parts(video):
        video_grad[:, part] += to_video(weights, imu, part)
        imu_grad[:, part] = to_partner(weights, video, part)


def own_kernel(*refs):
    scalars, (video, imu, audio, audio_ids), made = refs[:4], refs[4:8], refs[8:12]
    outs, (video_on, imu_on, products, weights) = refs[12:16], refs[16:]
    even = lax.axis_index("row") % 2 == 0
    video_on[...] = video[...]
    imu_on[...] = imu[...]

    @pl.when(even)
    def _():
        own_meetings(scalars, video, imu, (audio, audio_ids), outs, products, weights)

    @pl.when(jnp.logical_not(even))
    def _():
        for out, value in zip(outs, made):
            out[...] = value[...]


def put_losses(losses, packed):
    rows = losses.shape[1]
    terms = []
    for _ in range(3):
        terms.append(losses.astype(BF16).astype(F32))
        losses = losses - terms[-1]
    terms.append(jnp.zeros((TAG_ROWS - 3, rows), F32))
    packed[rows:, :rows] = jnp.concatenate(terms, axis=0).astype(BF16)
    packed[rows:, rows:] = jnp.zeros((TAG_ROWS, packed.shape[1] - rows), BF16)


def own_far_kernel(
    log_scale, bias, video, audio, audio_ids, loss_in, loss, weights, products
):
    scalars = (log_scale, bias)
    loss[...] = loss_in[...] + meet(video, (audio, audio_ids), scalars, products, weights)


def far_kernel(
    log_scale, bias, video, other_video, audio, audio_ids, own_weights, loss_in,
    loss, other_loss, sums, weights, products,
):
    loss[...] = loss_in[...]
    other_loss[...] = meet(other_video, (audio, audio_ids), (log_scale, bias), products, weights)
    for part in column_parts(video):
        both = to_partner(own_weights, video, part) + to_partner(weights, other_video, part)
        sums[:, part] = both.astype(BF16)


def near_kernel(
    log_scale, bias, other_video, audio, audio_ids, far_audio, far_weights, other_loss_in, loss_in,
    other_grad, weights, loss, products,
):
    audio = (audio, audio_ids)
    rows = weights.shape[0]
    loss[...] = loss_in[...]
    losses = meet(other_video, audio, (log_scale, bias), products, weights)
    put_losses(other_loss_in[...] + losses, other_grad)
    for part in column_parts(other_video):
        both = to_video(weights, audio, part) + to_video(far_weights, far_audio, part)
        other_grad[:rows, part] = both.astype(BF16)


def row_kernel(
    log_scale, bias, video, other_video, imu, other_imu, loss_in,
    loss, other_grad, sums, weights, near_weights, products, other_weights,
):
    scalars = (log_scale, bias)
    rows = sums.shape[0]
    losses = meet(other_video, imu, scalars, products, near_weights)
    losses = losses + meet(other_video, other_imu, scalars, products, other_weights)
    put_losses(losses, other_grad)
    loss[...] = loss_in[...] + meet(video, other_imu, scalars, products, weights)
    for part in column_parts(video):
        other_sum = to_video(near_weights, imu, part) + to_video(other_weights, other_imu, part)
        other_grad[:rows, part] = other_sum.astype(BF16)
        both = to_partner(weights, video, part) + to_partner(other_weights, other_video, part)
        sums[:, part] = both.astype(BF16)


def late_kernel(
    far_audio, far_weights, col_video, near_weights, row_imu, row_weights, row_video,
    row_near_weights, video_in, audio_in, imu_in, loss_in,
    video_grad, audio_grad, imu_grad, loss,
):
    loss[...] = loss_in[...]
    for part in column_parts(video_grad):
        video_sum = to_video(far_weights, far_audio, part) + to_video(row_weights, row_imu, part)
        video_grad[:, part] = video_in[:, part] + video_sum
        audio_grad[:, part] = audio_in[:, part] + to_partner(near_weights, col_video, part)
        imu_grad[:, part] = imu_in[:, part] + to_partner(row_near_weights, row_video, part)


def added(parts, out, buffer, done):
    rows = out.shape[0] // SUM_BLOCKS
    copies = []
    for k in range(SUM_BLOCKS):
        block = slice(k * rows, (k + 1) * rows)
        total = parts[0][block, :]
        for part in parts[1:]:
            total = total + part[block, :].astype(F32)
        buffer[block, :] = total
        copy = pltpu.make_async_copy(buffer.at[block, :], out.at[block, :], done.at[k])
        copy.start()
        copies.append(copy)
    return copies


def losses_in(packed):
    rows = packed.shape[0] - TAG_ROWS
    return jnp.sum(packed[rows:, :rows].astype(F32), axis=0, keepdims=True)


def partner_sum_kernel(got, grad_in, loss_in, grad, loss, buffer, done):
    copies = added((grad_in, got), grad, buffer, done)
    loss[...] = loss_in[...]
    for copy in copies:
        copy.wait()


def col_sum_kernel(got_video, video_in, loss_in, video_grad, loss):
    rows = video_grad.shape[0]
    video_grad[...] = video_in[...] + got_video[:rows, :].astype(F32)
    loss[...] = loss_in[...] + losses_in(got_video)


def row_sum_kernel(
    got_video, video_in, loss_in, video_grad, loss, buffer, done, losses, losses_done
):
    rows = video_in.shape[0]
    total = loss_in[...] + losses_in(got_video)
    losses[...] = (total / (2.0 * STEPS * rows)).reshape(rows)
    copy = pltpu.make_async_copy(losses, loss, losses_done)
    copy.start()
    for part in added((video_in, got_video), video_grad, buffer, done):
        part.wait()
    copy.wait()


def summed(kernel, outs, spaces, args, cost):
    vmem = pl.BlockSpec(memory_space=pltpu.VMEM)
    return pl.pallas_call(
        kernel,
        out_shape=[jax.ShapeDtypeStruct(*out) for out in outs],
        in_specs=[vmem] * len(args),
        out_specs=[pl.BlockSpec(memory_space=space) for space in spaces],
        scratch_shapes=[
            scratch
            for (shape, _), space in zip(outs, spaces)
            if space == pltpu.HBM
            for scratch in (
                pltpu.VMEM(shape, F32),
                pltpu.SemaphoreType.DMA((SUM_BLOCKS,) if len(shape) == 2 else ()),
            )
        ],
        compiler_params=pltpu.CompilerParams(vmem_limit_bytes=20 * 2**20),
        cost_estimate=pl.CostEstimate(flops=int(cost), bytes_accessed=0, transcendentals=0),
    )(*args)


def call(kernel, outs, scalars, args, rows, weights=1, cost=0, meets=True):
    smem, vmem = pl.BlockSpec(memory_space=pltpu.SMEM), pl.BlockSpec(memory_space=pltpu.VMEM)
    scratch = [pltpu.VMEM((rows, rows), F32)] + [pltpu.VMEM((rows, rows), BF16)] * weights
    scratch = scratch if meets else []
    return pl.pallas_call(
        kernel,
        out_shape=[jax.ShapeDtypeStruct(*out) for out in outs],
        in_specs=[smem] * len(scalars) + [vmem] * len(args),
        out_specs=[vmem] * len(outs),
        scratch_shapes=scratch,
        compiler_params=pltpu.CompilerParams(vmem_limit_bytes=20 * 2**20),
        cost_estimate=pl.CostEstimate(
            flops=int(cost),
            bytes_accessed=2 * sum(a.size * a.dtype.itemsize for a in args),
            transcendentals=0,
        ),
    )(*scalars, *args)


class Tile:
    def __init__(self, axis):
        self.axis = axis
        devices = lax.axis_size(axis)
        if devices == STEPS:
            self.video = [(p ^ 1, p) for p in range(devices)]
            self.partner = [(p ^ 2, p) for p in range(devices)]
        else:
            self.video = [((p + 1) % devices, p) for p in range(devices)]
            self.partner = [((p - 2) % devices, p) for p in range(devices)]

    def bring_video(self, block):
        return lax.ppermute(block, self.axis, self.video)

    def bring_partner(self, block):
        return lax.ppermute(block, self.axis, self.partner)

    def return_video(self, block):
        return lax.ppermute(block, self.axis, [(b, a) for a, b in self.video])

    def return_partner(self, block):
        return lax.ppermute(block, self.axis, [(b, a) for a, b in self.partner])


def per_device(
    video, video_ids, imu, imu_ids, audio, audio_ids,
    imu_log_scale, imu_bias, audio_log_scale, audio_bias,
):
    rows, width = video.shape
    line, square, narrow = ((1, rows), F32), ((rows, width), F32), ((rows, width), BF16)
    packed = ((rows + TAG_ROWS, width), BF16)
    of_imu, of_audio = (imu_log_scale, imu_bias), (audio_log_scale, audio_bias)
    along_row, along_col = Tile("row"), Tile("col")

    video, imu, audio, *made = pack(
        of_imu + of_audio, (video, imu, audio), (video_ids, imu_ids, audio_ids)
    )
    col_audio = along_col.bring_partner(audio), along_col.bring_partner(audio_ids)
    audio = (audio, audio_ids)
    col_video = along_col.bring_video(video)

    loss, video_grad, imu_grad, audio_grad, video_on, imu_on = call(
        own_kernel,
        [line, square, square, square, packed, packed],
        of_imu + of_audio,
        (video, imu, *audio, *made),
        rows, 1, COSTS["own"],
    )
    row_video = along_row.bring_video(video_on)
    row_imu = along_row.bring_partner(imu_on)
    tile = ((rows, rows), BF16)
    loss, far_weights = call(
        own_far_kernel,
        [line, tile],
        of_audio,
        (video, *col_audio, loss),
        rows, 0, COSTS["own_far"],
    )
    loss, col_loss, sums, far_col_weights = call(
        far_kernel,
        [line, line, narrow, tile],
        of_audio,
        (video, col_video, *col_audio, far_weights, loss),
        rows, 0, COSTS["far"],
    )
    got_audio = along_col.return_partner(sums)
    col_grad, near_weights, loss = call(
        near_kernel,
        [packed, tile, line],
        of_audio,
        (col_video, *audio, col_audio[0], far_col_weights, col_loss, loss),
        rows, 0, COSTS["near"],
    )
    got_col = along_col.return_video(col_grad)
    loss, row_grad, sums, row_weights, row_near_weights = call(
        row_kernel,
        [line, packed, narrow, tile, tile],
        of_imu,
        (video, row_video, imu, row_imu, loss),
        rows, 1, COSTS["row"],
    )
    got_row = along_row.return_video(row_grad)
    got_imu = along_row.return_partner(sums)
    video_grad, audio_grad, imu_grad, loss = call(
        late_kernel,
        [square, square, square, line],
        (),
        (
            col_audio[0], far_weights, col_video, near_weights, row_imu, row_weights, row_video,
            row_near_weights, video_grad, audio_grad, imu_grad, loss,
        ),
        rows, 0, COSTS["late"], False,
    )

    hbm, vmem = pltpu.HBM, pltpu.VMEM
    audio_grad, loss = summed(
        partner_sum_kernel,
        [square, line],
        [hbm, vmem],
        (got_audio, audio_grad, loss),
        COSTS["audio_sum"],
    )
    imu_grad, loss = summed(
        partner_sum_kernel,
        [square, line],
        [hbm, vmem],
        (got_imu, imu_grad, loss),
        COSTS["imu_sum"],
    )
    video_grad, loss = summed(
        col_sum_kernel,
        [square, line],
        [vmem, vmem],
        (got_col, video_grad, loss),
        COSTS["col_sum"],
    )
    video_grad, loss = summed(
        row_sum_kernel,
        [square, ((rows,), F32)],
        [hbm, hbm],
        (got_row, video_grad, loss),
        COSTS["row_sum"],
    )
    return (video_grad, imu_grad, audio_grad, loss)


def solution(mesh):
    rows, vector = P(("row", "col"), None), P(("row", "col"))
    return jax.shard_map(
        per_device,
        mesh=mesh,
        in_specs=(rows, vector, rows, vector, rows, vector, P(), P(), P(), P()),
        out_specs=(rows, rows, rows, vector),
        check_vma=False,
    )
```

```python
import jax
import jax.numpy as jnp
from jax import lax
from jax.experimental import pallas as pl
from jax.experimental.pallas import tpu as pltpu
from jax.sharding import PartitionSpec as P

STEPS = 4
SLAB = 16
COLUMNS = 1024
SUM_BLOCKS = 4
TAG_ROWS = 16
TAG_BASE = 256
COSTS = {
    "own": 0.5e9, "own_far": 0.5e9, "far": 0.5e9, "near": 0.5e9, "row": 0.5e9, "late": 0.01e9,
    "audio_sum": 5e9, "imu_sum": 0.01e9, "col_sum": 20e9, "row_sum": 0.5e9,
}

F32 = jnp.float32
BF16 = jnp.bfloat16


def pack_kernel(*refs):
    blocks, ids, packed = refs[:2], refs[2:4], refs[4:6]
    tags, (block_done, tags_done) = refs[6:8], refs[8:]
    rows, width = blocks[0].shape
    copies = [
        pltpu.make_async_copy(block, out.at[:rows, :], block_done.at[k])
        for k, (block, out) in enumerate(zip(blocks, packed))
    ]
    tag_copies = [
        pltpu.make_async_copy(source, tags[k], tags_done.at[k]) for k, source in enumerate(ids)
    ]
    for copy in tag_copies + copies:
        copy.start()
    for copy in tag_copies:
        copy.wait()
    for k, out in enumerate(packed):
        tag = tags[k][...].reshape(1, rows)
        high = tag // TAG_BASE
        low = tag - high * TAG_BASE
        both = jnp.concatenate([high, low, jnp.zeros((TAG_ROWS - 2, rows), jnp.int32)], axis=0)
        out[rows:, :rows] = both.astype(F32).astype(BF16)
        out[rows:, rows:] = jnp.zeros((TAG_ROWS, width - rows), BF16)
    for copy in copies:
        copy.wait()


def pack(blocks, ids):
    rows, width = blocks[0].shape
    hbm, vmem = pl.BlockSpec(memory_space=pltpu.HBM), pl.BlockSpec(memory_space=pltpu.VMEM)
    return pl.pallas_call(
        pack_kernel,
        out_shape=[pltpu.VMEM((rows + TAG_ROWS, width), BF16)] * 2,
        in_specs=[hbm] * 4,
        out_specs=[vmem] * 2,
        scratch_shapes=[
            *[pltpu.VMEM((rows,), jnp.int32)] * 2,
            pltpu.SemaphoreType.DMA((2,)),
            pltpu.SemaphoreType.DMA((2,)),
        ],
        compiler_params=pltpu.CompilerParams(vmem_limit_bytes=56 * 2**20),
    )(*blocks, *ids)


def tags_of(block):
    if isinstance(block, tuple):
        tags = block[1][...]
        return tags.reshape(1, tags.shape[0]).astype(F32)
    rows = block.shape[0] - TAG_ROWS
    tags = block[rows:, :rows].astype(F32)
    return tags[0:1] * TAG_BASE + tags[1:2]


def rows_of(block):
    return block[0] if isinstance(block, tuple) else block


def meet(video, partner, scalars, products, weights):
    rows = weights.shape[0]
    log_scale, offset = scalars[0][0], scalars[1][0]
    scale = jnp.exp(jnp.full((1, rows), log_scale, F32))
    products[...] = lax.dot_general(
        rows_of(partner)[:rows, :], video[:rows, :], (((1,), (1,)), ((), ())), preferred_element_type=F32
    )
    video_tags = tags_of(video)
    partner_tags = jnp.transpose(jnp.broadcast_to(tags_of(partner), (8, rows)))[:, :1]
    total = jnp.zeros((8, rows), F32)
    for start in range(0, rows, SLAB):
        part = slice(start, start + SLAB)
        logits = scale * products[part, :] + offset
        same = partner_tags[part, :] == video_tags
        flipped = -logits
        z = jnp.where(same, flipped, logits)
        e = jnp.exp(jnp.minimum(logits, flipped))
        inverse = 1.0 / (1.0 + e)
        sigmoid = jnp.where(z >= 0.0, inverse, e * inverse)
        weights[part, :] = (jnp.where(same, -scale, scale) * sigmoid).astype(BF16)
        log1p = jnp.where(e < 0.005, e * (1.0 - 0.5 * e), jnp.log(1.0 + e))
        losses = jnp.maximum(z, 0.0) + log1p
        total = total + jnp.sum(losses.reshape(SLAB // 8, 8, rows), axis=0)
    return jnp.sum(total, axis=0, keepdims=True)


def column_parts(ref):
    return [slice(c, c + COLUMNS) for c in range(0, ref.shape[1], COLUMNS)]


def to_video(weights, partner, part):
    rows = weights.shape[0]
    return lax.dot_general(
        weights[...], rows_of(partner)[:rows, part], (((0,), (0,)), ((), ())), preferred_element_type=F32
    )


def to_partner(weights, video, part):
    return jnp.dot(weights[...], video[: weights.shape[0], part], preferred_element_type=F32)


def own_kernel(
    imu_log_scale, imu_bias, audio_log_scale, audio_bias, video, imu, audio, audio_ids,
    loss, video_grad, imu_grad, audio_grad, video_on, imu_on, products, weights,
):
    video_on[...] = video[...]
    imu_on[...] = imu[...]
    audio = (audio, audio_ids)
    loss[...] = meet(video, audio, (audio_log_scale, audio_bias), products, weights)
    for part in column_parts(video):
        video_grad[:, part] = to_video(weights, audio, part)
        audio_grad[:, part] = to_partner(weights, video, part)
    loss[...] += meet(video, imu, (imu_log_scale, imu_bias), products, weights)
    for part in column_parts(video):
        video_grad[:, part] += to_video(weights, imu, part)
        imu_grad[:, part] = to_partner(weights, video, part)


def put_losses(losses, packed):
    rows = losses.shape[1]
    terms = []
    for _ in range(3):
        terms.append(losses.astype(BF16).astype(F32))
        losses = losses - terms[-1]
    terms.append(jnp.zeros((TAG_ROWS - 3, rows), F32))
    packed[rows:, :rows] = jnp.concatenate(terms, axis=0).astype(BF16)
    packed[rows:, rows:] = jnp.zeros((TAG_ROWS, packed.shape[1] - rows), BF16)


def own_far_kernel(
    log_scale, bias, video, audio, audio_ids, loss_in, loss, weights, products
):
    scalars = (log_scale, bias)
    loss[...] = loss_in[...] + meet(video, (audio, audio_ids), scalars, products, weights)


def far_kernel(
    log_scale, bias, video, other_video, audio, audio_ids, own_weights, loss_in,
    loss, other_loss, sums, weights, products,
):
    loss[...] = loss_in[...]
    other_loss[...] = meet(other_video, (audio, audio_ids), (log_scale, bias), products, weights)
    for part in column_parts(video):
        both = to_partner(own_weights, video, part) + to_partner(weights, other_video, part)
        sums[:, part] = both.astype(BF16)


def near_kernel(
    log_scale, bias, other_video, audio, audio_ids, far_audio, far_weights, other_loss_in, loss_in,
    other_grad, weights, loss, products,
):
    audio = (audio, audio_ids)
    rows = weights.shape[0]
    loss[...] = loss_in[...]
    losses = meet(other_video, audio, (log_scale, bias), products, weights)
    put_losses(other_loss_in[...] + losses, other_grad)
    for part in column_parts(other_video):
        both = to_video(weights, audio, part) + to_video(far_weights, far_audio, part)
        other_grad[:rows, part] = both.astype(BF16)


def row_kernel(
    log_scale, bias, video, other_video, imu, other_imu, loss_in,
    loss, other_grad, sums, weights, near_weights, products, other_weights,
):
    scalars = (log_scale, bias)
    rows = sums.shape[0]
    losses = meet(other_video, imu, scalars, products, near_weights)
    losses = losses + meet(other_video, other_imu, scalars, products, other_weights)
    put_losses(losses, other_grad)
    loss[...] = loss_in[...] + meet(video, other_imu, scalars, products, weights)
    for part in column_parts(video):
        other_sum = to_video(near_weights, imu, part) + to_video(other_weights, other_imu, part)
        other_grad[:rows, part] = other_sum.astype(BF16)
        both = to_partner(weights, video, part) + to_partner(other_weights, other_video, part)
        sums[:, part] = both.astype(BF16)


def late_kernel(
    far_audio, far_weights, col_video, near_weights, row_imu, row_weights, row_video,
    row_near_weights, video_in, audio_in, imu_in, loss_in,
    video_grad, audio_grad, imu_grad, loss,
):
    loss[...] = loss_in[...]
    for part in column_parts(video_grad):
        video_sum = to_video(far_weights, far_audio, part) + to_video(row_weights, row_imu, part)
        video_grad[:, part] = video_in[:, part] + video_sum
        audio_grad[:, part] = audio_in[:, part] + to_partner(near_weights, col_video, part)
        imu_grad[:, part] = imu_in[:, part] + to_partner(row_near_weights, row_video, part)


def added(parts, out, buffer, done):
    rows = out.shape[0] // SUM_BLOCKS
    copies = []
    for k in range(SUM_BLOCKS):
        block = slice(k * rows, (k + 1) * rows)
        total = parts[0][block, :]
        for part in parts[1:]:
            total = total + part[block, :].astype(F32)
        buffer[block, :] = total
        copy = pltpu.make_async_copy(buffer.at[block, :], out.at[block, :], done.at[k])
        copy.start()
        copies.append(copy)
    return copies


def losses_in(packed):
    rows = packed.shape[0] - TAG_ROWS
    return jnp.sum(packed[rows:, :rows].astype(F32), axis=0, keepdims=True)


def partner_sum_kernel(got, grad_in, loss_in, grad, loss, buffer, done):
    copies = added((grad_in, got), grad, buffer, done)
    loss[...] = loss_in[...]
    for copy in copies:
        copy.wait()


def col_sum_kernel(got_video, video_in, loss_in, video_grad, loss):
    rows = video_grad.shape[0]
    video_grad[...] = video_in[...] + got_video[:rows, :].astype(F32)
    loss[...] = loss_in[...] + losses_in(got_video)


def row_sum_kernel(
    got_video, video_in, loss_in, video_grad, loss, buffer, done, losses, losses_done
):
    rows = video_in.shape[0]
    total = loss_in[...] + losses_in(got_video)
    losses[...] = (total / (2.0 * STEPS * rows)).reshape(rows)
    copy = pltpu.make_async_copy(losses, loss, losses_done)
    copy.start()
    for part in added((video_in, got_video), video_grad, buffer, done):
        part.wait()
    copy.wait()


def summed(kernel, outs, spaces, args, cost):
    vmem = pl.BlockSpec(memory_space=pltpu.VMEM)
    return pl.pallas_call(
        kernel,
        out_shape=[jax.ShapeDtypeStruct(*out) for out in outs],
        in_specs=[vmem] * len(args),
        out_specs=[pl.BlockSpec(memory_space=space) for space in spaces],
        scratch_shapes=[
            scratch
            for (shape, _), space in zip(outs, spaces)
            if space == pltpu.HBM
            for scratch in (
                pltpu.VMEM(shape, F32),
                pltpu.SemaphoreType.DMA((SUM_BLOCKS,) if len(shape) == 2 else ()),
            )
        ],
        compiler_params=pltpu.CompilerParams(vmem_limit_bytes=20 * 2**20),
        cost_estimate=pl.CostEstimate(flops=int(cost), bytes_accessed=0, transcendentals=0),
    )(*args)


def call(kernel, outs, scalars, args, rows, weights=1, cost=0, meets=True):
    smem, vmem = pl.BlockSpec(memory_space=pltpu.SMEM), pl.BlockSpec(memory_space=pltpu.VMEM)
    scratch = [pltpu.VMEM((rows, rows), F32)] + [pltpu.VMEM((rows, rows), BF16)] * weights
    scratch = scratch if meets else []
    return pl.pallas_call(
        kernel,
        out_shape=[jax.ShapeDtypeStruct(*out) for out in outs],
        in_specs=[smem] * len(scalars) + [vmem] * len(args),
        out_specs=[vmem] * len(outs),
        scratch_shapes=scratch,
        compiler_params=pltpu.CompilerParams(vmem_limit_bytes=20 * 2**20),
        cost_estimate=pl.CostEstimate(
            flops=int(cost),
            bytes_accessed=2 * sum(a.size * a.dtype.itemsize for a in args),
            transcendentals=0,
        ),
    )(*scalars, *args)


class Tile:
    def __init__(self, axis):
        self.axis = axis
        devices = lax.axis_size(axis)
        if devices == STEPS:
            self.video = [(p ^ 1, p) for p in range(devices)]
            self.partner = [(p ^ 2, p) for p in range(devices)]
        else:
            self.video = [((p + 1) % devices, p) for p in range(devices)]
            self.partner = [((p - 2) % devices, p) for p in range(devices)]

    def bring_video(self, block):
        return lax.ppermute(block, self.axis, self.video)

    def bring_partner(self, block):
        return lax.ppermute(block, self.axis, self.partner)

    def return_video(self, block):
        return lax.ppermute(block, self.axis, [(b, a) for a, b in self.video])

    def return_partner(self, block):
        return lax.ppermute(block, self.axis, [(b, a) for a, b in self.partner])


def per_device(
    video, video_ids, imu, imu_ids, audio, audio_ids,
    imu_log_scale, imu_bias, audio_log_scale, audio_bias,
):
    rows, width = video.shape
    line, square, narrow = ((1, rows), F32), ((rows, width), F32), ((rows, width), BF16)
    packed = ((rows + TAG_ROWS, width), BF16)
    of_imu, of_audio = (imu_log_scale, imu_bias), (audio_log_scale, audio_bias)
    along_row, along_col = Tile("row"), Tile("col")

    col_audio = along_col.bring_partner(audio), along_col.bring_partner(audio_ids)
    audio = (audio, audio_ids)
    video, imu = pack((video, imu), (video_ids, imu_ids))
    col_video = along_col.bring_video(video)

    loss, video_grad, imu_grad, audio_grad, video_on, imu_on = call(
        own_kernel,
        [line, square, square, square, packed, packed],
        of_imu + of_audio,
        (video, imu, *audio),
        rows, 1, COSTS["own"],
    )
    row_video = along_row.bring_video(video_on)
    row_imu = along_row.bring_partner(imu_on)
    tile = ((rows, rows), BF16)
    loss, far_weights = call(
        own_far_kernel,
        [line, tile],
        of_audio,
        (video, *col_audio, loss),
        rows, 0, COSTS["own_far"],
    )
    loss, col_loss, sums, far_col_weights = call(
        far_kernel,
        [line, line, narrow, tile],
        of_audio,
        (video, col_video, *col_audio, far_weights, loss),
        rows, 0, COSTS["far"],
    )
    got_audio = along_col.return_partner(sums)
    col_grad, near_weights, loss = call(
        near_kernel,
        [packed, tile, line],
        of_audio,
        (col_video, *audio, col_audio[0], far_col_weights, col_loss, loss),
        rows, 0, COSTS["near"],
    )
    got_col = along_col.return_video(col_grad)
    loss, row_grad, sums, row_weights, row_near_weights = call(
        row_kernel,
        [line, packed, narrow, tile, tile],
        of_imu,
        (video, row_video, imu, row_imu, loss),
        rows, 1, COSTS["row"],
    )
    got_row = along_row.return_video(row_grad)
    got_imu = along_row.return_partner(sums)
    video_grad, audio_grad, imu_grad, loss = call(
        late_kernel,
        [square, square, square, line],
        (),
        (
            col_audio[0], far_weights, col_video, near_weights, row_imu, row_weights, row_video,
            row_near_weights, video_grad, audio_grad, imu_grad, loss,
        ),
        rows, 0, COSTS["late"], False,
    )

    hbm, vmem = pltpu.HBM, pltpu.VMEM
    audio_grad, loss = summed(
        partner_sum_kernel,
        [square, line],
        [hbm, vmem],
        (got_audio, audio_grad, loss),
        COSTS["audio_sum"],
    )
    imu_grad, loss = summed(
        partner_sum_kernel,
        [square, line],
        [hbm, vmem],
        (got_imu, imu_grad, loss),
        COSTS["imu_sum"],
    )
    video_grad, loss = summed(
        col_sum_kernel,
        [square, line],
        [vmem, vmem],
        (got_col, video_grad, loss),
        COSTS["col_sum"],
    )
    video_grad, loss = summed(
        row_sum_kernel,
        [square, ((rows,), F32)],
        [hbm, hbm],
        (got_row, video_grad, loss),
        COSTS["row_sum"],
    )
    return (video_grad, imu_grad, audio_grad, loss)


def solution(mesh):
    rows, vector = P(("row", "col"), None), P(("row", "col"))
    return jax.shard_map(
        per_device,
        mesh=mesh,
        in_specs=(rows, vector, rows, vector, rows, vector, P(), P(), P(), P()),
        out_specs=(rows, rows, rows, vector),
        check_vma=False,
    )
```

```python
import jax
import jax.numpy as jnp
from jax import lax
from jax.experimental import pallas as pl
from jax.experimental.pallas import tpu as pltpu
from jax.sharding import PartitionSpec as P

STEPS = 4
SLAB = 16
COLUMNS = 1024
SUM_BLOCKS = 4
TAG_ROWS = 16
TAG_BASE = 256
COSTS = {
    "own": 0.5e9, "own_far": 0.5e9, "far": 0.5e9, "near": 0.5e9, "row": 0.5e9, "late": 0.01e9,
    "audio_sum": 5e9, "imu_sum": 0.01e9, "col_sum": 20e9, "row_sum": 0.5e9,
}

F32 = jnp.float32
BF16 = jnp.bfloat16


def pack_kernel(*refs):
    blocks, ids, packed = refs[:2], refs[2:4], refs[4:6]
    tags, (block_done, tags_done) = refs[6:8], refs[8:]
    rows, width = blocks[0].shape
    copies = [
        pltpu.make_async_copy(block, out.at[:rows, :], block_done.at[k])
        for k, (block, out) in enumerate(zip(blocks, packed))
    ]
    tag_copies = [
        pltpu.make_async_copy(source, tags[k], tags_done.at[k]) for k, source in enumerate(ids)
    ]
    for copy in tag_copies + copies:
        copy.start()
    for copy in tag_copies:
        copy.wait()
    for k, out in enumerate(packed):
        tag = tags[k][...].reshape(1, rows)
        high = tag // TAG_BASE
        low = tag - high * TAG_BASE
        both = jnp.concatenate([high, low, jnp.zeros((TAG_ROWS - 2, rows), jnp.int32)], axis=0)
        out[rows:, :rows] = both.astype(F32).astype(BF16)
        out[rows:, rows:] = jnp.zeros((TAG_ROWS, width - rows), BF16)
    for copy in copies:
        copy.wait()


def pack(blocks, ids):
    rows, width = blocks[0].shape
    hbm, vmem = pl.BlockSpec(memory_space=pltpu.HBM), pl.BlockSpec(memory_space=pltpu.VMEM)
    return pl.pallas_call(
        pack_kernel,
        out_shape=[pltpu.VMEM((rows + TAG_ROWS, width), BF16)] * 2,
        in_specs=[hbm] * 4,
        out_specs=[vmem] * 2,
        scratch_shapes=[
            *[pltpu.VMEM((rows,), jnp.int32)] * 2,
            pltpu.SemaphoreType.DMA((2,)),
            pltpu.SemaphoreType.DMA((2,)),
        ],
        compiler_params=pltpu.CompilerParams(vmem_limit_bytes=56 * 2**20),
    )(*blocks, *ids)


def tags_of(block):
    if isinstance(block, tuple):
        tags = block[1][...]
        return tags.reshape(1, tags.shape[0]).astype(F32)
    rows = block.shape[0] - TAG_ROWS
    tags = block[rows:, :rows].astype(F32)
    return tags[0:1] * TAG_BASE + tags[1:2]


def rows_of(block):
    return block[0] if isinstance(block, tuple) else block


def meet(video, partner, scalars, products, weights):
    rows = weights.shape[0]
    log_scale, offset = scalars[0][0], scalars[1][0]
    scale = jnp.exp(jnp.full((1, rows), log_scale, F32))
    products[...] = lax.dot_general(
        rows_of(partner)[:rows, :], video[:rows, :], (((1,), (1,)), ((), ())), preferred_element_type=F32
    )
    video_tags = tags_of(video)
    partner_tags = jnp.transpose(jnp.broadcast_to(tags_of(partner), (8, rows)))[:, :1]
    total = jnp.zeros((8, rows), F32)
    for start in range(0, rows, SLAB):
        part = slice(start, start + SLAB)
        logits = scale * products[part, :] + offset
        same = partner_tags[part, :] == video_tags
        flipped = -logits
        z = jnp.where(same, flipped, logits)
        e = jnp.exp(jnp.minimum(logits, flipped))
        inverse = 1.0 / (1.0 + e)
        sigmoid = jnp.where(z >= 0.0, inverse, e * inverse)
        weights[part, :] = (jnp.where(same, -scale, scale) * sigmoid).astype(BF16)
        log1p = jnp.where(e < 0.005, e * (1.0 - 0.5 * e), jnp.log(1.0 + e))
        losses = jnp.maximum(z, 0.0) + log1p
        total = total + jnp.sum(losses.reshape(SLAB // 8, 8, rows), axis=0)
    return jnp.sum(total, axis=0, keepdims=True)


def column_parts(ref):
    return [slice(c, c + COLUMNS) for c in range(0, ref.shape[1], COLUMNS)]


def to_video(weights, partner, part):
    rows = weights.shape[0]
    return lax.dot_general(
        weights[...], rows_of(partner)[:rows, part], (((0,), (0,)), ((), ())), preferred_element_type=F32
    )


def to_partner(weights, video, part):
    return jnp.dot(weights[...], video[: weights.shape[0], part], preferred_element_type=F32)


def own_kernel(
    imu_log_scale, imu_bias, audio_log_scale, audio_bias, video, imu, audio, audio_ids,
    loss, video_grad, imu_grad, audio_grad, video_on, imu_on, products, weights,
):
    video_on[...] = video[...]
    imu_on[...] = imu[...]
    audio = (audio, audio_ids)
    loss[...] = meet(video, audio, (audio_log_scale, audio_bias), products, weights)
    for part in column_parts(video):
        video_grad[:, part] = to_video(weights, audio, part)
        audio_grad[:, part] = to_partner(weights, video, part)
    loss[...] += meet(video, imu, (imu_log_scale, imu_bias), products, weights)
    for part in column_parts(video):
        video_grad[:, part] += to_video(weights, imu, part)
        imu_grad[:, part] = to_partner(weights, video, part)


def put_losses(losses, packed):
    rows = losses.shape[1]
    terms = []
    for _ in range(3):
        terms.append(losses.astype(BF16).astype(F32))
        losses = losses - terms[-1]
    terms.append(jnp.zeros((TAG_ROWS - 3, rows), F32))
    packed[rows:, :rows] = jnp.concatenate(terms, axis=0).astype(BF16)
    packed[rows:, rows:] = jnp.zeros((TAG_ROWS, packed.shape[1] - rows), BF16)


def own_far_kernel(
    log_scale, bias, video, audio, audio_ids, loss_in, loss, weights, products
):
    scalars = (log_scale, bias)
    loss[...] = loss_in[...] + meet(video, (audio, audio_ids), scalars, products, weights)


def far_kernel(
    log_scale, bias, video, other_video, audio, audio_ids, own_weights, loss_in,
    loss, other_loss, sums, weights, products,
):
    loss[...] = loss_in[...]
    other_loss[...] = meet(other_video, (audio, audio_ids), (log_scale, bias), products, weights)
    for part in column_parts(video):
        both = to_partner(own_weights, video, part) + to_partner(weights, other_video, part)
        sums[:, part] = both.astype(BF16)


def near_kernel(
    log_scale, bias, other_video, audio, audio_ids, far_audio, far_weights, other_loss_in, loss_in,
    other_grad, weights, loss, products,
):
    audio = (audio, audio_ids)
    rows = weights.shape[0]
    loss[...] = loss_in[...]
    losses = meet(other_video, audio, (log_scale, bias), products, weights)
    put_losses(other_loss_in[...] + losses, other_grad)
    for part in column_parts(other_video):
        both = to_video(weights, audio, part) + to_video(far_weights, far_audio, part)
        other_grad[:rows, part] = both.astype(BF16)


def row_kernel(
    log_scale, bias, video, other_video, imu, other_imu, loss_in,
    loss, other_grad, sums, weights, near_weights, products, other_weights,
):
    scalars = (log_scale, bias)
    rows = sums.shape[0]
    losses = meet(other_video, imu, scalars, products, near_weights)
    losses = losses + meet(other_video, other_imu, scalars, products, other_weights)
    put_losses(losses, other_grad)
    loss[...] = loss_in[...] + meet(video, other_imu, scalars, products, weights)
    for part in column_parts(video):
        other_sum = to_video(near_weights, imu, part) + to_video(other_weights, other_imu, part)
        other_grad[:rows, part] = other_sum.astype(BF16)
        both = to_partner(weights, video, part) + to_partner(other_weights, other_video, part)
        sums[:, part] = both.astype(BF16)


def late_kernel(
    far_audio, far_weights, col_video, near_weights, row_imu, row_weights, row_video,
    row_near_weights, video_in, audio_in, imu_in, loss_in,
    video_grad, audio_grad, imu_grad, loss,
):
    loss[...] = loss_in[...]
    for part in column_parts(video_grad):
        video_sum = to_video(far_weights, far_audio, part) + to_video(row_weights, row_imu, part)
        video_grad[:, part] = video_in[:, part] + video_sum
        audio_grad[:, part] = audio_in[:, part] + to_partner(near_weights, col_video, part)
        imu_grad[:, part] = imu_in[:, part] + to_partner(row_near_weights, row_video, part)


def added(parts, out, buffer, done):
    rows = out.shape[0] // SUM_BLOCKS
    copies = []
    for k in range(SUM_BLOCKS):
        block = slice(k * rows, (k + 1) * rows)
        total = parts[0][block, :]
        for part in parts[1:]:
            total = total + part[block, :].astype(F32)
        buffer[block, :] = total
        copy = pltpu.make_async_copy(buffer.at[block, :], out.at[block, :], done.at[k])
        copy.start()
        copies.append(copy)
    return copies


def losses_in(packed):
    rows = packed.shape[0] - TAG_ROWS
    return jnp.sum(packed[rows:, :rows].astype(F32), axis=0, keepdims=True)


def partner_sum_kernel(got, grad_in, loss_in, grad, loss, buffer, done):
    copies = added((grad_in, got), grad, buffer, done)
    loss[...] = loss_in[...]
    for copy in copies:
        copy.wait()


def col_sum_kernel(got_video, video_in, loss_in, video_grad, loss):
    rows = video_grad.shape[0]
    video_grad[...] = video_in[...] + got_video[:rows, :].astype(F32)
    loss[...] = loss_in[...] + losses_in(got_video)


def row_sum_kernel(
    got_video, video_in, loss_in, video_grad, loss, buffer, done, losses, losses_done
):
    rows = video_in.shape[0]
    total = loss_in[...] + losses_in(got_video)
    losses[...] = (total / (2.0 * STEPS * rows)).reshape(rows)
    copy = pltpu.make_async_copy(losses, loss, losses_done)
    copy.start()
    for part in added((video_in, got_video), video_grad, buffer, done):
        part.wait()
    copy.wait()


def summed(kernel, outs, spaces, args, cost):
    vmem = pl.BlockSpec(memory_space=pltpu.VMEM)
    return pl.pallas_call(
        kernel,
        out_shape=[jax.ShapeDtypeStruct(*out) for out in outs],
        in_specs=[vmem] * len(args),
        out_specs=[pl.BlockSpec(memory_space=space) for space in spaces],
        scratch_shapes=[
            scratch
            for (shape, _), space in zip(outs, spaces)
            if space == pltpu.HBM
            for scratch in (
                pltpu.VMEM(shape, F32),
                pltpu.SemaphoreType.DMA((SUM_BLOCKS,) if len(shape) == 2 else ()),
            )
        ],
        compiler_params=pltpu.CompilerParams(vmem_limit_bytes=20 * 2**20),
        cost_estimate=pl.CostEstimate(flops=int(cost), bytes_accessed=0, transcendentals=0),
    )(*args)


def call(kernel, outs, scalars, args, rows, weights=1, cost=0, meets=True):
    smem, vmem = pl.BlockSpec(memory_space=pltpu.SMEM), pl.BlockSpec(memory_space=pltpu.VMEM)
    scratch = [pltpu.VMEM((rows, rows), F32)] + [pltpu.VMEM((rows, rows), BF16)] * weights
    scratch = scratch if meets else []
    return pl.pallas_call(
        kernel,
        out_shape=[jax.ShapeDtypeStruct(*out) for out in outs],
        in_specs=[smem] * len(scalars) + [vmem] * len(args),
        out_specs=[vmem] * len(outs),
        scratch_shapes=scratch,
        compiler_params=pltpu.CompilerParams(vmem_limit_bytes=20 * 2**20),
        cost_estimate=pl.CostEstimate(
            flops=int(cost),
            bytes_accessed=2 * sum(a.size * a.dtype.itemsize for a in args),
            transcendentals=0,
        ),
    )(*scalars, *args)


class Tile:
    def __init__(self, axis):
        self.axis = axis
        devices = lax.axis_size(axis)
        if devices == STEPS:
            self.video = [(p ^ 1, p) for p in range(devices)]
            self.partner = [(p ^ 3, p) for p in range(devices)]
        else:
            self.video = [((p + 1) % devices, p) for p in range(devices)]
            self.partner = [((p - 2) % devices, p) for p in range(devices)]

    def bring_video(self, block):
        return lax.ppermute(block, self.axis, self.video)

    def bring_partner(self, block):
        return lax.ppermute(block, self.axis, self.partner)

    def return_video(self, block):
        return lax.ppermute(block, self.axis, [(b, a) for a, b in self.video])

    def return_partner(self, block):
        return lax.ppermute(block, self.axis, [(b, a) for a, b in self.partner])


def per_device(
    video, video_ids, imu, imu_ids, audio, audio_ids,
    imu_log_scale, imu_bias, audio_log_scale, audio_bias,
):
    rows, width = video.shape
    line, square, narrow = ((1, rows), F32), ((rows, width), F32), ((rows, width), BF16)
    packed = ((rows + TAG_ROWS, width), BF16)
    of_imu, of_audio = (imu_log_scale, imu_bias), (audio_log_scale, audio_bias)
    along_row, along_col = Tile("row"), Tile("col")

    col_audio = along_col.bring_partner(audio), along_col.bring_partner(audio_ids)
    audio = (audio, audio_ids)
    video, imu = pack((video, imu), (video_ids, imu_ids))
    col_video = along_col.bring_video(video)

    loss, video_grad, imu_grad, audio_grad, video_on, imu_on = call(
        own_kernel,
        [line, square, square, square, packed, packed],
        of_imu + of_audio,
        (video, imu, *audio),
        rows, 1, COSTS["own"],
    )
    row_video = along_row.bring_video(video_on)
    row_imu = along_row.bring_partner(imu_on)
    tile = ((rows, rows), BF16)
    loss, far_weights = call(
        own_far_kernel,
        [line, tile],
        of_audio,
        (video, *col_audio, loss),
        rows, 0, COSTS["own_far"],
    )
    loss, col_loss, sums, far_col_weights = call(
        far_kernel,
        [line, line, narrow, tile],
        of_audio,
        (video, col_video, *col_audio, far_weights, loss),
        rows, 0, COSTS["far"],
    )
    got_audio = along_col.return_partner(sums)
    col_grad, near_weights, loss = call(
        near_kernel,
        [packed, tile, line],
        of_audio,
        (col_video, *audio, col_audio[0], far_col_weights, col_loss, loss),
        rows, 0, COSTS["near"],
    )
    got_col = along_col.return_video(col_grad)
    loss, row_grad, sums, row_weights, row_near_weights = call(
        row_kernel,
        [line, packed, narrow, tile, tile],
        of_imu,
        (video, row_video, imu, row_imu, loss),
        rows, 1, COSTS["row"],
    )
    got_row = along_row.return_video(row_grad)
    got_imu = along_row.return_partner(sums)
    video_grad, audio_grad, imu_grad, loss = call(
        late_kernel,
        [square, square, square, line],
        (),
        (
            col_audio[0], far_weights, col_video, near_weights, row_imu, row_weights, row_video,
            row_near_weights, video_grad, audio_grad, imu_grad, loss,
        ),
        rows, 0, COSTS["late"], False,
    )

    hbm, vmem = pltpu.HBM, pltpu.VMEM
    audio_grad, loss = summed(
        partner_sum_kernel,
        [square, line],
        [hbm, vmem],
        (got_audio, audio_grad, loss),
        COSTS["audio_sum"],
    )
    imu_grad, loss = summed(
        partner_sum_kernel,
        [square, line],
        [hbm, vmem],
        (got_imu, imu_grad, loss),
        COSTS["imu_sum"],
    )
    video_grad, loss = summed(
        col_sum_kernel,
        [square, line],
        [vmem, vmem],
        (got_col, video_grad, loss),
        COSTS["col_sum"],
    )
    video_grad, loss = summed(
        row_sum_kernel,
        [square, ((rows,), F32)],
        [hbm, hbm],
        (got_row, video_grad, loss),
        COSTS["row_sum"],
    )
    return (video_grad, imu_grad, audio_grad, loss)


def solution(mesh):
    rows, vector = P(("row", "col"), None), P(("row", "col"))
    return jax.shard_map(
        per_device,
        mesh=mesh,
        in_specs=(rows, vector, rows, vector, rows, vector, P(), P(), P(), P()),
        out_specs=(rows, rows, rows, vector),
        check_vma=False,
    )
```
